32 devices in a mesh: rows: 8 (over z, x), feat: 4 (over y, core).
Axes of the slice: x: 2, y: 2, z: 4, core: 2. Of those that a mesh axis runs over, the one named last changes fastest.
Arguments:
- predictions: bfloat16 [12288, 4096], P('rows', 'feat'), may hold values from -6 to 6
- labels: bfloat16 [12288, 4096], P('rows', 'feat'), may hold values from 0 to 1
- feature_codes: int32 [32, 12288], P('feat', 'rows'), may hold values from 0 to 255
- leaf_index: int32 [12288], P('rows'), may hold values from 0 to 63
- sketch_weight: bfloat16 [4096, 256], P('feat'), may hold values from -0.09375 to 0.09375
Outputs:
- histograms: float32 [256, 32, 256], P('rows', 'feat')
- leaf_values: float32 [64, 4096], P(None, 'feat')
- updated: bfloat16 [12288, 4096], P('rows', 'feat')
The draws below stay inside these ranges and needn't reach their ends.
All inputs are finite; a program needn't handle non-finite values.
Results may differ from the reference program's by a relative error of at most 0.008.
Values may be sent and summed in bfloat16 or wider, within the bound.
No kernel may reach another device: no remote copies, remote signals or barrier semaphores. Data moves between devices by JAX's collectives and lax.ppermute only.
A program may use at most 64 MiB of HBM per device.

```python
import jax
import jax.numpy as jnp
from jax import lax

LABELS = 4096
SKETCH = 256
BINS = 256
LEAVES = 64
ROW_DEV = 1536
ROWS = 12288
FEATURES = 32
N_FEAT = 4


def shared_leaves(key):
    return jax.random.randint(jax.random.fold_in(key, 101), (ROWS,), 0, LEAVES).astype(jnp.int32)


def label_blocks():
    return jnp.arange(LABELS, dtype=jnp.int32) // 16


def draw_leaf_index(key, part):
    return shared_leaves(key)


def draw_predictions(key, part):
    leaves = shared_leaves(key)
    block_count = (LABELS + 15) // 16
    table = jax.random.uniform(jax.random.fold_in(key, 202), (LEAVES, block_count), jnp.float32, -0.8, 0.8)
    factor_rows = jnp.exp(table)[leaves]
    factor = factor_rows[:, label_blocks()]
    noise_key = jax.random.fold_in(key, 203)
    base = jnp.clip(1.5 * jax.random.normal(noise_key, (ROWS, LABELS), jnp.float32), -5.0, 5.0)
    return jnp.clip(base * factor, -6.0, 6.0).astype(jnp.bfloat16)


def draw_labels(key, part):
    leaves = shared_leaves(key)
    block_count = (LABELS + 15) // 16
    centre = jax.random.uniform(jax.random.fold_in(key, 303), (LEAVES, block_count), jnp.float32, 0.15, 0.85)
    centre_full = centre[leaves][:, label_blocks()]
    noise_key = jax.random.fold_in(key, 304)
    noise = jax.random.uniform(noise_key, (ROWS, LABELS), jnp.float32, -0.15, 0.15)
    return jnp.clip(centre_full + noise, 0.0, 1.0).astype(jnp.bfloat16)


def plant(drawn, own_key, least, largest):
    longest = drawn.shape.index(max(drawn.shape))
    spots = []
    for shift in (0, 1):
        where = [jax.random.randint(jax.random.fold_in(own_key, axis), (), 0, length) for axis, length in enumerate(drawn.shape)]
        where[longest] = (where[longest] + shift) % drawn.shape[longest]
        spots.append(tuple(where))
    return drawn.at[spots[0]].set(least).at[spots[1]].set(largest)


def level_of(key, extent, cuts, low, largest):
    loudness = 1.0
    for axis_at, parts in cuts:
        heights = jax.random.uniform(jax.random.fold_in(jax.random.fold_in(key, 6), axis_at), (parts,), jnp.float32, low / len(cuts), largest / len(cuts))
        loudness = loudness * jnp.repeat(jnp.exp(heights), extent[axis_at] // parts).reshape((-1,) + (1,) * (len(extent) - 1 - axis_at))
    return loudness


def centred(rng, shape, spread, limit, shards=(), kind=jnp.bfloat16):
    gain = level_of(rng, shape, shards, -0.22, 0.18) if shards else 1.0
    array = jax.random.normal(rng, shape, jnp.float32) * spread * gain
    return jnp.minimum(jnp.maximum(array, -limit), limit).astype(kind)


def setup_inputs(seed: int = 0) -> dict:
    key_list = jax.random.split(jax.random.key(seed), 6)
    return {
        "predictions": draw_predictions(jax.random.fold_in(key_list[5], 71), 0),
        "labels": draw_labels(jax.random.fold_in(key_list[5], 71), 0),
        "feature_codes": plant(jax.random.randint(key_list[2], (FEATURES, ROWS), 0, BINS), jax.random.fold_in(key_list[2], 1), 0, BINS - 1).astype(jnp.int32),
        "leaf_index": draw_leaf_index(jax.random.fold_in(key_list[5], 71), 0),
        "sketch_weight": centred(key_list[4], (LABELS, SKETCH), LABELS ** -0.5, 0.09375, ((0, 4),)),
    }


shrinkage = 0.5
ridge_term = 1.0


def reference(predictions, labels, feature_codes, leaf_index, sketch_weight):
    blocks = predictions.shape[0] // ROW_DEV
    features = feature_codes.shape[0]
    width = predictions.shape[1]
    group_width = width // N_FEAT

    def one_block(carry, number):
        hist_acc, grad_acc, hess_acc = carry
        first = (number * ROW_DEV).astype(jnp.int32)
        logits = lax.dynamic_slice_in_dim(predictions, first, ROW_DEV, 0).astype(jnp.float32)
        targets = lax.dynamic_slice_in_dim(labels, first, ROW_DEV, 0).astype(jnp.float32)
        codes = lax.dynamic_slice_in_dim(feature_codes, first, ROW_DEV, 1)
        leaves = lax.dynamic_slice_in_dim(leaf_index, first, ROW_DEV, 0)
        probability = jax.nn.sigmoid(logits)
        gradient = (targets - probability).astype(jnp.bfloat16)
        hessian = (probability * (1.0 - probability)).astype(jnp.bfloat16)
        summed = jnp.zeros((ROW_DEV, SKETCH), jnp.float32)
        for group in range(N_FEAT):
            part = jnp.dot(gradient[:, group * group_width:(group + 1) * group_width],
                           sketch_weight[group * group_width:(group + 1) * group_width, :],
                           preferred_element_type=jnp.float32).astype(jnp.bfloat16)
            summed = summed + part.astype(jnp.float32)
        sketch = summed.astype(jnp.bfloat16)
        levels = jnp.arange(BINS, dtype=jnp.int32)
        one_hot = (levels[:, None, None] == codes[None, :, :]).astype(jnp.float32)
        hist_acc = hist_acc + jnp.einsum("bfr,rk->bfk", one_hot, sketch.astype(jnp.float32))
        leaf_hot = (jnp.arange(LEAVES, dtype=jnp.int32)[:, None] == leaves[None, :]).astype(jnp.bfloat16)
        grad_acc = grad_acc + jnp.dot(leaf_hot, gradient, preferred_element_type=jnp.float32)
        hess_acc = hess_acc + jnp.dot(leaf_hot, hessian, preferred_element_type=jnp.float32)
        return (hist_acc, grad_acc, hess_acc), None

    start_carry = (jnp.zeros((BINS, features, SKETCH), jnp.float32),
                   jnp.zeros((LEAVES, width), jnp.float32),
                   jnp.zeros((LEAVES, width), jnp.float32))
    (histograms, grad_sum, hess_sum), _ = lax.scan(one_block, start_carry, jnp.arange(blocks, dtype=jnp.int32))
    leaf_values = grad_sum / (hess_sum + ridge_term)

    def update_block(pieces):
        logits, leaves = pieces
        return (logits.astype(jnp.float32) + shrinkage * leaf_values[leaves]).astype(jnp.bfloat16)

    shaped = predictions.reshape(blocks, ROW_DEV, width)
    shaped_leaves = leaf_index.reshape(blocks, ROW_DEV)
    updated = lax.map(update_block, (shaped, shaped_leaves)).reshape(blocks * ROW_DEV, width)
    return histograms, leaf_values, updated
```

```python
import functools

import jax
import jax.numpy as jnp
from jax import lax
from jax.experimental import pallas as pl
from jax.experimental.pallas import tpu as pltpu
from jax.sharding import PartitionSpec as P

BINS = 256
LEAVES = 64


shrinkage = 0.5
ridge_term = 1.0

f32 = jnp.float32
bf16 = jnp.bfloat16
VMEM_LIMIT = 48 * 1024 * 1024


def block_rows(rows):
    for size in (256, 128, 64, 32, 16):
        if rows % size == 0:
            return size
    return rows


def swap(x, axis, size, by):
    return lax.ppermute(x, axis, [(i, i ^ by) for i in range(size)])


def rows_kernel(core_ref, pred_ref, lab_ref, leaf_ref, w_ref, *rest, first):
    if first:
        sk_refs, (g_ref, h_ref) = rest[:-2], rest[-2:]
    else:
        (g0_ref, h0_ref), sk_refs, (g_ref, h_ref) = rest[:2], rest[2:-2], rest[-2:]
    step = pl.program_id(0)

    @pl.when(step == 0)
    def _():
        if first:
            g_ref[...] = jnp.zeros_like(g_ref)
            h_ref[...] = jnp.zeros_like(h_ref)
        else:
            g_ref[...] = g0_ref[...]
            h_ref[...] = h0_ref[...]

    t = jnp.tanh(pred_ref[...].astype(f32) * 0.5)
    grad = ((lab_ref[...].astype(f32) - 0.5) - 0.5 * t).astype(bf16)
    hess = (0.25 - 0.25 * t * t).astype(bf16)
    sketch = jnp.dot(grad, w_ref[...], preferred_element_type=f32)
    width = sk_refs[0].shape[1]
    for i, ref in enumerate(sk_refs):
        ref[...] = sketch[:, i * width:(i + 1) * width].astype(bf16)
    blk = pred_ref.shape[0]
    hot = (lax.broadcasted_iota(jnp.int32, (LEAVES, blk), 0) == leaf_ref[0]).astype(f32).astype(bf16)
    g_ref[...] += jnp.dot(hot, grad, preferred_element_type=f32)
    h_ref[...] += jnp.dot(hot, hess, preferred_element_type=f32)


def rows_pass(which, pred, lab, leaf, w, before, parts):
    rows, cols = pred.shape
    half = rows // 2
    blk = block_rows(half)
    steps = half // blk
    width = w.shape[1] // parts
    first = before is None
    row_map = lambda i, c: (c[0] * steps + i, 0)
    fixed = lambda i, c: (0, 0)
    sums = pl.BlockSpec((LEAVES, cols), fixed)
    in_specs = [
        pl.BlockSpec((blk, cols), row_map),
        pl.BlockSpec((blk, cols), row_map),
        pl.BlockSpec((1, 1, blk), lambda i, c: (c[0] * steps + i, 0, 0)),
        pl.BlockSpec(w.shape, fixed),
    ]
    args = [pred, lab, leaf.reshape(rows // blk, 1, blk), w]
    if not first:
        in_specs += [sums, sums]
        args += list(before)
    out = pl.pallas_call(
        functools.partial(rows_kernel, first=first),
        grid_spec=pltpu.PrefetchScalarGridSpec(
            num_scalar_prefetch=1,
            grid=(steps,),
            in_specs=in_specs,
            out_specs=[pl.BlockSpec((blk, width), lambda i, c: (i, 0))] * parts + [sums, sums],
        ),
        out_shape=[jax.ShapeDtypeStruct((half, width), bf16)] * parts
        + [jax.ShapeDtypeStruct((LEAVES, cols), f32)] * 2,
        compiler_params=pltpu.CompilerParams(vmem_limit_bytes=VMEM_LIMIT),
        name="rows_first" if first else "rows_second",
    )(which, *args)
    return out[:parts], tuple(out[parts:])


def hist_kernel(codes_ref, own_ref, other_ref, out_ref, *, per, odd):
    feats = codes_ref.shape[1]
    half = codes_ref.shape[2]
    codes = codes_ref[...].astype(f32).astype(bf16)
    base = (2 * pl.program_id(0) + odd) * per
    levels = (lax.broadcasted_iota(jnp.int32, (per, 1, 1), 0) + base).astype(f32).astype(bf16)
    one = jnp.ones((), bf16)
    zero = jnp.zeros((), bf16)
    total = None
    for part, ref in ((0, own_ref), (1, other_ref)):
        hot = jnp.where(codes[part][None] == levels, one, zero).reshape(per * feats, half)
        term = jnp.dot(hot, ref[...], preferred_element_type=f32)
        total = term if total is None else total + term
    out_ref[0] = total.astype(out_ref.dtype)


def hist_pass(codes, own, other, per, blocks, odd, dtype):
    feats = codes.shape[1]
    width = own.shape[1]
    whole = lambda a: pl.BlockSpec(a.shape, lambda i: (0,) * a.ndim)
    return pl.pallas_call(
        functools.partial(hist_kernel, per=per, odd=odd),
        grid=(blocks,),
        in_specs=[whole(codes), whole(own), whole(other)],
        out_specs=pl.BlockSpec((1, per * feats, width), lambda i: (i, 0, 0)),
        out_shape=jax.ShapeDtypeStruct((blocks, per * feats, width), dtype),
        compiler_params=pltpu.CompilerParams(vmem_limit_bytes=VMEM_LIMIT),
        name="hist_send" if odd else "hist_keep",
    )(codes, own, other)


def update_kernel(me_ref, pred_ref, leaf_ref, table_ref, new_ref, values_ref):
    n = table_ref.shape[0]

    @pl.when(pl.program_id(0) == 0)
    def _():
        for d in range(n):
            values_ref[d] = table_ref[d ^ me_ref[0]]

    blk = pred_ref.shape[0]
    table = table_ref[...].reshape(LEAVES, table_ref.shape[2])
    hot = (lax.broadcasted_iota(jnp.int32, (LEAVES, blk), 0) == leaf_ref[0]).astype(f32).astype(bf16)
    found = lax.dot_general(hot, table.astype(bf16), (((0,), (0,)), ((), ())), preferred_element_type=f32)
    new_ref[...] = (pred_ref[...].astype(f32) + shrinkage * found).astype(bf16)


def update_pass(me, pred, leaf, table):
    rows, cols = pred.shape
    blk = block_rows(rows)
    return pl.pallas_call(
        update_kernel,
        grid_spec=pltpu.PrefetchScalarGridSpec(
            num_scalar_prefetch=1,
            grid=(rows // blk,),
            in_specs=[
                pl.BlockSpec((blk, cols), lambda i, m: (i, 0)),
                pl.BlockSpec((1, 1, blk), lambda i, m: (i, 0, 0)),
                pl.BlockSpec(table.shape, lambda i, m: (0, 0, 0)),
            ],
            out_specs=[
                pl.BlockSpec((blk, cols), lambda i, m: (i, 0)),
                pl.BlockSpec(table.shape, lambda i, m: (0, 0, 0)),
            ],
        ),
        out_shape=[
            jax.ShapeDtypeStruct((rows, cols), bf16),
            jax.ShapeDtypeStruct(table.shape, f32),
        ],
        compiler_params=pltpu.CompilerParams(vmem_limit_bytes=VMEM_LIMIT),
        name="update",
    )(me, pred, leaf.reshape(rows // blk, 1, blk), table)


def local(n, nf, predictions, labels, feature_codes, leaf_index, sketch_weight):
    rows, cols = predictions.shape
    feats = feature_codes.shape[0]
    half = rows // 2
    parts = 2
    me = lax.axis_index("rows")
    core = lax.axis_index("feat") & 1
    per = BINS // n
    leaf_per = LEAVES // n
    leaf = leaf_index ^ (me * leaf_per)
    codes = (feature_codes ^ (me * per)).reshape(feats, 2, half)
    codes = jnp.where(core == 0, codes, codes[:, ::-1]).swapaxes(0, 1)

    send, sums = rows_pass((1 - core).reshape(1), predictions, labels, leaf, sketch_weight, None, parts)
    got = [swap(s, "feat", nf, 1) for s in send]
    keep, sums = rows_pass(core.reshape(1), predictions, labels, leaf, sketch_weight, sums, parts)

    grad, hess = (s.reshape(n, leaf_per, cols) for s in sums)
    both = jnp.concatenate([grad, hess], axis=1)
    both16 = both.astype(bf16)
    total = both[0]
    for t in range(1, n):
        total = total + swap(both16[t], "rows", n, t).astype(f32)
    values = (total[:leaf_per] / (total[leaf_per:] + ridge_term)).astype(bf16)
    table = jnp.stack([values] + [swap(values, "rows", n, t) for t in range(1, n)]).astype(f32)
    updated, leaf_values = update_pass(me.reshape(1), predictions, leaf, table)

    finals = []
    for p in range(parts):
        pair = (keep[p].astype(f32) + got[p].astype(f32)).astype(bf16)
        acc = pair.astype(f32)
        for t in range(2, nf, 2):
            acc = acc + swap(pair, "feat", nf, t).astype(f32)
        own = acc.astype(bf16)
        other = swap(own, "feat", nf, 1)
        away = hist_pass(codes, own, other, per, n // 2, 1, bf16)
        back = swap(away, "rows", n, 1)
        here = hist_pass(codes, own, other, per, n // 2, 0, bf16)
        acc = here.astype(f32) + back.astype(f32)
        acc16 = acc.astype(bf16)
        final = acc[0]
        for t in range(1, n // 2):
            final = final + swap(acc16[t], "rows", n, 2 * t).astype(f32)
        finals.append(final.reshape(per, feats, -1))
    histograms = jnp.concatenate(finals, axis=2)
    return histograms, leaf_values.reshape(LEAVES, cols), updated


def solution(mesh):
    n, nf = mesh.shape["rows"], mesh.shape["feat"]
    return jax.shard_map(
        functools.partial(local, n, nf),
        mesh=mesh,
        in_specs=(
            P("rows", "feat"),
            P("rows", "feat"),
            P("feat", "rows"),
            P("rows"),
            P("feat", None),
        ),
        out_specs=(P("rows", "feat", None), P(None, "feat"), P("rows", "feat")),
        check_vma=False,
    )
```

```python
import functools

import jax
import jax.numpy as jnp
from jax import lax
from jax.experimental import pallas as pl
from jax.experimental.pallas import tpu as pltpu
from jax.sharding import PartitionSpec as P

BINS = 256
LEAVES = 64


shrinkage = 0.5
ridge_term = 1.0

f32 = jnp.float32
bf16 = jnp.bfloat16
VMEM_LIMIT = 48 * 1024 * 1024


def block_rows(rows):
    for size in (256, 128, 64, 32, 16):
        if rows % size == 0:
            return size
    return rows


def cost(us):
    return pl.CostEstimate(flops=0, transcendentals=0, bytes_accessed=int(us * 3.69e6))


def swap(x, axis, size, by):
    return lax.ppermute(x, axis, [(i, i ^ by) for i in range(size)])


def sketch_kernel(core_ref, pred_ref, lab_ref, w_ref, out_ref):
    t = jnp.tanh(pred_ref[...].astype(f32) * 0.5)
    grad = ((lab_ref[...].astype(f32) - 0.5) - 0.5 * t).astype(bf16)
    out_ref[...] = jnp.dot(grad, w_ref[...], preferred_element_type=f32).astype(bf16)


def sketch_pass(which, pred, lab, w, name):
    rows, cols = pred.shape
    half = rows // 2
    blk = block_rows(half)
    steps = half // blk
    row_map = lambda i, c: (c[0] * steps + i, 0)
    return pl.pallas_call(
        sketch_kernel,
        grid_spec=pltpu.PrefetchScalarGridSpec(
            num_scalar_prefetch=1,
            grid=(steps,),
            in_specs=[
                pl.BlockSpec((blk, cols), row_map),
                pl.BlockSpec((blk, cols), row_map),
                pl.BlockSpec(w.shape, lambda i, c: (0, 0)),
            ],
            out_specs=pl.BlockSpec((blk, w.shape[1]), lambda i, c: (i, 0)),
        ),
        out_shape=jax.ShapeDtypeStruct((half, w.shape[1]), bf16),
        compiler_params=pltpu.CompilerParams(vmem_limit_bytes=VMEM_LIMIT),
        cost_estimate=cost(1.6),
        name=name,
    )(which, pred, lab, w)


def pair_kernel(keep_ref, got_ref, out_ref):
    out_ref[...] = (keep_ref[...].astype(f32) + got_ref[...].astype(f32)).astype(out_ref.dtype)


def pair_pass(keep, got, part, parts, name):
    rows, cols = keep.shape
    width = cols // parts
    spec = pl.BlockSpec((rows, width), lambda i: (0, part))
    return pl.pallas_call(
        pair_kernel,
        grid=(1,),
        in_specs=[spec, spec],
        out_specs=pl.BlockSpec((rows, width), lambda i: (0, 0)),
        out_shape=jax.ShapeDtypeStruct((rows, width), bf16),
        compiler_params=pltpu.CompilerParams(vmem_limit_bytes=VMEM_LIMIT),
        cost_estimate=cost(0.2),
        name=name,
    )(keep, got)


def leaf_kernel(side_ref, pred_ref, lab_ref, leaf_ref, after_ref, keep_ref, send_ref, g_ref, h_ref):
    step = pl.program_id(0)

    @pl.when(step == 0)
    def _():
        g_ref[...] = jnp.zeros_like(g_ref)
        h_ref[...] = jnp.zeros_like(h_ref)

    t = jnp.tanh(pred_ref[...].astype(f32) * 0.5)
    grad = ((lab_ref[...].astype(f32) - 0.5) - 0.5 * t).astype(bf16)
    hess = (0.25 - 0.25 * t * t).astype(bf16)
    blk = pred_ref.shape[0]
    leaf = leaf_ref[0] ^ (side_ref[0] * (LEAVES // 2))
    hot = (lax.broadcasted_iota(jnp.int32, (LEAVES, blk), 0) == leaf).astype(f32).astype(bf16)
    g_ref[...] += jnp.dot(hot, grad, preferred_element_type=f32)
    h_ref[...] += jnp.dot(hot, hess, preferred_element_type=f32)

    @pl.when(step == pl.num_programs(0) - 1)
    def _():
        half = LEAVES // 2
        keep_ref[:half] = g_ref[:half]
        keep_ref[half:] = h_ref[:half]
        send_ref[:half] = g_ref[half:].astype(bf16)
        send_ref[half:] = h_ref[half:].astype(bf16)


def leaf_pass(side, pred, lab, leaf, after):
    rows, cols = pred.shape
    blk = block_rows(rows)
    fixed = lambda i, c: (0, 0)
    return pl.pallas_call(
        leaf_kernel,
        grid_spec=pltpu.PrefetchScalarGridSpec(
            num_scalar_prefetch=1,
            grid=(rows // blk,),
            in_specs=[
                pl.BlockSpec((blk, cols), lambda i, c: (i, 0)),
                pl.BlockSpec((blk, cols), lambda i, c: (i, 0)),
                pl.BlockSpec((1, 1, blk), lambda i, c: (i, 0, 0)),
                pl.BlockSpec(memory_space=pl.ANY),
            ],
            out_specs=[pl.BlockSpec((LEAVES, cols), fixed)] * 2,
            scratch_shapes=[pltpu.VMEM((LEAVES, cols), f32)] * 2,
        ),
        out_shape=[
            jax.ShapeDtypeStruct((LEAVES, cols), f32),
            jax.ShapeDtypeStruct((LEAVES, cols), bf16),
        ],
        compiler_params=pltpu.CompilerParams(vmem_limit_bytes=VMEM_LIMIT),
        cost_estimate=cost(5.0),
        name="leaf_sums",
    )(side, pred, lab, leaf.reshape(rows // blk, 1, blk), after)


def hist_kernel(codes_ref, own_ref, other_ref, out_ref, *, per, odd, bits):
    feats = codes_ref.shape[1]
    half = codes_ref.shape[2]
    codes = codes_ref[...].astype(f32).astype(bf16)
    step = pl.program_id(0)
    place = sum(((step >> b) & 1) << (bits - 1 - b) for b in range(bits))
    base = (2 * place + odd) * per
    levels = (lax.broadcasted_iota(jnp.int32, (per, 1, 1), 0) + base).astype(f32).astype(bf16)
    one = jnp.ones((), bf16)
    zero = jnp.zeros((), bf16)
    total = None
    for part, ref in ((0, own_ref), (1, other_ref)):
        hot = jnp.where(codes[part][None] == levels, one, zero).reshape(per * feats, half)
        term = jnp.dot(hot, ref[...], preferred_element_type=f32)
        total = term if total is None else total + term
    out_ref[0] = total.astype(out_ref.dtype)


def hist_pass(codes, own, other, per, blocks, odd, dtype):
    feats = codes.shape[1]
    width = own.shape[1]
    whole = lambda a: pl.BlockSpec(a.shape, lambda i: (0,) * a.ndim)
    return pl.pallas_call(
        functools.partial(hist_kernel, per=per, odd=odd, bits=blocks.bit_length() - 1),
        grid=(blocks,),
        in_specs=[whole(codes), whole(own), whole(other)],
        out_specs=pl.BlockSpec((1, per * feats, width), lambda i: (i, 0, 0)),
        out_shape=jax.ShapeDtypeStruct((blocks, per * feats, width), dtype),
        compiler_params=pltpu.CompilerParams(vmem_limit_bytes=VMEM_LIMIT),
        cost_estimate=cost(1.5),
        name="hist_send" if odd else "hist_keep",
    )(codes, own, other)


def update_kernel(side_ref, pred_ref, leaf_ref, own_ref, other_ref, new_ref, values_ref):
    half = LEAVES // 2
    own, other = own_ref[...], other_ref[...]

    @pl.when(pl.program_id(0) == 0)
    def _():
        first = side_ref[0] == 0
        values_ref[:half] = jnp.where(first, own.astype(f32), other.astype(f32))
        values_ref[half:] = jnp.where(first, other.astype(f32), own.astype(f32))

    blk = pred_ref.shape[0]
    leaf = leaf_ref[0] ^ (side_ref[0] * half)
    hot = (lax.broadcasted_iota(jnp.int32, (LEAVES, blk), 0) == leaf).astype(f32).astype(bf16)
    table = jnp.concatenate([own, other], axis=0)
    found = lax.dot_general(hot, table, (((0,), (0,)), ((), ())), preferred_element_type=f32)
    new_ref[...] = (pred_ref[...].astype(f32) + shrinkage * found).astype(bf16)


def update_pass(side, pred, leaf, own, other):
    rows, cols = pred.shape
    blk = block_rows(rows)
    fixed = lambda i, m: (0, 0)
    return pl.pallas_call(
        update_kernel,
        grid_spec=pltpu.PrefetchScalarGridSpec(
            num_scalar_prefetch=1,
            grid=(rows // blk,),
            in_specs=[
                pl.BlockSpec((blk, cols), lambda i, m: (i, 0)),
                pl.BlockSpec((1, 1, blk), lambda i, m: (i, 0, 0)),
                pl.BlockSpec(own.shape, fixed),
                pl.BlockSpec(own.shape, fixed),
            ],
            out_specs=[
                pl.BlockSpec((blk, cols), lambda i, m: (i, 0)),
                pl.BlockSpec((LEAVES, cols), fixed),
            ],
        ),
        out_shape=[
            jax.ShapeDtypeStruct((rows, cols), bf16),
            jax.ShapeDtypeStruct((LEAVES, cols), f32),
        ],
        compiler_params=pltpu.CompilerParams(vmem_limit_bytes=VMEM_LIMIT),
        cost_estimate=cost(3.7),
        name="update",
    )(side, pred, leaf.reshape(rows // blk, 1, blk), own, other)


def last_kernel(*refs):
    out_ref = refs[-1]
    width = refs[0].shape[1]
    for p in range(len(refs) // 2):
        out_ref[:, p * width:(p + 1) * width] = refs[2 * p][...] + refs[2 * p + 1][...].astype(f32)


def last_pass(pairs):
    rows, width = pairs[0][0].shape
    return pl.pallas_call(
        last_kernel,
        out_shape=jax.ShapeDtypeStruct((rows, width * len(pairs)), f32),
        compiler_params=pltpu.CompilerParams(vmem_limit_bytes=VMEM_LIMIT),
        cost_estimate=cost(0.5),
        name="last_add",
    )(*[a for pair in pairs for a in pair])


def local(n, nf, predictions, labels, feature_codes, leaf_index, sketch_weight):
    rows, cols = predictions.shape
    feats = feature_codes.shape[0]
    half = rows // 2
    parts = 2
    width = sketch_weight.shape[1] // parts
    me = lax.axis_index("rows")
    core = lax.axis_index("feat") & 1
    side = (me & 1).reshape(1)
    per = BINS // n
    codes = (feature_codes ^ (me * per)).reshape(feats, 2, half)
    codes = jnp.where(core == 0, codes, codes[:, ::-1]).swapaxes(0, 1)

    pred = pltpu.with_memory_space_constraint(predictions, pltpu.HBM)
    lab = pltpu.with_memory_space_constraint(labels, pltpu.HBM)
    weight = pltpu.with_memory_space_constraint(sketch_weight, pltpu.HBM)

    send = sketch_pass((1 - core).reshape(1), pred, lab, weight, "sketch_send")
    got = swap(send, "feat", nf, 1)
    keep = sketch_pass(core.reshape(1), pred, lab, weight, "sketch_keep")
    pair = [pair_pass(keep, got, p, parts, "core_add") for p in range(parts)]
    owns = []
    for p in range(parts):
        own = pair[p]
        for t in range(2, nf, 2):
            own = pair_pass(own, swap(pair[p], "feat", nf, t), 0, 1, "feat_add")
        owns.append(own)

    kept, sent = leaf_pass(side, pred, lab, leaf_index, pair[0])
    acc = kept + swap(sent, "rows", n, 1).astype(f32)
    by = 2
    while by < n:
        acc16 = acc.astype(bf16)
        acc = acc16.astype(f32) + swap(acc16, "rows", n, by).astype(f32)
        by *= 2
    values = (acc[:LEAVES // 2] / (acc[LEAVES // 2:] + ridge_term)).astype(bf16)
    updated, leaf_values = update_pass(side, pred, leaf_index, values, swap(values, "rows", n, 1))

    pairs = []
    for p in range(parts):
        own = owns[p]
        other = swap(own, "feat", nf, 1)
        away = hist_pass(codes, own, other, per, n // 2, 1, bf16)
        back = swap(away, "rows", n, 1)
        here = hist_pass(codes, own, other, per, n // 2, 0, f32)
        blocks, by = n // 2, 2
        while blocks > 1:
            acc = here + back.astype(f32)
            blocks //= 2
            back = swap(acc[blocks:].astype(bf16), "rows", n, by)
            here = acc[:blocks]
            by *= 2
        pairs.append((here[0], back[0]))
    histograms = last_pass(pairs).reshape(per, feats, -1)
    return histograms, leaf_values, updated


def solution(mesh):
    n, nf = mesh.shape["rows"], mesh.shape["feat"]
    return jax.shard_map(
        functools.partial(local, n, nf),
        mesh=mesh,
        in_specs=(
            P("rows", "feat"),
            P("rows", "feat"),
            P("feat", "rows"),
            P("rows"),
            P("feat", None),
        ),
        out_specs=(P("rows", "feat", None), P(None, "feat"), P("rows", "feat")),
        check_vma=False,
    )
```

```python
import functools

import jax
import jax.numpy as jnp
from jax import lax
from jax.experimental import pallas as pl
from jax.experimental.pallas import tpu as pltpu
from jax.sharding import PartitionSpec as P

BINS = 256
LEAVES = 64


shrinkage = 0.5
ridge_term = 1.0

f32 = jnp.float32
bf16 = jnp.bfloat16
VMEM_LIMIT = 48 * 1024 * 1024


def block_rows(rows):
    for size in (256, 128, 64, 32, 16):
        if rows % size == 0:
            return size
    return rows


PARAMS = pltpu.CompilerParams(vmem_limit_bytes=VMEM_LIMIT)


def swap(x, axis, size, by):
    return lax.ppermute(x, axis, [(i, i ^ by) for i in range(size)])


def ordered(kernel, out_shape, args, after, name):
    def body(*refs):
        kernel(*refs[:len(args)], *refs[len(args) + 1:])

    many = isinstance(out_shape, (list, tuple))
    return pl.pallas_call(
        body,
        in_specs=[pl.BlockSpec(memory_space=pltpu.VMEM)] * len(args) + [pl.BlockSpec(memory_space=pl.ANY)],
        out_specs=[pl.BlockSpec(memory_space=pltpu.VMEM)] * len(out_shape)
        if many else pl.BlockSpec(memory_space=pltpu.VMEM),
        out_shape=out_shape,
        compiler_params=PARAMS,
        name=name,
    )(*args, after)


def rows_kernel(pos_ref, leaf_ref, pred_hbm, lab_hbm, w_hbm, send_ref, keep_ref, g_ref, h_ref,
                pred_buf, lab_buf, w_buf, pred_sem, lab_sem, w_sem):
    core, side = pos_ref[0], pos_ref[1]
    chunks, _, blk = leaf_ref.shape
    per_half = chunks // 2

    def place(i):
        half = 1 - core if i < per_half else core
        return half * per_half + i % per_half

    def copies(i):
        at = pl.ds(pl.multiple_of(place(i) * blk, blk), blk)
        return (pltpu.make_async_copy(pred_hbm.at[at], pred_buf.at[i], pred_sem.at[i]),
                pltpu.make_async_copy(lab_hbm.at[at], lab_buf.at[i], lab_sem.at[i]))

    w_copy = pltpu.make_async_copy(w_hbm, w_buf, w_sem)
    for i in range(chunks):
        for copy in copies(i):
            copy.start()
        if i == 0:
            w_copy.start()
    for i in range(chunks):
        for copy in copies(i):
            copy.wait()
        if i == 0:
            w_copy.wait()
        p = 0.5 * jnp.tanh((pred_buf[i] * 0.5).astype(f32)) + 0.5
        grad = (lab_buf[i].astype(f32) - p).astype(bf16)
        hess = (p - p * p).astype(bf16)
        out = send_ref if i < per_half else keep_ref
        out[pl.ds(i % per_half * blk, blk)] = jnp.dot(grad, w_buf[...], preferred_element_type=f32).astype(bf16)
        leaf = leaf_ref[place(i)] ^ (side * (LEAVES // 2))
        hot = (lax.broadcasted_iota(jnp.int32, (LEAVES, blk), 0) == leaf).astype(f32).astype(bf16)
        g = jnp.dot(hot, grad, preferred_element_type=f32)
        h = jnp.dot(hot, hess, preferred_element_type=f32)
        if i == 0:
            g_ref[...] = g
            h_ref[...] = h
        else:
            g_ref[...] += g
            h_ref[...] += h


def rows_pass(pos, leaf, pred, lab, w):
    chunks, _, blk = leaf.shape
    rows, cols = pred.shape
    vmem = pl.BlockSpec(memory_space=pltpu.VMEM)
    hbm = pl.BlockSpec(memory_space=pl.ANY)
    return pl.pallas_call(
        rows_kernel,
        in_specs=[pl.BlockSpec(memory_space=pltpu.SMEM), vmem, hbm, hbm, hbm],
        out_specs=[vmem] * 4,
        out_shape=[jax.ShapeDtypeStruct((rows // 2, w.shape[1]), bf16)] * 2
        + [jax.ShapeDtypeStruct((LEAVES, cols), f32)] * 2,
        scratch_shapes=[
            pltpu.VMEM((chunks, blk, cols), bf16),
            pltpu.VMEM((chunks, blk, cols), bf16),
            pltpu.VMEM(w.shape, bf16),
            pltpu.SemaphoreType.DMA((chunks,)),
            pltpu.SemaphoreType.DMA((chunks,)),
            pltpu.SemaphoreType.DMA,
        ],
        compiler_params=PARAMS,
        name="rows",
    )(pos, leaf, pred, lab, w)


def part_add(part, parts):
    def kernel(a_ref, b_ref, out_ref):
        width = out_ref.shape[1]
        at = slice(part * width, (part + 1) * width)
        out_ref[...] = (a_ref[:, at].astype(f32) + b_ref[:, at].astype(f32)).astype(bf16)
    return kernel


def add_kernel(a_ref, b_ref, out_ref):
    out_ref[...] = (a_ref[...].astype(f32) + b_ref[...].astype(f32)).astype(out_ref.dtype)


def leaf_pack_kernel(g_ref, h_ref, keep_ref, send_ref):
    half = LEAVES // 2
    keep_ref[:half] = g_ref[:half]
    keep_ref[half:] = h_ref[:half]
    send_ref[:half] = g_ref[half:].astype(bf16)
    send_ref[half:] = h_ref[half:].astype(bf16)


def value_kernel(a_ref, b_ref, out_ref):
    half = LEAVES // 2
    total = a_ref[...].astype(f32) + b_ref[...].astype(f32)
    out_ref[...] = (total[:half] / (total[half:] + ridge_term)).astype(bf16)


def halving_kernel(here_ref, back_ref, keep_ref, send_ref):
    half = keep_ref.shape[0]
    keep_ref[...] = here_ref[:half] + back_ref[:half].astype(f32)
    send_ref[...] = (here_ref[half:] + back_ref[half:].astype(f32)).astype(bf16)


def last_kernel(*refs):
    out_ref = refs[-1]
    width = refs[0].shape[2]
    for p in range(len(refs) // 2):
        out_ref[:, p * width:(p + 1) * width] = refs[2 * p][0] + refs[2 * p + 1][0].astype(f32)


def hist_kernel(codes_ref, own_ref, other_ref, after_ref, out_ref, *, per, odd, bits):
    feats = codes_ref.shape[1]
    half = codes_ref.shape[2]
    codes = codes_ref[...].astype(f32).astype(bf16)
    step = pl.program_id(0)
    place = sum(((step >> b) & 1) << (bits - 1 - b) for b in range(bits))
    base = (2 * place + odd) * per
    levels = (lax.broadcasted_iota(jnp.int32, (per, 1, 1), 0) + base).astype(f32).astype(bf16)
    one = jnp.ones((), bf16)
    zero = jnp.zeros((), bf16)
    total = None
    for part, ref in ((0, own_ref), (1, other_ref)):
        hot = jnp.where(codes[part][None] == levels, one, zero).reshape(per * feats, half)
        term = jnp.dot(hot, ref[...], preferred_element_type=f32)
        total = term if total is None else total + term
    out_ref[0] = total.astype(out_ref.dtype)


def hist_pass(codes, own, other, per, blocks, odd, dtype, after):
    feats = codes.shape[1]
    width = own.shape[1]
    whole = lambda a: pl.BlockSpec(a.shape, lambda i: (0,) * a.ndim)
    return pl.pallas_call(
        functools.partial(hist_kernel, per=per, odd=odd, bits=blocks.bit_length() - 1),
        grid=(blocks,),
        in_specs=[whole(codes), whole(own), whole(other), pl.BlockSpec(memory_space=pl.ANY)],
        out_specs=pl.BlockSpec((1, per * feats, width), lambda i: (i, 0, 0)),
        out_shape=jax.ShapeDtypeStruct((blocks, per * feats, width), dtype),
        compiler_params=PARAMS,
        name="hist_send" if odd else "hist_keep",
    )(codes, own, other, after)


def update_kernel(pos_ref, leaf_ref, own_ref, other_ref, pred_hbm, after_ref, new_hbm, values_ref,
                  pred_buf, new_buf, pred_sem, new_sem):
    side = pos_ref[1]
    chunks, _, blk = leaf_ref.shape
    half = LEAVES // 2

    def read(i):
        return pltpu.make_async_copy(pred_hbm.at[pl.ds(i * blk, blk)], pred_buf.at[i], pred_sem.at[i])

    def write(i):
        return pltpu.make_async_copy(new_buf.at[i], new_hbm.at[pl.ds(i * blk, blk)], new_sem.at[i])

    for i in range(chunks):
        read(i).start()
    own, other = own_ref[...], other_ref[...]
    first = side == 0
    values_ref[:half] = jnp.where(first, own.astype(f32), other.astype(f32))
    values_ref[half:] = jnp.where(first, other.astype(f32), own.astype(f32))
    table = jnp.concatenate([own, other], axis=0)
    for i in range(chunks):
        leaf = leaf_ref[i] ^ (side * half)
        hot = (lax.broadcasted_iota(jnp.int32, (LEAVES, blk), 0) == leaf).astype(f32) * shrinkage
        found = lax.dot_general(hot.astype(bf16), table, (((0,), (0,)), ((), ())), preferred_element_type=f32)
        read(i).wait()
        new_buf[i] = (pred_buf[i].astype(f32) + found).astype(bf16)
        write(i).start()
    for i in range(chunks):
        write(i).wait()


def update_pass(pos, leaf, own, other, pred, after):
    chunks, _, blk = leaf.shape
    rows, cols = pred.shape
    vmem = pl.BlockSpec(memory_space=pltpu.VMEM)
    hbm = pl.BlockSpec(memory_space=pl.ANY)
    return pl.pallas_call(
        update_kernel,
        in_specs=[pl.BlockSpec(memory_space=pltpu.SMEM), vmem, vmem, vmem, hbm, hbm],
        out_specs=[hbm, vmem],
        out_shape=[
            jax.ShapeDtypeStruct((rows, cols), bf16),
            jax.ShapeDtypeStruct((LEAVES, cols), f32),
        ],
        scratch_shapes=[
            pltpu.VMEM((chunks, blk, cols), bf16),
            pltpu.VMEM((chunks, blk, cols), bf16),
            pltpu.SemaphoreType.DMA((chunks,)),
            pltpu.SemaphoreType.DMA((chunks,)),
        ],
        compiler_params=PARAMS,
        name="update",
    )(pos, leaf, own, other, pred, after)


def local(n, nf, predictions, labels, feature_codes, leaf_index, sketch_weight):
    rows, cols = predictions.shape
    feats = feature_codes.shape[0]
    half = rows // 2
    parts = 2
    width = sketch_weight.shape[1] // parts
    me = lax.axis_index("rows")
    core = lax.axis_index("feat") & 1
    pos = jnp.stack([core, me & 1])
    per = BINS // n
    codes = (feature_codes ^ (me * per)).reshape(feats, 2, half)
    codes = jnp.where(core == 0, codes, codes[:, ::-1]).swapaxes(0, 1)
    blk = block_rows(half)
    leaf = leaf_index.reshape(rows // blk, 1, blk)

    pred = pltpu.with_memory_space_constraint(predictions, pltpu.HBM)
    lab = pltpu.with_memory_space_constraint(labels, pltpu.HBM)
    weight = pltpu.with_memory_space_constraint(sketch_weight, pltpu.HBM)
    sketch16 = jax.ShapeDtypeStruct((half, width), bf16)
    sums16 = jax.ShapeDtypeStruct((LEAVES, cols), bf16)
    sums32 = jax.ShapeDtypeStruct((LEAVES, cols), f32)

    send, keep, grad, hess = rows_pass(pos, leaf, pred, lab, weight)
    got = swap(send, "feat", nf, 1)
    pair, crossed, after = [], [], keep
    for p in range(parts):
        after = ordered(part_add(p, parts), sketch16, [keep, got], after, "core_add")
        pair.append(after)
        crossed.append([swap(after, "feat", nf, t) for t in range(2, nf, 2)])

    leaf_acc, sent = ordered(leaf_pack_kernel, [sums32, sums16], [grad, hess], after, "leaf_pack")
    leaf_got, leaf_by = swap(sent, "rows", n, 1), 2
    after = leaf_acc

    def leaf_step(acc, got, by, after):
        if by < n:
            acc = ordered(add_kernel, sums16, [acc, got], after, "leaf_add")
            return acc, swap(acc, "rows", n, by), 2 * by, acc
        if by == n:
            values16 = jax.ShapeDtypeStruct((LEAVES // 2, cols), bf16)
            acc = ordered(value_kernel, values16, [acc, got], after, "leaf_value")
            return acc, swap(acc, "rows", n, 1), 2 * by, acc
        return acc, got, by, after

    owns, others, backs, heres = [], [], [], []
    for p in range(parts):
        own = pair[p]
        for recv in crossed[p]:
            own = ordered(add_kernel, sketch16, [own, recv], after, "feat_add")
        owns.append(own)
        others.append(swap(own, "feat", nf, 1))
        after = hist_pass(codes, own, others[p], per, n // 2, 1, bf16, own)
        backs.append(swap(after, "rows", n, 1))
        if p == 0:
            leaf_acc, leaf_got, leaf_by, after = leaf_step(leaf_acc, leaf_got, leaf_by, after)
    after = hist_pass(codes, owns[0], others[0], per, n // 2, 0, f32, after)
    heres.append(after)

    levels = (n // 2).bit_length() - 1
    for slot in range(levels + parts - 1):
        for p in range(parts):
            level = slot - p
            if 0 <= level < levels:
                blocks = heres[p].shape[0] // 2
                shape = (blocks,) + heres[p].shape[1:]
                after, sent = ordered(
                    halving_kernel,
                    [jax.ShapeDtypeStruct(shape, f32), jax.ShapeDtypeStruct(shape, bf16)],
                    [heres[p], backs[p]], after, "hist_add")
                heres[p] = after
                backs[p] = swap(sent, "rows", n, 2 << level)
                if p == 1:
                    continue
                leaf_acc, leaf_got, leaf_by, after = leaf_step(leaf_acc, leaf_got, leaf_by, after)
                if slot == 0:
                    after = hist_pass(codes, owns[1], others[1], per, n // 2, 0, f32, after)
                    heres.append(after)
    while leaf_by <= n:
        leaf_acc, leaf_got, leaf_by, after = leaf_step(leaf_acc, leaf_got, leaf_by, after)
    updated, leaf_values = update_pass(pos, leaf, leaf_acc, leaf_got, pred, after)
    histograms = ordered(
        last_kernel, jax.ShapeDtypeStruct((per * feats, width * parts), f32),
        [a for p in range(parts) for a in (heres[p], backs[p])], leaf_values, "last_add")
    return histograms.reshape(per, feats, -1), leaf_values, updated


def solution(mesh):
    n, nf = mesh.shape["rows"], mesh.shape["feat"]
    return jax.shard_map(
        functools.partial(local, n, nf),
        mesh=mesh,
        in_specs=(
            P("rows", "feat"),
            P("rows", "feat"),
            P("feat", "rows"),
            P("rows"),
            P("feat", None),
        ),
        out_specs=(P("rows", "feat", None), P(None, "feat"), P("rows", "feat")),
        check_vma=False,
    )
```

```python
import functools

import jax
import jax.numpy as jnp
from jax import lax
from jax.experimental import pallas as pl
from jax.experimental.pallas import tpu as pltpu
from jax.sharding import PartitionSpec as P

BINS = 256
LEAVES = 64


shrinkage = 0.5
ridge_term = 1.0

f32 = jnp.float32
bf16 = jnp.bfloat16
VMEM_LIMIT = 48 * 1024 * 1024


def block_rows(rows):
    for size in (256, 128, 64, 32, 16):
        if rows % size == 0:
            return size
    return rows


PARAMS = pltpu.CompilerParams(vmem_limit_bytes=VMEM_LIMIT)


def swap(x, axis, size, by):
    return lax.ppermute(x, axis, [(i, i ^ by) for i in range(size)])


def ordered(kernel, out_shape, args, after, name):
    def body(*refs):
        kernel(*refs[:len(args)], *refs[len(args) + 1:])

    many = isinstance(out_shape, (list, tuple))
    return pl.pallas_call(
        body,
        in_specs=[pl.BlockSpec(memory_space=pltpu.VMEM)] * len(args) + [pl.BlockSpec(memory_space=pl.ANY)],
        out_specs=[pl.BlockSpec(memory_space=pltpu.VMEM)] * len(out_shape)
        if many else pl.BlockSpec(memory_space=pltpu.VMEM),
        out_shape=out_shape,
        compiler_params=PARAMS,
        name=name,
    )(*args, after)


def leaf_hot(leaf_ref, chunk, blk, flip, scale):
    lanes = leaf_ref.shape[1]
    lines = blk // lanes
    leaf = jnp.concatenate([leaf_ref[pl.ds(chunk * lines + j, 1)] for j in range(lines)], axis=1)
    hot = lax.broadcasted_iota(jnp.int32, (LEAVES, blk), 0) == (leaf ^ flip)
    return jnp.where(hot, f32(scale), f32(0)).astype(bf16)


def chunk_place(i, chunks, core):
    per_half = chunks // 2
    half = 1 - core if i < per_half else core
    return half * per_half + i % per_half


def rows_kernel(pos_ref, leaf_hbm, pred_hbm, lab_hbm, w_hbm, send_ref, keep_ref, g_ref, h_ref, pred_buf,
                leaf_buf, lab_buf, w_buf, pred_sem, lab_sem, w_sem, leaf_sem):
    core, side = pos_ref[0], pos_ref[1]
    chunks, blk, _ = pred_buf.shape
    per_half = chunks // 2

    def copies(i):
        at = pl.ds(pl.multiple_of(chunk_place(i, chunks, core) * blk, blk), blk)
        return (pltpu.make_async_copy(pred_hbm.at[at], pred_buf.at[i], pred_sem.at[i]),
                pltpu.make_async_copy(lab_hbm.at[at], lab_buf.at[i], lab_sem.at[i]))

    w_copy = pltpu.make_async_copy(w_hbm, w_buf, w_sem)
    leaf_copy = pltpu.make_async_copy(leaf_hbm, leaf_buf, leaf_sem)
    for i in range(chunks):
        for j, copy in enumerate(copies(i)):
            copy.start(priority=j)
        if i == 0:
            w_copy.start()
            leaf_copy.start(priority=1)
    for i in range(chunks):
        for copy in copies(i):
            copy.wait()
        if i == 0:
            w_copy.wait()
            leaf_copy.wait()
        p = 0.5 * jnp.tanh((pred_buf[i] * 0.5).astype(f32)) + 0.5
        grad = (lab_buf[i].astype(f32) - p).astype(bf16)
        hess = (p - p * p).astype(bf16)
        out = send_ref if i < per_half else keep_ref
        out[pl.ds(i % per_half * blk, blk)] = jnp.dot(grad, w_buf[...], preferred_element_type=f32).astype(bf16)
        hot = leaf_hot(leaf_buf, chunk_place(i, chunks, core), blk, side * (LEAVES // 2), 1.0)
        g = jnp.dot(hot, grad, preferred_element_type=f32)
        h = jnp.dot(hot, hess, preferred_element_type=f32)
        if i == 0:
            g_ref[...] = g
            h_ref[...] = h
        else:
            g_ref[...] += g
            h_ref[...] += h


def rows_pass(pos, leaf, pred, lab, w):
    rows, cols = pred.shape
    blk = block_rows(rows // 2)
    chunks = rows // blk
    vmem = pl.BlockSpec(memory_space=pltpu.VMEM)
    hbm = pl.BlockSpec(memory_space=pl.ANY)
    return pl.pallas_call(
        rows_kernel,
        in_specs=[pl.BlockSpec(memory_space=pltpu.SMEM), hbm, hbm, hbm, hbm],
        out_specs=[vmem] * 5,
        out_shape=[jax.ShapeDtypeStruct((rows // 2, w.shape[1]), bf16)] * 2
        + [jax.ShapeDtypeStruct((LEAVES, cols), f32)] * 2
        + [jax.ShapeDtypeStruct((chunks, blk, cols), bf16)],
        scratch_shapes=[
            pltpu.VMEM(leaf.shape, jnp.int32),
            pltpu.VMEM((chunks, blk, cols), bf16),
            pltpu.VMEM(w.shape, bf16),
            pltpu.SemaphoreType.DMA((chunks,)),
            pltpu.SemaphoreType.DMA((chunks,)),
            pltpu.SemaphoreType.DMA,
            pltpu.SemaphoreType.DMA,
        ],
        compiler_params=PARAMS,
        name="rows",
    )(pos, leaf, pred, lab, w)


def part_add(part, parts):
    def kernel(a_ref, b_ref, out_ref):
        width = out_ref.shape[1]
        at = slice(part * width, (part + 1) * width)
        out_ref[...] = (a_ref[:, at].astype(f32) + b_ref[:, at].astype(f32)).astype(bf16)
    return kernel


def add_kernel(a_ref, b_ref, out_ref):
    out_ref[...] = (a_ref[...].astype(f32) + b_ref[...].astype(f32)).astype(out_ref.dtype)


def leaf_pack_kernel(g_ref, h_ref, keep_ref, send_ref):
    half = LEAVES // 2
    keep_ref[:half] = g_ref[:half]
    keep_ref[half:] = h_ref[:half]
    send_ref[:half] = g_ref[half:].astype(bf16)
    send_ref[half:] = h_ref[half:].astype(bf16)


def value_kernel(a_ref, b_ref, out_ref):
    half = LEAVES // 2
    total = a_ref[...].astype(f32) + b_ref[...].astype(f32)
    out_ref[...] = (total[:half] / (total[half:] + ridge_term)).astype(bf16)


def halving_kernel(here_ref, back_ref, keep_ref, send_ref):
    half = keep_ref.shape[0]
    keep_ref[...] = here_ref[:half] + back_ref[:half].astype(f32)
    send_ref[...] = (here_ref[half:] + back_ref[half:].astype(f32)).astype(bf16)


def last_kernel(*refs):
    out_ref = refs[-1]
    width = refs[0].shape[2]
    for p in range(len(refs) // 2):
        out_ref[:, p * width:(p + 1) * width] = refs[2 * p][0] + refs[2 * p + 1][0].astype(f32)


def hist_kernel(codes_ref, own_ref, other_ref, after_ref, out_ref, *, per, odd, bits):
    feats = codes_ref.shape[1]
    half = codes_ref.shape[2]
    codes = codes_ref[...].astype(f32).astype(bf16)
    step = pl.program_id(0)
    place = sum(((step >> b) & 1) << (bits - 1 - b) for b in range(bits))
    base = (2 * place + odd) * per
    levels = (lax.broadcasted_iota(jnp.int32, (per, 1, 1), 0) + base).astype(f32).astype(bf16)
    one = jnp.ones((), bf16)
    zero = jnp.zeros((), bf16)
    total = None
    for part, ref in ((0, own_ref), (1, other_ref)):
        hot = jnp.where(codes[part][None] == levels, one, zero).reshape(per * feats, half)
        term = jnp.dot(hot, ref[...], preferred_element_type=f32)
        total = term if total is None else total + term
    out_ref[0] = total.astype(out_ref.dtype)


def hist_pass(codes, own, other, per, blocks, odd, dtype, after):
    feats = codes.shape[1]
    width = own.shape[1]
    whole = lambda a: pl.BlockSpec(a.shape, lambda i: (0,) * a.ndim)
    return pl.pallas_call(
        functools.partial(hist_kernel, per=per, odd=odd, bits=blocks.bit_length() - 1),
        grid=(blocks,),
        in_specs=[whole(codes), whole(own), whole(other), pl.BlockSpec(memory_space=pl.ANY)],
        out_specs=pl.BlockSpec((1, per * feats, width), lambda i: (i, 0, 0)),
        out_shape=jax.ShapeDtypeStruct((blocks, per * feats, width), dtype),
        compiler_params=PARAMS,
        name="hist_send" if odd else "hist_keep",
    )(codes, own, other, after)


def update_kernel(pos_ref, leaf_ref, own_ref, other_ref, pred_ref, after_ref, new_hbm, values_hbm, done_ref,
                  new_buf, values_buf, new_sem, values_sem):
    core, side = pos_ref[0], pos_ref[1]
    chunks, blk, _ = pred_ref.shape
    half = LEAVES // 2

    def write(i):
        at = pl.ds(pl.multiple_of(chunk_place(i, chunks, core) * blk, blk), blk)
        return pltpu.make_async_copy(new_buf.at[i], new_hbm.at[at], new_sem.at[i])

    own, other = own_ref[...], other_ref[...]
    first = side == 0
    values_buf[:half] = jnp.where(first, own.astype(f32), other.astype(f32))
    values_buf[half:] = jnp.where(first, other.astype(f32), own.astype(f32))
    values_copy = pltpu.make_async_copy(values_buf, values_hbm, values_sem)
    values_copy.start(priority=1)
    table = jnp.concatenate([own, other], axis=0)
    for i in range(chunks):
        hot = leaf_hot(leaf_ref, chunk_place(i, chunks, core), blk, side * half, shrinkage)
        found = lax.dot_general(hot, table, (((0,), (0,)), ((), ())), preferred_element_type=f32)
        new_buf[i] = (pred_ref[i].astype(f32) + found).astype(bf16)
        write(i).start(priority=i % 2)
    done_ref[...] = jnp.zeros_like(done_ref)
    values_copy.wait()
    for i in range(chunks):
        write(i).wait()


def update_pass(pos, leaf, own, other, pred, after):
    chunks, blk, cols = pred.shape
    vmem = pl.BlockSpec(memory_space=pltpu.VMEM)
    hbm = pl.BlockSpec(memory_space=pl.ANY)
    return pl.pallas_call(
        update_kernel,
        in_specs=[pl.BlockSpec(memory_space=pltpu.SMEM), vmem, vmem, vmem, vmem, hbm],
        out_specs=[pl.BlockSpec(memory_space=pltpu.HBM)] * 2 + [vmem],
        out_shape=[
            jax.ShapeDtypeStruct((chunks * blk, cols), bf16),
            jax.ShapeDtypeStruct((LEAVES, cols), f32),
            jax.ShapeDtypeStruct((8, 128), f32),
        ],
        scratch_shapes=[
            pltpu.VMEM((chunks, blk, cols), bf16),
            pltpu.VMEM((LEAVES, cols), f32),
            pltpu.SemaphoreType.DMA((chunks,)),
            pltpu.SemaphoreType.DMA,
        ],
        compiler_params=PARAMS,
        name="update",
    )(pos, leaf, own, other, pred, after)


def local(n, nf, predictions, labels, feature_codes, leaf_index, sketch_weight):
    rows, cols = predictions.shape
    feats = feature_codes.shape[0]
    half = rows // 2
    parts = 2
    width = sketch_weight.shape[1] // parts
    me = lax.axis_index("rows")
    core = lax.axis_index("feat") & 1
    pos = jnp.stack([core, me & 1])
    per = BINS // n
    codes = (feature_codes ^ (me * per)).reshape(feats, 2, half)
    codes = jnp.where(core == 0, codes, codes[:, ::-1]).swapaxes(0, 1)
    lanes = min(128, block_rows(half))
    leaf = leaf_index.reshape(rows // lanes, lanes)

    pred = pltpu.with_memory_space_constraint(predictions, pltpu.HBM)
    lab = pltpu.with_memory_space_constraint(labels, pltpu.HBM)
    weight = pltpu.with_memory_space_constraint(sketch_weight, pltpu.HBM)
    sketch16 = jax.ShapeDtypeStruct((half, width), bf16)
    sums16 = jax.ShapeDtypeStruct((LEAVES, cols), bf16)
    sums32 = jax.ShapeDtypeStruct((LEAVES, cols), f32)

    send, keep, grad, hess, held = rows_pass(pos, pltpu.with_memory_space_constraint(leaf, pltpu.HBM), pred, lab, weight)
    got = swap(send, "feat", nf, 1)
    pair, crossed, after = [], [], keep
    for p in range(parts):
        after = ordered(part_add(p, parts), sketch16, [keep, got], after, "core_add")
        pair.append(after)
        crossed.append([swap(after, "feat", nf, t) for t in range(2, nf, 2)])
        if p == 0:
            after, sent = ordered(leaf_pack_kernel, [sums32, sums16], [grad, hess], after, "leaf_pack")
            leaf_state = (after, swap(sent, "rows", n, 1), 2)

    def leaf_step(after):
        nonlocal leaf_state
        acc, got, by = leaf_state
        if by < n:
            acc = ordered(add_kernel, sums16, [acc, got], after, "leaf_add")
            leaf_state = (acc, swap(acc, "rows", n, by), 2 * by)
        elif by == n:
            values16 = jax.ShapeDtypeStruct((LEAVES // 2, cols), bf16)
            acc = ordered(value_kernel, values16, [acc, got], after, "leaf_value")
            leaf_state = (acc, swap(acc, "rows", n, 1), 2 * by)
        else:
            return after
        return acc

    owns, others, backs, heres = [], [], [], []
    for p in range(parts):
        own = pair[p]
        for recv in crossed[p]:
            after = own = ordered(add_kernel, sketch16, [own, recv], after, "feat_add")
        owns.append(own)
        others.append(swap(own, "feat", nf, 1))
        if p > 0:
            after = hist_pass(codes, owns[p - 1], others[p - 1], per, n // 2, 0, f32, after)
            heres.append(after)
        after = leaf_step(after)
        after = hist_pass(codes, own, others[p], per, n // 2, 1, bf16, after)
        backs.append(swap(after, "rows", n, 1))
    after = hist_pass(codes, owns[-1], others[-1], per, n // 2, 0, f32, after)
    heres.append(after)

    levels = (n // 2).bit_length() - 1
    for slot in range(levels + parts - 1):
        for p in range(parts):
            level = slot - p
            if 0 <= level < levels:
                if p == parts - 1 and level == levels - 1:
                    while leaf_state[2] <= n:
                        after = leaf_step(after)
                    updated, leaf_values, after = update_pass(
                        pos, leaf, leaf_state[0], leaf_state[1], held, after)
                blocks = heres[p].shape[0] // 2
                shape = (blocks,) + heres[p].shape[1:]
                after, sent = ordered(
                    halving_kernel,
                    [jax.ShapeDtypeStruct(shape, f32), jax.ShapeDtypeStruct(shape, bf16)],
                    [heres[p], backs[p]], after, "hist_add")
                heres[p] = after
                backs[p] = swap(sent, "rows", n, 2 << level)
                if slot == 0:
                    after = leaf_step(after)
    histograms = ordered(
        last_kernel, jax.ShapeDtypeStruct((per * feats, width * parts), f32),
        [a for p in range(parts) for a in (heres[p], backs[p])], after, "last_add")
    return histograms.reshape(per, feats, -1), leaf_values, updated


def solution(mesh):
    n, nf = mesh.shape["rows"], mesh.shape["feat"]
    return jax.shard_map(
        functools.partial(local, n, nf),
        mesh=mesh,
        in_specs=(
            P("rows", "feat"),
            P("rows", "feat"),
            P("feat", "rows"),
            P("rows"),
            P("feat", None),
        ),
        out_specs=(P("rows", "feat", None), P(None, "feat"), P("rows", "feat")),
        check_vma=False,
    )
```

```python
import functools

import jax
import jax.numpy as jnp
from jax import lax
from jax.experimental import pallas as pl
from jax.experimental.pallas import tpu as pltpu
from jax.sharding import PartitionSpec as P

BINS = 256
LEAVES = 64


shrinkage = 0.5
ridge_term = 1.0

f32 = jnp.float32
bf16 = jnp.bfloat16
VMEM_LIMIT = 16 * 1024 * 1024


def block_rows(rows):
    for size in (256, 128, 64, 32, 16):
        if rows % size == 0:
            return size
    return rows


PARAMS = pltpu.CompilerParams(vmem_limit_bytes=VMEM_LIMIT)


def swap(x, axis, size, by):
    return lax.ppermute(x, axis, [(i, i ^ by) for i in range(size)])


def ordered(kernel, out_shape, args, after, name):
    def body(*refs):
        kernel(*refs[:len(args)], *refs[len(args) + 1:])

    many = isinstance(out_shape, (list, tuple))
    return pl.pallas_call(
        body,
        in_specs=[pl.BlockSpec(memory_space=pltpu.VMEM)] * len(args) + [pl.BlockSpec(memory_space=pl.ANY)],
        out_specs=[pl.BlockSpec(memory_space=pltpu.VMEM)] * len(out_shape)
        if many else pl.BlockSpec(memory_space=pltpu.VMEM),
        out_shape=out_shape,
        compiler_params=PARAMS,
        name=name,
    )(*args, after)


def leaf_hot(leaf_ref, chunk, blk, flip, scale):
    lanes = leaf_ref.shape[1]
    lines = blk // lanes
    leaf = jnp.concatenate([leaf_ref[pl.ds(chunk * lines + j, 1)] for j in range(lines)], axis=1)
    hot = lax.broadcasted_iota(jnp.int32, (LEAVES, blk), 0) == (leaf ^ flip)
    return jnp.where(hot, f32(scale), f32(0)).astype(bf16)


def chunk_place(i, chunks, core):
    per_half = chunks // 2
    half = 1 - core if i < per_half else core
    return half * per_half + i % per_half


def rows_kernel(pos_ref, leaf_hbm, pred_hbm, lab_hbm, w_hbm, send_ref, keep_ref, g_ref, h_ref, pred_buf,
                leaf_buf, lab_buf, w_buf, pred_sem, lab_sem, w_sem, leaf_sem):
    core, side = pos_ref[0], pos_ref[1]
    chunks, blk, _ = pred_buf.shape
    per_half = chunks // 2

    def copies(i):
        at = pl.ds(pl.multiple_of(chunk_place(i, chunks, core) * blk, blk), blk)
        return (pltpu.make_async_copy(pred_hbm.at[at], pred_buf.at[i], pred_sem.at[i]),
                pltpu.make_async_copy(lab_hbm.at[at], lab_buf.at[i], lab_sem.at[i]))

    w_copy = pltpu.make_async_copy(w_hbm, w_buf, w_sem)
    leaf_copy = pltpu.make_async_copy(leaf_hbm, leaf_buf, leaf_sem)
    for i in range(chunks):
        for j, copy in enumerate(copies(i)):
            copy.start(priority=j)
        if i == 0:
            w_copy.start()
            leaf_copy.start(priority=1)
    for i in range(chunks):
        for copy in copies(i):
            copy.wait()
        if i == 0:
            w_copy.wait()
            leaf_copy.wait()
        p = 0.5 * jnp.tanh((pred_buf[i] * 0.5).astype(f32)) + 0.5
        grad = (lab_buf[i].astype(f32) - p).astype(bf16)
        hess = (p - p * p).astype(bf16)
        out = send_ref if i < per_half else keep_ref
        out[pl.ds(i % per_half * blk, blk)] = jnp.dot(grad, w_buf[...], preferred_element_type=f32).astype(bf16)
        hot = leaf_hot(leaf_buf, chunk_place(i, chunks, core), blk, side * (LEAVES // 2), 1.0)
        g = jnp.dot(hot, grad, preferred_element_type=f32)
        h = jnp.dot(hot, hess, preferred_element_type=f32)
        if i == 0:
            g_ref[...] = g
            h_ref[...] = h
        else:
            g_ref[...] += g
            h_ref[...] += h


def rows_pass(pos, leaf, pred, lab, w):
    rows, cols = pred.shape
    blk = block_rows(rows // 2)
    chunks = rows // blk
    vmem = pl.BlockSpec(memory_space=pltpu.VMEM)
    hbm = pl.BlockSpec(memory_space=pl.ANY)
    return pl.pallas_call(
        rows_kernel,
        in_specs=[pl.BlockSpec(memory_space=pltpu.SMEM), hbm, hbm, hbm, hbm],
        out_specs=[vmem] * 5,
        out_shape=[jax.ShapeDtypeStruct((rows // 2, w.shape[1]), bf16)] * 2
        + [jax.ShapeDtypeStruct((LEAVES, cols), f32)] * 2
        + [jax.ShapeDtypeStruct((chunks, blk, cols), bf16)],
        scratch_shapes=[
            pltpu.VMEM(leaf.shape, jnp.int32),
            pltpu.VMEM((chunks, blk, cols), bf16),
            pltpu.VMEM(w.shape, bf16),
            pltpu.SemaphoreType.DMA((chunks,)),
            pltpu.SemaphoreType.DMA((chunks,)),
            pltpu.SemaphoreType.DMA,
            pltpu.SemaphoreType.DMA,
        ],
        compiler_params=PARAMS,
        name="rows",
    )(pos, leaf, pred, lab, w)


def part_add(part, parts):
    def kernel(a_ref, b_ref, out_ref):
        width = out_ref.shape[1]
        at = slice(part * width, (part + 1) * width)
        out_ref[...] = (a_ref[:, at].astype(f32) + b_ref[:, at].astype(f32)).astype(bf16)
    return kernel


def add_kernel(a_ref, b_ref, out_ref):
    out_ref[...] = (a_ref[...].astype(f32) + b_ref[...].astype(f32)).astype(out_ref.dtype)


def leaf_pack_kernel(g_ref, h_ref, keep_ref, send_ref):
    half = LEAVES // 2
    keep_ref[:half] = g_ref[:half]
    keep_ref[half:] = h_ref[:half]
    send_ref[:half] = g_ref[half:].astype(bf16)
    send_ref[half:] = h_ref[half:].astype(bf16)


def value_kernel(a_ref, b_ref, out_ref):
    half = LEAVES // 2
    total = a_ref[...].astype(f32) + b_ref[...].astype(f32)
    out_ref[...] = (total[:half] / (total[half:] + ridge_term)).astype(bf16)


def halving_kernel(here_ref, back_ref, keep_ref, send_ref):
    half = keep_ref.shape[0]
    keep_ref[...] = here_ref[:half] + back_ref[:half].astype(f32)
    send_ref[...] = (here_ref[half:] + back_ref[half:].astype(f32)).astype(bf16)


def last_kernel(*refs):
    out_ref = refs[-1]
    width = refs[0].shape[2]
    for p in range(len(refs) // 2):
        out_ref[:, p * width:(p + 1) * width] = refs[2 * p][0] + refs[2 * p + 1][0].astype(f32)


def hist_kernel(codes_ref, own_ref, other_ref, after_ref, out_ref, *, per, odd, bits):
    feats = codes_ref.shape[1]
    half = codes_ref.shape[2]
    codes = codes_ref[...].astype(f32).astype(bf16)
    step = pl.program_id(0)
    place = sum(((step >> b) & 1) << (bits - 1 - b) for b in range(bits))
    base = (2 * place + odd) * per
    levels = (lax.broadcasted_iota(jnp.int32, (per, 1, 1), 0) + base).astype(f32).astype(bf16)
    one = jnp.ones((), bf16)
    zero = jnp.zeros((), bf16)
    total = None
    for part, ref in ((0, own_ref), (1, other_ref)):
        hot = jnp.where(codes[part][None] == levels, one, zero).reshape(per * feats, half)
        term = jnp.dot(hot, ref[...], preferred_element_type=f32)
        total = term if total is None else total + term
    out_ref[0] = total.astype(out_ref.dtype)


def hist_pass(codes, own, other, per, blocks, odd, dtype, after):
    feats = codes.shape[1]
    width = own.shape[1]
    whole = lambda a: pl.BlockSpec(a.shape, lambda i: (0,) * a.ndim)
    return pl.pallas_call(
        functools.partial(hist_kernel, per=per, odd=odd, bits=blocks.bit_length() - 1),
        grid=(blocks,),
        in_specs=[whole(codes), whole(own), whole(other), pl.BlockSpec(memory_space=pl.ANY)],
        out_specs=pl.BlockSpec((1, per * feats, width), lambda i: (i, 0, 0)),
        out_shape=jax.ShapeDtypeStruct((blocks, per * feats, width), dtype),
        compiler_params=PARAMS,
        name="hist_send" if odd else "hist_keep",
    )(codes, own, other, after)


def update_kernel(pos_ref, leaf_ref, own_ref, other_ref, pred_ref, after_ref, new_hbm, values_hbm, done_ref,
                  new_buf, values_buf, new_sem, values_sem):
    core, side = pos_ref[0], pos_ref[1]
    chunks, blk, _ = pred_ref.shape
    half = LEAVES // 2

    def write(i):
        at = pl.ds(pl.multiple_of(chunk_place(i, chunks, core) * blk, blk), blk)
        return pltpu.make_async_copy(new_buf.at[i], new_hbm.at[at], new_sem.at[i])

    own, other = own_ref[...], other_ref[...]
    first = side == 0
    values_buf[:half] = jnp.where(first, own.astype(f32), other.astype(f32))
    values_buf[half:] = jnp.where(first, other.astype(f32), own.astype(f32))
    values_copy = pltpu.make_async_copy(values_buf, values_hbm, values_sem)
    values_copy.start(priority=1)
    table = jnp.concatenate([own, other], axis=0)
    for i in range(chunks):
        hot = leaf_hot(leaf_ref, chunk_place(i, chunks, core), blk, side * half, shrinkage)
        found = lax.dot_general(hot, table, (((0,), (0,)), ((), ())), preferred_element_type=f32)
        new_buf[i] = (pred_ref[i].astype(f32) + found).astype(bf16)
        write(i).start(priority=i % 2)
    done_ref[...] = jnp.zeros_like(done_ref)
    values_copy.wait()
    for i in range(chunks):
        write(i).wait()


def update_pass(pos, leaf, own, other, pred, after):
    chunks, blk, cols = pred.shape
    vmem = pl.BlockSpec(memory_space=pltpu.VMEM)
    hbm = pl.BlockSpec(memory_space=pl.ANY)
    return pl.pallas_call(
        update_kernel,
        in_specs=[pl.BlockSpec(memory_space=pltpu.SMEM), vmem, vmem, vmem, vmem, hbm],
        out_specs=[pl.BlockSpec(memory_space=pltpu.HBM)] * 2 + [vmem],
        out_shape=[
            jax.ShapeDtypeStruct((chunks * blk, cols), bf16),
            jax.ShapeDtypeStruct((LEAVES, cols), f32),
            jax.ShapeDtypeStruct((8, 128), f32),
        ],
        scratch_shapes=[
            pltpu.VMEM((chunks, blk, cols), bf16),
            pltpu.VMEM((LEAVES, cols), f32),
            pltpu.SemaphoreType.DMA((chunks,)),
            pltpu.SemaphoreType.DMA,
        ],
        compiler_params=PARAMS,
        name="update",
    )(pos, leaf, own, other, pred, after)


def local(n, nf, predictions, labels, feature_codes, leaf_index, sketch_weight):
    rows, cols = predictions.shape
    feats = feature_codes.shape[0]
    half = rows // 2
    parts = 2
    width = sketch_weight.shape[1] // parts
    me = lax.axis_index("rows")
    core = lax.axis_index("feat") & 1
    pos = jnp.stack([core, me & 1])
    per = BINS // n
    codes = (feature_codes ^ (me * per)).reshape(feats, 2, half)
    codes = jnp.where(core == 0, codes, codes[:, ::-1]).swapaxes(0, 1)
    lanes = min(128, block_rows(half))
    leaf = leaf_index.reshape(rows // lanes, lanes)

    pred = pltpu.with_memory_space_constraint(predictions, pltpu.HBM)
    lab = pltpu.with_memory_space_constraint(labels, pltpu.HBM)
    weight = pltpu.with_memory_space_constraint(sketch_weight, pltpu.HBM)
    sketch16 = jax.ShapeDtypeStruct((half, width), bf16)
    sums16 = jax.ShapeDtypeStruct((LEAVES, cols), bf16)
    sums32 = jax.ShapeDtypeStruct((LEAVES, cols), f32)

    send, keep, grad, hess, held = rows_pass(pos, pltpu.with_memory_space_constraint(leaf, pltpu.HBM), pred, lab, weight)
    got = swap(send, "feat", nf, 1)
    pair, crossed, after = [], [], keep
    for p in range(parts):
        after = ordered(part_add(p, parts), sketch16, [keep, got], after, "core_add")
        pair.append(after)
        crossed.append([swap(after, "feat", nf, t) for t in range(2, nf, 2)])
        if p == 0:
            after, sent = ordered(leaf_pack_kernel, [sums32, sums16], [grad, hess], after, "leaf_pack")
            leaf_state = (after, swap(sent, "rows", n, 1), 2)

    def leaf_step(after):
        nonlocal leaf_state
        acc, got, by = leaf_state
        if by < n:
            acc = ordered(add_kernel, sums16, [acc, got], after, "leaf_add")
            leaf_state = (acc, swap(acc, "rows", n, by), 2 * by)
        elif by == n:
            values16 = jax.ShapeDtypeStruct((LEAVES // 2, cols), bf16)
            acc = ordered(value_kernel, values16, [acc, got], after, "leaf_value")
            leaf_state = (acc, swap(acc, "rows", n, 1), 2 * by)
        else:
            return after
        return acc

    owns, others, backs, heres = [], [], [], []
    after = leaf_step(after)
    for p in range(parts):
        own = pair[p]
        for recv in crossed[p]:
            after = own = ordered(add_kernel, sketch16, [own, recv], after, "feat_add")
        owns.append(own)
        others.append(swap(own, "feat", nf, 1))
        if p > 0:
            after = leaf_step(after)
            after = hist_pass(codes, owns[p - 1], others[p - 1], per, n // 2, 0, f32, after)
            heres.append(after)
        after = hist_pass(codes, own, others[p], per, n // 2, 1, bf16, after)
        backs.append(swap(after, "rows", n, 1))
    after = hist_pass(codes, owns[-1], others[-1], per, n // 2, 0, f32, after)
    heres.append(after)

    levels = (n // 2).bit_length() - 1
    for slot in range(levels + parts - 1):
        for p in range(parts):
            level = slot - p
            if 0 <= level < levels:
                if p == parts - 1 and level == levels - 1:
                    while leaf_state[2] <= n:
                        after = leaf_step(after)
                    updated, leaf_values, after = update_pass(
                        pos, leaf, leaf_state[0], leaf_state[1], held, after)
                blocks = heres[p].shape[0] // 2
                shape = (blocks,) + heres[p].shape[1:]
                after, sent = ordered(
                    halving_kernel,
                    [jax.ShapeDtypeStruct(shape, f32), jax.ShapeDtypeStruct(shape, bf16)],
                    [heres[p], backs[p]], after, "hist_add")
                heres[p] = after
                backs[p] = swap(sent, "rows", n, 2 << level)
                if slot == 0:
                    after = leaf_step(after)
    histograms = ordered(
        last_kernel, jax.ShapeDtypeStruct((per * feats, width * parts), f32),
        [a for p in range(parts) for a in (heres[p], backs[p])], after, "last_add")
    return histograms.reshape(per, feats, -1), leaf_values, updated


def solution(mesh):
    n, nf = mesh.shape["rows"], mesh.shape["feat"]
    return jax.shard_map(
        functools.partial(local, n, nf),
        mesh=mesh,
        in_specs=(
            P("rows", "feat"),
            P("rows", "feat"),
            P("feat", "rows"),
            P("rows"),
            P("feat", None),
        ),
        out_specs=(P("rows", "feat", None), P(None, "feat"), P("rows", "feat")),
        check_vma=False,
    )
```

```python
import functools

import jax
import jax.numpy as jnp
from jax import lax
from jax.experimental import pallas as pl
from jax.experimental.pallas import tpu as pltpu
from jax.sharding import PartitionSpec as P

BINS = 256
LEAVES = 64


shrinkage = 0.5
ridge_term = 1.0

f32 = jnp.float32
bf16 = jnp.bfloat16
VMEM_LIMIT = 16 * 1024 * 1024


def block_rows(rows):
    for size in (256, 128, 64, 32, 16):
        if rows % size == 0:
            return size
    return rows


PARAMS = pltpu.CompilerParams(vmem_limit_bytes=VMEM_LIMIT)


def pin(x):
    return pltpu.with_memory_space_constraint(x, pltpu.VMEM)


def swap(x, axis, size, by):
    return lax.ppermute(x, axis, [(i, i ^ by) for i in range(size)])


def ordered(kernel, out_shape, args, after, name):
    def body(*refs):
        kernel(*refs[:len(args)], *refs[len(args) + 1:])

    many = isinstance(out_shape, (list, tuple))
    return pl.pallas_call(
        body,
        in_specs=[pl.BlockSpec(memory_space=pltpu.VMEM)] * len(args) + [pl.BlockSpec(memory_space=pl.ANY)],
        out_specs=[pl.BlockSpec(memory_space=pltpu.VMEM)] * len(out_shape)
        if many else pl.BlockSpec(memory_space=pltpu.VMEM),
        out_shape=out_shape,
        compiler_params=PARAMS,
        name=name,
    )(*[pin(a) for a in args], after)


def leaf_hot(leaf_ref, chunk, blk, flip, scale):
    lanes = leaf_ref.shape[1]
    lines = blk // lanes
    leaf = jnp.concatenate([leaf_ref[pl.ds(chunk * lines + j, 1)] for j in range(lines)], axis=1)
    hot = lax.broadcasted_iota(jnp.int32, (LEAVES, blk), 0) == (leaf ^ flip)
    return jnp.where(hot, f32(scale), f32(0)).astype(bf16)


def chunk_place(i, chunks, core):
    per_half = chunks // 2
    half = 1 - core if i < per_half else core
    return half * per_half + i % per_half


def rows_kernel(pos_ref, leaf_hbm, pred_hbm, lab_hbm, w_hbm, send_ref, keep_ref, g_ref, h_ref, pred_buf,
                leaf_buf, lab_buf, w_buf, pred_sem, lab_sem, w_sem, leaf_sem):
    core, side = pos_ref[0], pos_ref[1]
    chunks, blk, _ = pred_buf.shape
    per_half = chunks // 2

    def copies(i):
        at = pl.ds(pl.multiple_of(chunk_place(i, chunks, core) * blk, blk), blk)
        return (pltpu.make_async_copy(pred_hbm.at[at], pred_buf.at[i], pred_sem.at[i]),
                pltpu.make_async_copy(lab_hbm.at[at], lab_buf.at[i], lab_sem.at[i]))

    w_copy = pltpu.make_async_copy(w_hbm, w_buf, w_sem)
    leaf_copy = pltpu.make_async_copy(leaf_hbm, leaf_buf, leaf_sem)
    for i in range(chunks):
        for j, copy in enumerate(copies(i)):
            copy.start(priority=j)
        if i == 0:
            w_copy.start()
            leaf_copy.start(priority=1)
    for i in range(chunks):
        for copy in copies(i):
            copy.wait()
        if i == 0:
            w_copy.wait()
            leaf_copy.wait()
        p = 0.5 * jnp.tanh((pred_buf[i] * 0.5).astype(f32)) + 0.5
        grad = (lab_buf[i].astype(f32) - p).astype(bf16)
        hess = (p - p * p).astype(bf16)
        out = send_ref if i < per_half else keep_ref
        out[pl.ds(i % per_half * blk, blk)] = jnp.dot(grad, w_buf[...], preferred_element_type=f32).astype(bf16)
        hot = leaf_hot(leaf_buf, chunk_place(i, chunks, core), blk, side * (LEAVES // 2), 1.0)
        g = jnp.dot(hot, grad, preferred_element_type=f32)
        h = jnp.dot(hot, hess, preferred_element_type=f32)
        if i == 0:
            g_ref[...] = g
            h_ref[...] = h
        else:
            g_ref[...] += g
            h_ref[...] += h


def rows_pass(pos, leaf, pred, lab, w):
    rows, cols = pred.shape
    blk = block_rows(rows // 2)
    chunks = rows // blk
    vmem = pl.BlockSpec(memory_space=pltpu.VMEM)
    hbm = pl.BlockSpec(memory_space=pl.ANY)
    return pl.pallas_call(
        rows_kernel,
        in_specs=[pl.BlockSpec(memory_space=pltpu.SMEM), hbm, hbm, hbm, hbm],
        out_specs=[vmem] * 5,
        out_shape=[pltpu.VMEM((rows // 2, w.shape[1]), bf16)] * 2
        + [pltpu.VMEM((LEAVES, cols), f32)] * 2
        + [pltpu.VMEM((chunks, blk, cols), bf16)],
        scratch_shapes=[
            pltpu.VMEM(leaf.shape, jnp.int32),
            pltpu.VMEM((chunks, blk, cols), bf16),
            pltpu.VMEM(w.shape, bf16),
            pltpu.SemaphoreType.DMA((chunks,)),
            pltpu.SemaphoreType.DMA((chunks,)),
            pltpu.SemaphoreType.DMA,
            pltpu.SemaphoreType.DMA,
        ],
        compiler_params=PARAMS,
        name="rows",
    )(pos, leaf, pred, lab, w)


def part_add(part, parts):
    def kernel(a_ref, b_ref, out_ref):
        width = out_ref.shape[1]
        at = slice(part * width, (part + 1) * width)
        out_ref[...] = (a_ref[:, at].astype(f32) + b_ref[:, at].astype(f32)).astype(bf16)
    return kernel


def add_kernel(a_ref, b_ref, out_ref):
    out_ref[...] = (a_ref[...].astype(f32) + b_ref[...].astype(f32)).astype(out_ref.dtype)


def leaf_pack_kernel(g_ref, h_ref, keep_ref, send_ref):
    half = LEAVES // 2
    keep_ref[:half] = g_ref[:half]
    keep_ref[half:] = h_ref[:half]
    send_ref[:half] = g_ref[half:].astype(bf16)
    send_ref[half:] = h_ref[half:].astype(bf16)


def value_kernel(a_ref, b_ref, out_ref):
    half = LEAVES // 2
    total = a_ref[...].astype(f32) + b_ref[...].astype(f32)
    out_ref[...] = (total[:half] / (total[half:] + ridge_term)).astype(bf16)


def halving_kernel(here_ref, back_ref, keep_ref, send_ref):
    half = keep_ref.shape[0]
    keep_ref[...] = here_ref[:half] + back_ref[:half].astype(f32)
    send_ref[...] = (here_ref[half:] + back_ref[half:].astype(f32)).astype(bf16)


def last_kernel(*refs):
    out_ref = refs[-1]
    width = refs[0].shape[2]
    for p in range(len(refs) // 2):
        out_ref[:, p * width:(p + 1) * width] = refs[2 * p][0] + refs[2 * p + 1][0].astype(f32)


def hist_kernel(codes_ref, own_ref, other_ref, after_ref, out_ref, *, per, odd, bits):
    feats = codes_ref.shape[1]
    half = codes_ref.shape[2]
    codes = codes_ref[...].astype(f32).astype(bf16)
    step = pl.program_id(0)
    place = sum(((step >> b) & 1) << (bits - 1 - b) for b in range(bits))
    base = (2 * place + odd) * per
    levels = (lax.broadcasted_iota(jnp.int32, (per, 1, 1), 0) + base).astype(f32).astype(bf16)
    one = jnp.ones((), bf16)
    zero = jnp.zeros((), bf16)
    total = None
    for part, ref in ((0, own_ref), (1, other_ref)):
        hot = jnp.where(codes[part][None] == levels, one, zero).reshape(per * feats, half)
        term = jnp.dot(hot, ref[...], preferred_element_type=f32)
        total = term if total is None else total + term
    out_ref[0] = total.astype(out_ref.dtype)


def hist_pass(codes, own, other, per, blocks, odd, dtype, after):
    feats = codes.shape[1]
    width = own.shape[1]
    whole = lambda a: pl.BlockSpec(a.shape, lambda i: (0,) * a.ndim)
    return pl.pallas_call(
        functools.partial(hist_kernel, per=per, odd=odd, bits=blocks.bit_length() - 1),
        grid=(blocks,),
        in_specs=[whole(codes), whole(own), whole(other), pl.BlockSpec(memory_space=pl.ANY)],
        out_specs=pl.BlockSpec((1, per * feats, width), lambda i: (i, 0, 0)),
        out_shape=pltpu.VMEM((blocks, per * feats, width), dtype),
        compiler_params=PARAMS,
        name="hist_send" if odd else "hist_keep",
    )(pin(codes), pin(own), pin(other), after)


def update_kernel(pos_ref, leaf_ref, own_ref, other_ref, pred_ref, after_ref, new_hbm, values_hbm, done_ref,
                  new_buf, values_buf, new_sem, values_sem):
    core, side = pos_ref[0], pos_ref[1]
    chunks, blk, _ = pred_ref.shape
    half = LEAVES // 2

    def write(i):
        at = pl.ds(pl.multiple_of(chunk_place(i, chunks, core) * blk, blk), blk)
        return pltpu.make_async_copy(new_buf.at[i], new_hbm.at[at], new_sem.at[i])

    own, other = own_ref[...], other_ref[...]
    first = side == 0
    values_buf[:half] = jnp.where(first, own.astype(f32), other.astype(f32))
    values_buf[half:] = jnp.where(first, other.astype(f32), own.astype(f32))
    values_copy = pltpu.make_async_copy(values_buf, values_hbm, values_sem)
    values_copy.start(priority=1)
    table = jnp.concatenate([own, other], axis=0)
    for i in range(chunks):
        hot = leaf_hot(leaf_ref, chunk_place(i, chunks, core), blk, side * half, shrinkage)
        found = lax.dot_general(hot, table, (((0,), (0,)), ((), ())), preferred_element_type=f32)
        new_buf[i] = (pred_ref[i].astype(f32) + found).astype(bf16)
        write(i).start(priority=i % 2)
    done_ref[...] = jnp.zeros_like(done_ref)
    values_copy.wait()
    for i in range(chunks):
        write(i).wait()


def update_pass(pos, leaf, own, other, pred, after):
    chunks, blk, cols = pred.shape
    vmem = pl.BlockSpec(memory_space=pltpu.VMEM)
    hbm = pl.BlockSpec(memory_space=pl.ANY)
    return pl.pallas_call(
        update_kernel,
        in_specs=[pl.BlockSpec(memory_space=pltpu.SMEM), vmem, vmem, vmem, vmem, hbm],
        out_specs=[pl.BlockSpec(memory_space=pltpu.HBM)] * 2 + [vmem],
        out_shape=[
            pltpu.HBM((chunks * blk, cols), bf16),
            pltpu.HBM((LEAVES, cols), f32),
            pltpu.VMEM((8, 128), f32),
        ],
        scratch_shapes=[
            pltpu.VMEM((chunks, blk, cols), bf16),
            pltpu.VMEM((LEAVES, cols), f32),
            pltpu.SemaphoreType.DMA((chunks,)),
            pltpu.SemaphoreType.DMA,
        ],
        compiler_params=PARAMS,
        name="update",
    )(pos, leaf, pin(own), pin(other), pin(pred), after)


def local(n, nf, predictions, labels, feature_codes, leaf_index, sketch_weight):
    rows, cols = predictions.shape
    feats = feature_codes.shape[0]
    half = rows // 2
    parts = 2
    width = sketch_weight.shape[1] // parts
    me = lax.axis_index("rows")
    core = lax.axis_index("feat") & 1
    pos = jnp.stack([core, me & 1])
    per = BINS // n
    codes = (feature_codes ^ (me * per)).reshape(feats, 2, half)
    codes = jnp.where(core == 0, codes, codes[:, ::-1]).swapaxes(0, 1)
    lanes = min(128, block_rows(half))
    leaf = leaf_index.reshape(rows // lanes, lanes)

    pred = pltpu.with_memory_space_constraint(predictions, pltpu.HBM)
    lab = pltpu.with_memory_space_constraint(labels, pltpu.HBM)
    weight = pltpu.with_memory_space_constraint(sketch_weight, pltpu.HBM)
    sketch16 = pltpu.VMEM((half, width), bf16)
    sums16 = pltpu.VMEM((LEAVES, cols), bf16)
    sums32 = pltpu.VMEM((LEAVES, cols), f32)

    send, keep, grad, hess, held = rows_pass(pos, pltpu.with_memory_space_constraint(leaf, pltpu.HBM), pred, lab, weight)
    got = swap(send, "feat", nf, 1)
    pair, crossed, after = [], [], keep
    for p in range(parts):
        after = ordered(part_add(p, parts), sketch16, [keep, got], after, "core_add")
        pair.append(after)
        crossed.append([swap(after, "feat", nf, t) for t in range(2, nf, 2)])
        if p == 0:
            after, sent = ordered(leaf_pack_kernel, [sums32, sums16], [grad, hess], after, "leaf_pack")
            leaf_state = (after, swap(sent, "rows", n, 1), 2)

    def leaf_step(after):
        nonlocal leaf_state
        acc, got, by = leaf_state
        if by < n:
            acc = ordered(add_kernel, sums16, [acc, got], after, "leaf_add")
            leaf_state = (acc, swap(acc, "rows", n, by), 2 * by)
        elif by == n:
            values16 = pltpu.VMEM((LEAVES // 2, cols), bf16)
            acc = ordered(value_kernel, values16, [acc, got], after, "leaf_value")
            leaf_state = (acc, swap(acc, "rows", n, 1), 2 * by)
        else:
            return after
        return acc

    owns, others, backs, heres = [], [], [], []
    after = leaf_step(after)
    for p in range(parts):
        own = pair[p]
        for recv in crossed[p]:
            after = own = ordered(add_kernel, sketch16, [own, recv], after, "feat_add")
        owns.append(own)
        others.append(swap(own, "feat", nf, 1))
        if p > 0:
            after = leaf_step(after)
            after = hist_pass(codes, owns[p - 1], others[p - 1], per, n // 2, 0, f32, after)
            heres.append(after)
        after = hist_pass(codes, own, others[p], per, n // 2, 1, bf16, after)
        backs.append(swap(after, "rows", n, 1))
    after = hist_pass(codes, owns[-1], others[-1], per, n // 2, 0, f32, after)
    heres.append(after)

    levels = (n // 2).bit_length() - 1
    for slot in range(levels + parts - 1):
        for p in range(parts):
            level = slot - p
            if 0 <= level < levels:
                blocks = heres[p].shape[0] // 2
                shape = (blocks,) + heres[p].shape[1:]
                after, sent = ordered(
                    halving_kernel,
                    [pltpu.VMEM(shape, f32), pltpu.VMEM(shape, bf16)],
                    [heres[p], backs[p]], after, "hist_add")
                heres[p] = after
                backs[p] = swap(sent, "rows", n, 2 << level)
                if slot == 0:
                    after = leaf_step(after)
    while leaf_state[2] <= n:
        after = leaf_step(after)
    updated, leaf_values, after = update_pass(pos, leaf, leaf_state[0], leaf_state[1], held, after)
    histograms = ordered(
        last_kernel, jax.ShapeDtypeStruct((per * feats, width * parts), f32),
        [a for p in range(parts) for a in (heres[p], backs[p])], after, "last_add")
    return histograms.reshape(per, feats, -1), leaf_values, updated


def solution(mesh):
    n, nf = mesh.shape["rows"], mesh.shape["feat"]
    return jax.shard_map(
        functools.partial(local, n, nf),
        mesh=mesh,
        in_specs=(
            P("rows", "feat"),
            P("rows", "feat"),
            P("feat", "rows"),
            P("rows"),
            P("feat", None),
        ),
        out_specs=(P("rows", "feat", None), P(None, "feat"), P("rows", "feat")),
        check_vma=False,
    )
```

```python
import functools

import jax
import jax.numpy as jnp
from jax import lax
from jax.experimental import pallas as pl
from jax.experimental.pallas import tpu as pltpu
from jax.sharding import PartitionSpec as P

BINS = 256
LEAVES = 64


shrinkage = 0.5
ridge_term = 1.0

f32 = jnp.float32
bf16 = jnp.bfloat16
VMEM_LIMIT = 16 * 1024 * 1024


def block_rows(rows):
    for size in (256, 128, 64, 32, 16):
        if rows % size == 0:
            return size
    return rows


PARAMS = pltpu.CompilerParams(vmem_limit_bytes=VMEM_LIMIT)


def swap(x, axis, size, by):
    return lax.ppermute(x, axis, [(i, i ^ by) for i in range(size)])


def ordered(kernel, out_shape, args, after, name):
    def body(*refs):
        kernel(*refs[:len(args)], *refs[len(args) + 1:])

    many = isinstance(out_shape, (list, tuple))
    return pl.pallas_call(
        body,
        in_specs=[pl.BlockSpec(memory_space=pltpu.VMEM)] * len(args) + [pl.BlockSpec(memory_space=pl.ANY)],
        out_specs=[pl.BlockSpec(memory_space=pltpu.VMEM)] * len(out_shape)
        if many else pl.BlockSpec(memory_space=pltpu.VMEM),
        out_shape=out_shape,
        compiler_params=PARAMS,
        name=name,
    )(*args, after)


def leaf_hot(leaf_ref, chunk, blk, flip, scale):
    lanes = leaf_ref.shape[1]
    lines = blk // lanes
    leaf = jnp.concatenate([leaf_ref[pl.ds(chunk * lines + j, 1)] for j in range(lines)], axis=1)
    hot = lax.broadcasted_iota(jnp.int32, (LEAVES, blk), 0) == (leaf ^ flip)
    return jnp.where(hot, f32(scale), f32(0)).astype(bf16)


def chunk_place(i, chunks, core):
    per_half = chunks // 2
    half = 1 - core if i < per_half else core
    return half * per_half + i % per_half


def rows_kernel(pos_ref, leaf_hbm, pred_hbm, lab_hbm, w_hbm, send_ref, keep_ref, g_ref, h_ref,
                leaf_buf, pred_buf, lab_buf, w_buf, pred_sem, lab_sem, w_sem, leaf_sem):
    core, side = pos_ref[0], pos_ref[1]
    chunks, blk, _ = pred_buf.shape
    per_half = chunks // 2

    def copies(i):
        at = pl.ds(pl.multiple_of(chunk_place(i, chunks, core) * blk, blk), blk)
        return (pltpu.make_async_copy(pred_hbm.at[at], pred_buf.at[i], pred_sem.at[i]),
                pltpu.make_async_copy(lab_hbm.at[at], lab_buf.at[i], lab_sem.at[i]))

    w_copy = pltpu.make_async_copy(w_hbm, w_buf, w_sem)
    leaf_copy = pltpu.make_async_copy(leaf_hbm, leaf_buf, leaf_sem)
    for i in range(chunks):
        for copy in copies(i):
            copy.start()
        if i == 0:
            w_copy.start()
            leaf_copy.start()
    for i in range(chunks):
        for copy in copies(i):
            copy.wait()
        if i == 0:
            w_copy.wait()
            leaf_copy.wait()
        p = 0.5 * jnp.tanh((pred_buf[i] * 0.5).astype(f32)) + 0.5
        grad = (lab_buf[i].astype(f32) - p).astype(bf16)
        hess = (p - p * p).astype(bf16)
        out = send_ref if i < per_half else keep_ref
        out[pl.ds(i % per_half * blk, blk)] = jnp.dot(grad, w_buf[...], preferred_element_type=f32).astype(bf16)
        hot = leaf_hot(leaf_buf, chunk_place(i, chunks, core), blk, side * (LEAVES // 2), 1.0)
        g = jnp.dot(hot, grad, preferred_element_type=f32)
        h = jnp.dot(hot, hess, preferred_element_type=f32)
        if i == 0:
            g_ref[...] = g
            h_ref[...] = h
        else:
            g_ref[...] += g
            h_ref[...] += h


def rows_pass(pos, leaf, pred, lab, w):
    rows, cols = pred.shape
    blk = block_rows(rows // 2)
    chunks = rows // blk
    vmem = pl.BlockSpec(memory_space=pltpu.VMEM)
    hbm = pl.BlockSpec(memory_space=pl.ANY)
    return pl.pallas_call(
        rows_kernel,
        in_specs=[pl.BlockSpec(memory_space=pltpu.SMEM), hbm, hbm, hbm, hbm],
        out_specs=[vmem] * 4,
        out_shape=[jax.ShapeDtypeStruct((rows // 2, w.shape[1]), bf16)] * 2
        + [jax.ShapeDtypeStruct((LEAVES, cols), f32)] * 2,
        scratch_shapes=[
            pltpu.VMEM(leaf.shape, jnp.int32),
            pltpu.VMEM((chunks, blk, cols), bf16),
            pltpu.VMEM((chunks, blk, cols), bf16),
            pltpu.VMEM(w.shape, bf16),
            pltpu.SemaphoreType.DMA((chunks,)),
            pltpu.SemaphoreType.DMA((chunks,)),
            pltpu.SemaphoreType.DMA,
            pltpu.SemaphoreType.DMA,
        ],
        compiler_params=PARAMS,
        cost_estimate=pl.CostEstimate(flops=int(1.38e+10), transcendentals=0, bytes_accessed=0),
        name="rows",
    )(pos, leaf, pred, lab, w)


def part_add(part, parts):
    def kernel(a_ref, b_ref, out_ref):
        width = out_ref.shape[1]
        at = slice(part * width, (part + 1) * width)
        out_ref[...] = (a_ref[:, at].astype(f32) + b_ref[:, at].astype(f32)).astype(bf16)
    return kernel


def add_kernel(a_ref, b_ref, out_ref):
    out_ref[...] = (a_ref[...].astype(f32) + b_ref[...].astype(f32)).astype(out_ref.dtype)


def leaf_pack_kernel(g_ref, h_ref, keep_ref, send_ref):
    half = LEAVES // 2
    keep_ref[:half] = g_ref[:half]
    keep_ref[half:] = h_ref[:half]
    send_ref[:half] = g_ref[half:].astype(bf16)
    send_ref[half:] = h_ref[half:].astype(bf16)


def value_kernel(a_ref, b_ref, out_ref):
    half = LEAVES // 2
    total = a_ref[...].astype(f32) + b_ref[...].astype(f32)
    out_ref[...] = (total[:half] / (total[half:] + ridge_term)).astype(bf16)


def halving_kernel(here_ref, back_ref, keep_ref, send_ref):
    half = keep_ref.shape[0]
    keep_ref[...] = here_ref[:half] + back_ref[:half].astype(f32)
    send_ref[...] = (here_ref[half:] + back_ref[half:].astype(f32)).astype(bf16)


def last_kernel(*refs):
    out_ref = refs[-1]
    width = refs[0].shape[2]
    for p in range(len(refs) // 2):
        out_ref[:, p * width:(p + 1) * width] = refs[2 * p][0] + refs[2 * p + 1][0].astype(f32)


def hist_kernel(codes_ref, own_ref, other_ref, after_ref, out_ref, *, per, odd, bits):
    feats = codes_ref.shape[1]
    half = codes_ref.shape[2]
    codes = codes_ref[...].astype(f32).astype(bf16)
    step = pl.program_id(0)
    place = sum(((step >> b) & 1) << (bits - 1 - b) for b in range(bits))
    base = (2 * place + odd) * per
    levels = (lax.broadcasted_iota(jnp.int32, (per, 1, 1), 0) + base).astype(f32).astype(bf16)
    one = jnp.ones((), bf16)
    zero = jnp.zeros((), bf16)
    total = None
    for part, ref in ((0, own_ref), (1, other_ref)):
        hot = jnp.where(codes[part][None] == levels, one, zero).reshape(per * feats, half)
        term = jnp.dot(hot, ref[...], preferred_element_type=f32)
        total = term if total is None else total + term
    out_ref[0] = total.astype(out_ref.dtype)


def hist_pass(codes, own, other, per, blocks, odd, dtype, after):
    feats = codes.shape[1]
    width = own.shape[1]
    whole = lambda a: pl.BlockSpec(a.shape, lambda i: (0,) * a.ndim)
    return pl.pallas_call(
        functools.partial(hist_kernel, per=per, odd=odd, bits=blocks.bit_length() - 1),
        grid=(blocks,),
        in_specs=[whole(codes), whole(own), whole(other), pl.BlockSpec(memory_space=pl.ANY)],
        out_specs=pl.BlockSpec((1, per * feats, width), lambda i: (i, 0, 0)),
        out_shape=jax.ShapeDtypeStruct((blocks, per * feats, width), dtype),
        compiler_params=PARAMS,
        cost_estimate=pl.CostEstimate(flops=int(3.45e+09), transcendentals=0, bytes_accessed=0),
        name="hist_send" if odd else "hist_keep",
    )(codes, own, other, after)


def update_kernel(pos_ref, leaf_ref, own_ref, other_ref, pred_hbm, after_ref, *rest, first):
    if first:
        new_hbm, values_hbm, done_ref, pred_buf, new_buf, pred_sem, new_sem, values_buf, values_sem = rest
    else:
        _, new_hbm, done_ref, pred_buf, new_buf, pred_sem, new_sem = rest
    side = pos_ref[1]
    chunks, blk, _ = pred_buf.shape
    start = 0 if first else chunks
    half = LEAVES // 2

    def read(i):
        return pltpu.make_async_copy(pred_hbm.at[pl.ds((start + i) * blk, blk)], pred_buf.at[i], pred_sem.at[i])

    def write(i):
        return pltpu.make_async_copy(new_buf.at[i], new_hbm.at[pl.ds((start + i) * blk, blk)], new_sem.at[i])

    for i in range(chunks):
        read(i).start()
    own, other = own_ref[...], other_ref[...]
    if first:
        low = side == 0
        values_buf[:half] = jnp.where(low, own.astype(f32), other.astype(f32))
        values_buf[half:] = jnp.where(low, other.astype(f32), own.astype(f32))
        values_copy = pltpu.make_async_copy(values_buf, values_hbm, values_sem)
        values_copy.start()
    table = jnp.concatenate([own, other], axis=0)
    for i in range(chunks):
        hot = leaf_hot(leaf_ref, start + i, blk, side * half, shrinkage)
        found = lax.dot_general(hot, table, (((0,), (0,)), ((), ())), preferred_element_type=f32)
        read(i).wait()
        new_buf[i] = (pred_buf[i].astype(f32) + found).astype(bf16)
        write(i).start()
    done_ref[...] = jnp.zeros_like(done_ref)
    if first:
        values_copy.wait()
    for i in range(chunks):
        write(i).wait()


def update_pass(pos, leaf, own, other, pred, after, begun):
    rows, cols = pred.shape
    blk = block_rows(rows // 2)
    chunks = rows // blk // 2
    first = begun is None
    vmem = pl.BlockSpec(memory_space=pltpu.VMEM)
    hbm = pl.BlockSpec(memory_space=pl.ANY)
    new = jax.ShapeDtypeStruct((rows, cols), bf16)
    done = jax.ShapeDtypeStruct((8, 128), f32)
    return pl.pallas_call(
        functools.partial(update_kernel, first=first),
        in_specs=[pl.BlockSpec(memory_space=pltpu.SMEM), vmem, vmem, vmem, hbm, hbm] + [hbm] * (not first),
        out_specs=[hbm] * (1 + first) + [vmem],
        out_shape=[new, jax.ShapeDtypeStruct((LEAVES, cols), f32), done] if first else [new, done],
        scratch_shapes=[
            pltpu.VMEM((chunks, blk, cols), bf16),
            pltpu.VMEM((chunks, blk, cols), bf16),
            pltpu.SemaphoreType.DMA((chunks,)),
            pltpu.SemaphoreType.DMA((chunks,)),
        ] + ([pltpu.VMEM((LEAVES, cols), f32), pltpu.SemaphoreType.DMA] if first else []),
        input_output_aliases={} if first else {6: 0},
        compiler_params=PARAMS,
        cost_estimate=pl.CostEstimate(flops=int(6.44e+09), transcendentals=0, bytes_accessed=0),
        name="update_first" if first else "update_second",
    )(pos, leaf, own, other, pred, after, *([] if first else [begun]))


def local(n, nf, predictions, labels, feature_codes, leaf_index, sketch_weight):
    rows, cols = predictions.shape
    feats = feature_codes.shape[0]
    half = rows // 2
    parts = 2
    width = sketch_weight.shape[1] // parts
    me = lax.axis_index("rows")
    core = lax.axis_index("feat") & 1
    pos = jnp.stack([core, me & 1])
    per = BINS // n
    codes = (feature_codes ^ (me * per)).reshape(feats, 2, half)
    codes = jnp.where(core == 0, codes, codes[:, ::-1]).swapaxes(0, 1)
    lanes = min(128, block_rows(half))
    leaf = leaf_index.reshape(rows // lanes, lanes)

    pred = pltpu.with_memory_space_constraint(predictions, pltpu.HBM)
    lab = pltpu.with_memory_space_constraint(labels, pltpu.HBM)
    weight = pltpu.with_memory_space_constraint(sketch_weight, pltpu.HBM)
    sketch16 = jax.ShapeDtypeStruct((half, width), bf16)
    sums16 = jax.ShapeDtypeStruct((LEAVES, cols), bf16)
    sums32 = jax.ShapeDtypeStruct((LEAVES, cols), f32)

    send, keep, grad, hess = rows_pass(pos, pltpu.with_memory_space_constraint(leaf, pltpu.HBM), pred, lab, weight)
    got = swap(send, "feat", nf, 1)
    after = keep
    pair, crossed, owns, others, backs, heres = ([None] * parts for _ in range(6))
    leaf_state = None
    updated = leaf_values = None
    levels = (n // 2).bit_length() - 1

    def core_add(p):
        nonlocal after
        after = pair[p] = ordered(part_add(p, parts), sketch16, [keep, got], after, "core_add")
        crossed[p] = [swap(after, "feat", nf, t) for t in range(2, nf, 2)]

    def feat_add(p):
        nonlocal after
        own = pair[p]
        for recv in crossed[p]:
            after = own = ordered(add_kernel, sketch16, [own, recv], after, "feat_add")
        owns[p] = own
        others[p] = swap(own, "feat", nf, 1)

    def leaf_pack():
        nonlocal after, leaf_state
        after, sent = ordered(leaf_pack_kernel, [sums32, sums16], [grad, hess], after, "leaf_pack")
        leaf_state = (after, swap(sent, "rows", n, 1), 2)

    def leaf_step():
        nonlocal after, leaf_state
        acc, recv, by = leaf_state
        if by < n:
            after = ordered(add_kernel, sums16, [acc, recv], after, "leaf_add")
            leaf_state = (after, swap(after, "rows", n, by), 2 * by)
        elif by == n:
            values16 = jax.ShapeDtypeStruct((LEAVES // 2, cols), bf16)
            after = ordered(value_kernel, values16, [acc, recv], after, "leaf_value")
            leaf_state = (after, swap(after, "rows", n, 1), 2 * by)

    def update():
        nonlocal after, updated, leaf_values
        while leaf_state[2] <= n:
            leaf_step()
        if updated is None:
            updated, leaf_values, after = update_pass(pos, leaf, leaf_state[0], leaf_state[1], pred, after, None)
        else:
            updated, after = update_pass(pos, leaf, leaf_state[0], leaf_state[1], pred, after, updated)

    def hist_send(p):
        nonlocal after
        after = hist_pass(codes, owns[p], others[p], per, n // 2, 1, bf16, after)
        backs[p] = swap(after, "rows", n, 1)

    def hist_keep(p):
        nonlocal after
        after = heres[p] = hist_pass(codes, owns[p], others[p], per, n // 2, 0, f32, after)

    def hist_add(p, level):
        nonlocal after
        blocks = heres[p].shape[0] // 2
        shape = (blocks,) + heres[p].shape[1:]
        heres[p], sent = ordered(
            halving_kernel,
            [jax.ShapeDtypeStruct(shape, f32), jax.ShapeDtypeStruct(shape, bf16)],
            [heres[p], backs[p]], after, "hist_add")
        after = heres[p]
        backs[p] = swap(sent, "rows", n, 2 << level)

    core_add(0)
    leaf_pack()
    core_add(1)
    leaf_step()
    feat_add(0)
    hist_send(0)
    feat_add(1)
    hist_keep(0)
    leaf_step()
    hist_send(1)
    hist_keep(1)
    for level in range(levels):
        hist_add(0, level)
        if level == 0:
            leaf_step()
        if level > 0:
            hist_add(1, level - 1)
    update()
    hist_add(1, levels - 1)
    update()
    histograms = ordered(
        last_kernel, jax.ShapeDtypeStruct((per * feats, width * parts), f32),
        [a for p in range(parts) for a in (heres[p], backs[p])], after, "last_add")
    return histograms.reshape(per, feats, -1), leaf_values, updated


def solution(mesh):
    n, nf = mesh.shape["rows"], mesh.shape["feat"]
    return jax.shard_map(
        functools.partial(local, n, nf),
        mesh=mesh,
        in_specs=(
            P("rows", "feat"),
            P("rows", "feat"),
            P("feat", "rows"),
            P("rows"),
            P("feat", None),
        ),
        out_specs=(P("rows", "feat", None), P(None, "feat"), P("rows", "feat")),
        check_vma=False,
    )
```

```python
import functools

import jax
import jax.numpy as jnp
from jax import lax
from jax.experimental import pallas as pl
from jax.experimental.pallas import tpu as pltpu
from jax.sharding import PartitionSpec as P

BINS = 256
LEAVES = 64


shrinkage = 0.5
ridge_term = 1.0

f32 = jnp.float32
bf16 = jnp.bfloat16
VMEM_LIMIT = 16 * 1024 * 1024


def block_rows(rows):
    for size in (256, 128, 64, 32, 16):
        if rows % size == 0:
            return size
    return rows


PARAMS = pltpu.CompilerParams(vmem_limit_bytes=VMEM_LIMIT)


def swap(x, axis, size, by):
    return lax.ppermute(x, axis, [(i, i ^ by) for i in range(size)])


def ordered(kernel, out_shape, args, after, name):
    def body(*refs):
        kernel(*refs[:len(args)], *refs[len(args) + 1:])

    many = isinstance(out_shape, (list, tuple))
    return pl.pallas_call(
        body,
        in_specs=[pl.BlockSpec(memory_space=pltpu.VMEM)] * len(args) + [pl.BlockSpec(memory_space=pl.ANY)],
        out_specs=[pl.BlockSpec(memory_space=pltpu.VMEM)] * len(out_shape)
        if many else pl.BlockSpec(memory_space=pltpu.VMEM),
        out_shape=out_shape,
        compiler_params=PARAMS,
        name=name,
    )(*args, after)


def leaf_hot(leaf_ref, chunk, blk, flip, scale):
    lanes = leaf_ref.shape[1]
    lines = blk // lanes
    leaf = jnp.concatenate([leaf_ref[pl.ds(chunk * lines + j, 1)] for j in range(lines)], axis=1)
    hot = lax.broadcasted_iota(jnp.int32, (LEAVES, blk), 0) == (leaf ^ flip)
    return jnp.where(hot, f32(scale), f32(0)).astype(bf16)


def chunk_place(i, chunks, core):
    per_half = chunks // 2
    half = 1 - core if i < per_half else core
    return half * per_half + i % per_half


def rows_kernel(pos_ref, leaf_hbm, pred_hbm, lab_hbm, w_hbm, send_ref, keep_ref, g_ref, h_ref,
                leaf_buf, pred_buf, lab_buf, w_buf, pred_sem, lab_sem, w_sem, leaf_sem):
    core, side = pos_ref[0], pos_ref[1]
    chunks, blk, _ = pred_buf.shape
    per_half = chunks // 2

    def copies(i):
        at = pl.ds(pl.multiple_of(chunk_place(i, chunks, core) * blk, blk), blk)
        return (pltpu.make_async_copy(pred_hbm.at[at], pred_buf.at[i], pred_sem.at[i]),
                pltpu.make_async_copy(lab_hbm.at[at], lab_buf.at[i], lab_sem.at[i]))

    w_copy = pltpu.make_async_copy(w_hbm, w_buf, w_sem)
    leaf_copy = pltpu.make_async_copy(leaf_hbm, leaf_buf, leaf_sem)
    for i in range(chunks):
        for copy in copies(i):
            copy.start()
        if i == 0:
            w_copy.start()
            leaf_copy.start()
    for i in range(chunks):
        for copy in copies(i):
            copy.wait()
        if i == 0:
            w_copy.wait()
            leaf_copy.wait()
        p = 0.5 * jnp.tanh((pred_buf[i] * 0.5).astype(f32)) + 0.5
        grad = (lab_buf[i].astype(f32) - p).astype(bf16)
        hess = (p - p * p).astype(bf16)
        out = send_ref if i < per_half else keep_ref
        out[pl.ds(i % per_half * blk, blk)] = jnp.dot(grad, w_buf[...], preferred_element_type=f32).astype(bf16)
        hot = leaf_hot(leaf_buf, chunk_place(i, chunks, core), blk, side * (LEAVES // 2), 1.0)
        g = jnp.dot(hot, grad, preferred_element_type=f32)
        h = jnp.dot(hot, hess, preferred_element_type=f32)
        if i == 0:
            g_ref[...] = g
            h_ref[...] = h
        else:
            g_ref[...] += g
            h_ref[...] += h


def rows_pass(pos, leaf, pred, lab, w):
    rows, cols = pred.shape
    blk = block_rows(rows // 2)
    chunks = rows // blk
    vmem = pl.BlockSpec(memory_space=pltpu.VMEM)
    hbm = pl.BlockSpec(memory_space=pl.ANY)
    return pl.pallas_call(
        rows_kernel,
        in_specs=[pl.BlockSpec(memory_space=pltpu.SMEM), hbm, hbm, hbm, hbm],
        out_specs=[vmem] * 4,
        out_shape=[jax.ShapeDtypeStruct((rows // 2, w.shape[1]), bf16)] * 2
        + [jax.ShapeDtypeStruct((LEAVES, cols), f32)] * 2,
        scratch_shapes=[
            pltpu.VMEM(leaf.shape, jnp.int32),
            pltpu.VMEM((chunks, blk, cols), bf16),
            pltpu.VMEM((chunks, blk, cols), bf16),
            pltpu.VMEM(w.shape, bf16),
            pltpu.SemaphoreType.DMA((chunks,)),
            pltpu.SemaphoreType.DMA((chunks,)),
            pltpu.SemaphoreType.DMA,
            pltpu.SemaphoreType.DMA,
        ],
        compiler_params=PARAMS,
        name="rows",
    )(pos, leaf, pred, lab, w)


def part_add(part, parts):
    def kernel(a_ref, b_ref, out_ref):
        width = out_ref.shape[1]
        at = slice(part * width, (part + 1) * width)
        out_ref[...] = (a_ref[:, at].astype(f32) + b_ref[:, at].astype(f32)).astype(bf16)
    return kernel


def add_kernel(a_ref, b_ref, out_ref):
    out_ref[...] = (a_ref[...].astype(f32) + b_ref[...].astype(f32)).astype(out_ref.dtype)


def leaf_pack_kernel(g_ref, h_ref, keep_ref, send_ref):
    half = LEAVES // 2
    keep_ref[:half] = g_ref[:half]
    keep_ref[half:] = h_ref[:half]
    send_ref[:half] = g_ref[half:].astype(bf16)
    send_ref[half:] = h_ref[half:].astype(bf16)


def value_kernel(a_ref, b_ref, out_ref):
    half = LEAVES // 2
    total = a_ref[...].astype(f32) + b_ref[...].astype(f32)
    out_ref[...] = (total[:half] / (total[half:] + ridge_term)).astype(bf16)


def halving_kernel(here_ref, back_ref, keep_ref, send_ref):
    half = keep_ref.shape[0]
    keep_ref[...] = here_ref[:half] + back_ref[:half].astype(f32)
    send_ref[...] = (here_ref[half:] + back_ref[half:].astype(f32)).astype(bf16)


def last_kernel(*refs):
    out_ref = refs[-1]
    width = refs[0].shape[2]
    for p in range(len(refs) // 2):
        out_ref[:, p * width:(p + 1) * width] = refs[2 * p][0] + refs[2 * p + 1][0].astype(f32)


def hist_kernel(codes_ref, after_ref, *refs, per, odd, bits):
    parts = len(refs) // 3
    feats = codes_ref.shape[1]
    half = codes_ref.shape[2]
    codes = codes_ref[...].astype(f32).astype(bf16)
    step = pl.program_id(0)
    place = sum(((step >> b) & 1) << (bits - 1 - b) for b in range(bits))
    base = (2 * place + odd) * per
    levels = (lax.broadcasted_iota(jnp.int32, (per, 1, 1), 0) + base).astype(f32).astype(bf16)
    one = jnp.ones((), bf16)
    zero = jnp.zeros((), bf16)
    total = None
    for h in range(2):
        hot = jnp.where(codes[h][None] == levels, one, zero).reshape(per * feats, half)
        rows = refs[h * parts:(h + 1) * parts]
        sketch = jnp.concatenate([r[...] for r in rows], axis=1) if parts > 1 else rows[0][...]
        term = jnp.dot(hot, sketch, preferred_element_type=f32)
        total = term if total is None else total + term
    width = refs[-1].shape[2]
    for p in range(parts):
        out = refs[2 * parts + p]
        out[0] = total[:, p * width:(p + 1) * width].astype(out.dtype)


def hist_pass(codes, owns, others, per, blocks, odd, dtype, after):
    feats = codes.shape[1]
    width = owns[0].shape[1]
    parts = len(owns)
    whole = lambda a: pl.BlockSpec(a.shape, lambda i: (0,) * a.ndim)
    return pl.pallas_call(
        functools.partial(hist_kernel, per=per, odd=odd, bits=blocks.bit_length() - 1),
        grid=(blocks,),
        in_specs=[whole(codes), pl.BlockSpec(memory_space=pl.ANY)] + [whole(a) for a in owns + others],
        out_specs=[pl.BlockSpec((1, per * feats, width), lambda i: (i, 0, 0))] * parts,
        out_shape=[jax.ShapeDtypeStruct((blocks, per * feats, width), dtype)] * parts,
        compiler_params=PARAMS,
        name="hist_send" if odd else "hist_keep",
    )(codes, after, *owns, *others)


def update_kernel(pos_ref, leaf_ref, own_ref, other_ref, pred_ref, after_ref, *rest, first):
    if first:
        new_hbm, values_hbm, done_ref, new_buf, new_sem, values_buf, values_sem = rest
    else:
        _, new_hbm, done_ref, new_buf, new_sem = rest
    side = pos_ref[1]
    chunks, blk, _ = new_buf.shape
    start = 0 if first else chunks
    half = LEAVES // 2

    def write(i):
        return pltpu.make_async_copy(new_buf.at[i], new_hbm.at[pl.ds((start + i) * blk, blk)], new_sem.at[i])

    own, other = own_ref[...], other_ref[...]
    if first:
        low = side == 0
        values_buf[:half] = jnp.where(low, own.astype(f32), other.astype(f32))
        values_buf[half:] = jnp.where(low, other.astype(f32), own.astype(f32))
        values_copy = pltpu.make_async_copy(values_buf, values_hbm, values_sem)
        values_copy.start()
    table = jnp.concatenate([own, other], axis=0)
    for i in range(chunks):
        hot = leaf_hot(leaf_ref, start + i, blk, side * half, shrinkage)
        found = lax.dot_general(hot, table, (((0,), (0,)), ((), ())), preferred_element_type=f32)
        pred = pred_ref[pl.ds((start + i) * blk, blk)]
        new_buf[i] = (pred.astype(f32) + found).astype(bf16)
        write(i).start()
    done_ref[...] = jnp.zeros_like(done_ref)
    if first:
        values_copy.wait()
    for i in range(chunks):
        write(i).wait()


def update_pass(pos, leaf, own, other, pred, after, begun):
    rows, cols = pred.shape
    blk = block_rows(rows // 2)
    chunks = rows // blk // 2
    first = begun is None
    vmem = pl.BlockSpec(memory_space=pltpu.VMEM)
    hbm = pl.BlockSpec(memory_space=pl.ANY)
    new = jax.ShapeDtypeStruct((rows, cols), bf16)
    done = jax.ShapeDtypeStruct((8, 128), f32)
    return pl.pallas_call(
        functools.partial(update_kernel, first=first),
        in_specs=[pl.BlockSpec(memory_space=pltpu.SMEM), vmem, vmem, vmem, vmem, hbm] + [hbm] * (not first),
        out_specs=[hbm] * (1 + first) + [vmem],
        out_shape=[new, jax.ShapeDtypeStruct((LEAVES, cols), f32), done] if first else [new, done],
        scratch_shapes=[
            pltpu.VMEM((chunks, blk, cols), bf16),
            pltpu.SemaphoreType.DMA((chunks,)),
        ] + ([pltpu.VMEM((LEAVES, cols), f32), pltpu.SemaphoreType.DMA] if first else []),
        input_output_aliases={} if first else {6: 0},
        compiler_params=PARAMS,
        name="update_first" if first else "update_second",
    )(pos, leaf, own, other, pred, after, *([] if first else [begun]))


def local(n, nf, predictions, labels, feature_codes, leaf_index, sketch_weight):
    rows, cols = predictions.shape
    feats = feature_codes.shape[0]
    half = rows // 2
    parts = 2
    width = sketch_weight.shape[1] // parts
    me = lax.axis_index("rows")
    core = lax.axis_index("feat") & 1
    pos = jnp.stack([core, me & 1])
    per = BINS // n
    codes = (feature_codes ^ (me * per)).reshape(feats, 2, half)
    codes = jnp.where(core == 0, codes, codes[:, ::-1]).swapaxes(0, 1)
    lanes = min(128, block_rows(half))
    leaf = leaf_index.reshape(rows // lanes, lanes)

    pred = pltpu.with_memory_space_constraint(predictions, pltpu.HBM)
    lab = pltpu.with_memory_space_constraint(labels, pltpu.HBM)
    weight = pltpu.with_memory_space_constraint(sketch_weight, pltpu.HBM)
    sketch16 = jax.ShapeDtypeStruct((half, width), bf16)
    sums16 = jax.ShapeDtypeStruct((LEAVES, cols), bf16)
    sums32 = jax.ShapeDtypeStruct((LEAVES, cols), f32)

    send, keep, grad, hess = rows_pass(pos, pltpu.with_memory_space_constraint(leaf, pltpu.HBM), pred, lab, weight)
    got = swap(send, "feat", nf, 1)
    after = keep
    pair, crossed, owns, others, backs, heres = ([None] * parts for _ in range(6))
    leaf_state = None
    updated = leaf_values = None
    levels = (n // 2).bit_length() - 1

    def core_add(p):
        nonlocal after
        after = pair[p] = ordered(part_add(p, parts), sketch16, [keep, got], after, "core_add")
        crossed[p] = [swap(after, "feat", nf, t) for t in range(2, nf, 2)]

    def feat_add(p):
        nonlocal after
        own = pair[p]
        for recv in crossed[p]:
            after = own = ordered(add_kernel, sketch16, [own, recv], after, "feat_add")
        owns[p] = own
        others[p] = swap(own, "feat", nf, 1)

    def leaf_pack():
        nonlocal after, leaf_state
        after, sent = ordered(leaf_pack_kernel, [sums32, sums16], [grad, hess], after, "leaf_pack")
        leaf_state = (after, swap(sent, "rows", n, 1), 2)

    def leaf_step():
        nonlocal after, leaf_state
        acc, recv, by = leaf_state
        if by < n:
            after = ordered(add_kernel, sums16, [acc, recv], after, "leaf_add")
            leaf_state = (after, swap(after, "rows", n, by), 2 * by)
        elif by == n:
            values16 = jax.ShapeDtypeStruct((LEAVES // 2, cols), bf16)
            after = ordered(value_kernel, values16, [acc, recv], after, "leaf_value")
            leaf_state = (after, swap(after, "rows", n, 1), 2 * by)

    def update():
        nonlocal after, updated, leaf_values
        while leaf_state[2] <= n:
            leaf_step()
        if updated is None:
            updated, leaf_values, after = update_pass(pos, leaf, leaf_state[0], leaf_state[1], predictions, after, None)
        else:
            updated, after = update_pass(pos, leaf, leaf_state[0], leaf_state[1], predictions, after, updated)

    def hist_send(p):
        nonlocal after
        after, = hist_pass(codes, [owns[p]], [others[p]], per, n // 2, 1, bf16, after)
        backs[p] = swap(after, "rows", n, 1)

    def hist_keep():
        nonlocal after
        heres[:] = hist_pass(codes, owns, others, per, n // 2, 0, f32, after)
        after = heres[-1]

    def hist_add(p, level):
        nonlocal after
        blocks = heres[p].shape[0] // 2
        shape = (blocks,) + heres[p].shape[1:]
        heres[p], sent = ordered(
            halving_kernel,
            [jax.ShapeDtypeStruct(shape, f32), jax.ShapeDtypeStruct(shape, bf16)],
            [heres[p], backs[p]], after, "hist_add")
        after = heres[p]
        backs[p] = swap(sent, "rows", n, 2 << level)

    core_add(0)
    leaf_pack()
    core_add(1)
    leaf_step()
    feat_add(0)
    hist_send(0)
    feat_add(1)
    hist_send(1)
    hist_keep()
    leaf_step()
    for level in range(levels):
        hist_add(0, level)
        if level == levels - 1:
            update()
        hist_add(1, level)
        if level == 0:
            leaf_step()
    update()
    histograms = ordered(
        last_kernel, jax.ShapeDtypeStruct((per * feats, width * parts), f32),
        [a for p in range(parts) for a in (heres[p], backs[p])], after, "last_add")
    return histograms.reshape(per, feats, -1), leaf_values, updated


def solution(mesh):
    n, nf = mesh.shape["rows"], mesh.shape["feat"]
    return jax.shard_map(
        functools.partial(local, n, nf),
        mesh=mesh,
        in_specs=(
            P("rows", "feat"),
            P("rows", "feat"),
            P("feat", "rows"),
            P("rows"),
            P("feat", None),
        ),
        out_specs=(P("rows", "feat", None), P(None, "feat"), P("rows", "feat")),
        check_vma=False,
    )
```

```python
import functools

import jax
import jax.numpy as jnp
from jax import lax
from jax.experimental import pallas as pl
from jax.experimental.pallas import tpu as pltpu
from jax.sharding import PartitionSpec as P

BINS = 256
LEAVES = 64


shrinkage = 0.5
ridge_term = 1.0

f32 = jnp.float32
bf16 = jnp.bfloat16
VMEM_LIMIT = 16 * 1024 * 1024


def block_rows(rows):
    for size in (256, 128, 64, 32, 16):
        if rows % size == 0:
            return size
    return rows


def cost(gflop):
    return pl.CostEstimate(flops=int(gflop * 1e9), transcendentals=0, bytes_accessed=0)


PARAMS = pltpu.CompilerParams(vmem_limit_bytes=VMEM_LIMIT)


def swap(x, axis, size, by):
    return lax.ppermute(x, axis, [(i, i ^ by) for i in range(size)])


def ordered(kernel, out_shape, args, after, name, gflop=0):
    def body(*refs):
        kernel(*refs[:len(args)], *refs[len(args) + 1:])

    many = isinstance(out_shape, (list, tuple))
    return pl.pallas_call(
        body,
        in_specs=[pl.BlockSpec(memory_space=pltpu.VMEM)] * len(args) + [pl.BlockSpec(memory_space=pl.ANY)],
        out_specs=[pl.BlockSpec(memory_space=pltpu.VMEM)] * len(out_shape)
        if many else pl.BlockSpec(memory_space=pltpu.VMEM),
        out_shape=out_shape,
        cost_estimate=cost(gflop),
        compiler_params=PARAMS,
        name=name,
    )(*args, after)


def leaf_hot(leaf_ref, chunk, blk, flip, scale):
    lanes = leaf_ref.shape[1]
    lines = blk // lanes
    leaf = jnp.concatenate([leaf_ref[pl.ds(chunk * lines + j, 1)] for j in range(lines)], axis=1)
    hot = lax.broadcasted_iota(jnp.int32, (LEAVES, blk), 0) == (leaf ^ flip)
    return jnp.where(hot, f32(scale), f32(0)).astype(bf16)


def chunk_place(i, chunks, core):
    per_half = chunks // 2
    half = 1 - core if i < per_half else core
    return half * per_half + i % per_half


def rows_kernel(pos_ref, leaf_hbm, pred_hbm, lab_hbm, w_hbm, send_ref, keep_ref, g_ref, h_ref,
                leaf_buf, pred_buf, lab_buf, w_buf, pred_sem, lab_sem, w_sem, leaf_sem):
    core, side = pos_ref[0], pos_ref[1]
    chunks, blk, _ = pred_buf.shape
    per_half = chunks // 2

    def copies(i):
        at = pl.ds(pl.multiple_of(chunk_place(i, chunks, core) * blk, blk), blk)
        return (pltpu.make_async_copy(pred_hbm.at[at], pred_buf.at[i], pred_sem.at[i]),
                pltpu.make_async_copy(lab_hbm.at[at], lab_buf.at[i], lab_sem.at[i]))

    w_copy = pltpu.make_async_copy(w_hbm, w_buf, w_sem)
    leaf_copy = pltpu.make_async_copy(leaf_hbm, leaf_buf, leaf_sem)
    for i in range(chunks):
        for copy in copies(i):
            copy.start()
        if i == 0:
            w_copy.start()
            leaf_copy.start()
    for i in range(chunks):
        for copy in copies(i):
            copy.wait()
        if i == 0:
            w_copy.wait()
            leaf_copy.wait()
        p = 0.5 * jnp.tanh((pred_buf[i] * 0.5).astype(f32)) + 0.5
        grad = (lab_buf[i].astype(f32) - p).astype(bf16)
        hess = (p - p * p).astype(bf16)
        out = send_ref if i < per_half else keep_ref
        out[pl.ds(i % per_half * blk, blk)] = jnp.dot(grad, w_buf[...], preferred_element_type=f32).astype(bf16)
        hot = leaf_hot(leaf_buf, chunk_place(i, chunks, core), blk, side * (LEAVES // 2), 1.0)
        g = jnp.dot(hot, grad, preferred_element_type=f32)
        h = jnp.dot(hot, hess, preferred_element_type=f32)
        if i == 0:
            g_ref[...] = g
            h_ref[...] = h
        else:
            g_ref[...] += g
            h_ref[...] += h


def rows_pass(pos, leaf, pred, lab, w):
    rows, cols = pred.shape
    blk = block_rows(rows // 2)
    chunks = rows // blk
    vmem = pl.BlockSpec(memory_space=pltpu.VMEM)
    hbm = pl.BlockSpec(memory_space=pl.ANY)
    return pl.pallas_call(
        rows_kernel,
        in_specs=[pl.BlockSpec(memory_space=pltpu.SMEM), hbm, hbm, hbm, hbm],
        out_specs=[vmem] * 4,
        out_shape=[jax.ShapeDtypeStruct((rows // 2, w.shape[1]), bf16)] * 2
        + [jax.ShapeDtypeStruct((LEAVES, cols), f32)] * 2,
        scratch_shapes=[
            pltpu.VMEM(leaf.shape, jnp.int32),
            pltpu.VMEM((chunks, blk, cols), bf16),
            pltpu.VMEM((chunks, blk, cols), bf16),
            pltpu.VMEM(w.shape, bf16),
            pltpu.SemaphoreType.DMA((chunks,)),
            pltpu.SemaphoreType.DMA((chunks,)),
            pltpu.SemaphoreType.DMA,
            pltpu.SemaphoreType.DMA,
        ],
        compiler_params=PARAMS,
        name="rows",
    )(pos, leaf, pred, lab, w)


def part_add(part, parts):
    def kernel(a_ref, b_ref, out_ref):
        width = out_ref.shape[1]
        at = slice(part * width, (part + 1) * width)
        out_ref[...] = (a_ref[:, at].astype(f32) + b_ref[:, at].astype(f32)).astype(bf16)
    return kernel


def add_kernel(a_ref, b_ref, out_ref):
    out_ref[...] = (a_ref[...].astype(f32) + b_ref[...].astype(f32)).astype(out_ref.dtype)


def leaf_pack_kernel(g_ref, h_ref, keep_ref, send_ref):
    half = LEAVES // 2
    keep_ref[:half] = g_ref[:half]
    keep_ref[half:] = h_ref[:half]
    send_ref[:half] = g_ref[half:].astype(bf16)
    send_ref[half:] = h_ref[half:].astype(bf16)


def value_kernel(a_ref, b_ref, out_ref):
    half = LEAVES // 2
    total = a_ref[...].astype(f32) + b_ref[...].astype(f32)
    out_ref[...] = (total[:half] / (total[half:] + ridge_term)).astype(bf16)


def halving_kernel(here_ref, back_ref, keep_ref, send_ref):
    half = keep_ref.shape[0]
    keep_ref[...] = here_ref[:half] + back_ref[:half].astype(f32)
    send_ref[...] = (here_ref[half:] + back_ref[half:].astype(f32)).astype(bf16)


def last_kernel(*refs):
    out_ref = refs[-1]
    width = refs[0].shape[2]
    for p in range(len(refs) // 2):
        out_ref[:, p * width:(p + 1) * width] = refs[2 * p][0] + refs[2 * p + 1][0].astype(f32)


def hist_kernel(codes_ref, after_ref, *refs, per, odd, bits):
    parts = len(refs) // 3
    feats = codes_ref.shape[1]
    half = codes_ref.shape[2]
    codes = codes_ref[...].astype(f32).astype(bf16)
    step = pl.program_id(0)
    place = sum(((step >> b) & 1) << (bits - 1 - b) for b in range(bits))
    base = (2 * place + odd) * per
    levels = (lax.broadcasted_iota(jnp.int32, (per, 1, 1), 0) + base).astype(f32).astype(bf16)
    one = jnp.ones((), bf16)
    zero = jnp.zeros((), bf16)
    total = None
    for h in range(2):
        hot = jnp.where(codes[h][None] == levels, one, zero).reshape(per * feats, half)
        rows = refs[h * parts:(h + 1) * parts]
        sketch = jnp.concatenate([r[...] for r in rows], axis=1) if parts > 1 else rows[0][...]
        term = jnp.dot(hot, sketch, preferred_element_type=f32)
        total = term if total is None else total + term
    width = refs[-1].shape[2]
    for p in range(parts):
        out = refs[2 * parts + p]
        out[0] = total[:, p * width:(p + 1) * width].astype(out.dtype)


def hist_pass(codes, owns, others, per, blocks, odd, dtype, after, gflop):
    feats = codes.shape[1]
    width = owns[0].shape[1]
    parts = len(owns)
    whole = lambda a: pl.BlockSpec(a.shape, lambda i: (0,) * a.ndim)
    return pl.pallas_call(
        functools.partial(hist_kernel, per=per, odd=odd, bits=blocks.bit_length() - 1),
        grid=(blocks,),
        in_specs=[whole(codes), pl.BlockSpec(memory_space=pl.ANY)] + [whole(a) for a in owns + others],
        out_specs=[pl.BlockSpec((1, per * feats, width), lambda i: (i, 0, 0))] * parts,
        out_shape=[jax.ShapeDtypeStruct((blocks, per * feats, width), dtype)] * parts,
        cost_estimate=cost(gflop),
        compiler_params=PARAMS,
        name="hist_send" if odd else "hist_keep",
    )(codes, after, *owns, *others)


def update_kernel(pos_ref, leaf_ref, own_ref, other_ref, pred_ref, after_ref, *rest, first):
    if first:
        new_hbm, values_hbm, done_ref, new_buf, new_sem, values_buf, values_sem = rest
    else:
        _, new_hbm, done_ref, new_buf, new_sem = rest
    side = pos_ref[1]
    chunks, blk, _ = new_buf.shape
    start = 0 if first else chunks
    half = LEAVES // 2

    def write(i):
        return pltpu.make_async_copy(new_buf.at[i], new_hbm.at[pl.ds((start + i) * blk, blk)], new_sem.at[i])

    own, other = own_ref[...], other_ref[...]
    if first:
        low = side == 0
        values_buf[:half] = jnp.where(low, own.astype(f32), other.astype(f32))
        values_buf[half:] = jnp.where(low, other.astype(f32), own.astype(f32))
        values_copy = pltpu.make_async_copy(values_buf, values_hbm, values_sem)
        values_copy.start()
    table = jnp.concatenate([own, other], axis=0)
    for i in range(chunks):
        hot = leaf_hot(leaf_ref, start + i, blk, side * half, shrinkage)
        found = lax.dot_general(hot, table, (((0,), (0,)), ((), ())), preferred_element_type=f32)
        pred = pred_ref[pl.ds((start + i) * blk, blk)]
        new_buf[i] = (pred.astype(f32) + found).astype(bf16)
        write(i).start()
    done_ref[...] = jnp.zeros_like(done_ref)
    if first:
        values_copy.wait()
    for i in range(chunks):
        write(i).wait()


def update_pass(pos, leaf, own, other, pred, after, begun):
    rows, cols = pred.shape
    blk = block_rows(rows // 2)
    chunks = rows // blk // 2
    first = begun is None
    vmem = pl.BlockSpec(memory_space=pltpu.VMEM)
    hbm = pl.BlockSpec(memory_space=pl.ANY)
    new = jax.ShapeDtypeStruct((rows, cols), bf16)
    done = jax.ShapeDtypeStruct((8, 128), f32)
    return pl.pallas_call(
        functools.partial(update_kernel, first=first),
        in_specs=[pl.BlockSpec(memory_space=pltpu.SMEM), vmem, vmem, vmem, vmem, hbm] + [hbm] * (not first),
        out_specs=[hbm] * (1 + first) + [vmem],
        out_shape=[new, jax.ShapeDtypeStruct((LEAVES, cols), f32), done] if first else [new, done],
        scratch_shapes=[
            pltpu.VMEM((chunks, blk, cols), bf16),
            pltpu.SemaphoreType.DMA((chunks,)),
        ] + ([pltpu.VMEM((LEAVES, cols), f32), pltpu.SemaphoreType.DMA] if first else []),
        input_output_aliases={} if first else {6: 0},
        cost_estimate=cost(3.0),
        compiler_params=PARAMS,
        name="update_first" if first else "update_second",
    )(pos, leaf, own, other, pred, after, *([] if first else [begun]))


def local(n, nf, predictions, labels, feature_codes, leaf_index, sketch_weight):
    rows, cols = predictions.shape
    feats = feature_codes.shape[0]
    half = rows // 2
    parts = 2
    width = sketch_weight.shape[1] // parts
    me = lax.axis_index("rows")
    core = lax.axis_index("feat") & 1
    pos = jnp.stack([core, me & 1])
    per = BINS // n
    codes = (feature_codes ^ (me * per)).reshape(feats, 2, half)
    codes = jnp.where(core == 0, codes, codes[:, ::-1]).swapaxes(0, 1)
    lanes = min(128, block_rows(half))
    leaf = leaf_index.reshape(rows // lanes, lanes)

    pred = pltpu.with_memory_space_constraint(predictions, pltpu.HBM)
    lab = pltpu.with_memory_space_constraint(labels, pltpu.HBM)
    weight = pltpu.with_memory_space_constraint(sketch_weight, pltpu.HBM)
    sketch16 = jax.ShapeDtypeStruct((half, width), bf16)
    sums16 = jax.ShapeDtypeStruct((LEAVES, cols), bf16)
    sums32 = jax.ShapeDtypeStruct((LEAVES, cols), f32)

    send, keep, grad, hess = rows_pass(pos, pltpu.with_memory_space_constraint(leaf, pltpu.HBM), pred, lab, weight)
    got = swap(send, "feat", nf, 1)
    after = keep
    pair, crossed, owns, others, backs, heres = ([None] * parts for _ in range(6))
    leaf_state = None
    updated = leaf_values = None
    levels = (n // 2).bit_length() - 1

    def core_add(p):
        nonlocal after
        after = pair[p] = ordered(part_add(p, parts), sketch16, [keep, got], after, "core_add")
        crossed[p] = [swap(after, "feat", nf, t) for t in range(2, nf, 2)]

    def feat_add(p):
        nonlocal after
        own = pair[p]
        for recv in crossed[p]:
            after = own = ordered(add_kernel, sketch16, [own, recv], after, "feat_add", (0, 0.0)[p])
        owns[p] = own
        others[p] = swap(own, "feat", nf, 1)

    def leaf_pack():
        nonlocal after, leaf_state
        after, sent = ordered(leaf_pack_kernel, [sums32, sums16], [grad, hess], after, "leaf_pack")
        leaf_state = (after, swap(sent, "rows", n, 1), 2)

    def leaf_step():
        nonlocal after, leaf_state
        acc, recv, by = leaf_state
        if by < n:
            after = ordered(add_kernel, sums16, [acc, recv], after, "leaf_add")
            leaf_state = (after, swap(after, "rows", n, by), 2 * by)
        elif by == n:
            values16 = jax.ShapeDtypeStruct((LEAVES // 2, cols), bf16)
            after = ordered(value_kernel, values16, [acc, recv], after, "leaf_value")
            leaf_state = (after, swap(after, "rows", n, 1), 2 * by)

    def update():
        nonlocal after, updated, leaf_values
        while leaf_state[2] <= n:
            leaf_step()
        if updated is None:
            updated, leaf_values, after = update_pass(pos, leaf, leaf_state[0], leaf_state[1], predictions, after, None)
        else:
            updated, after = update_pass(pos, leaf, leaf_state[0], leaf_state[1], predictions, after, updated)

    def hist_send(p):
        nonlocal after
        after, = hist_pass(codes, [owns[p]], [others[p]], per, n // 2, 1, bf16, after, (2.0, 0.0)[p])
        backs[p] = swap(after, "rows", n, 1)

    def hist_keep():
        nonlocal after
        heres[:] = hist_pass(codes, owns, others, per, n // 2, 0, f32, after, 0.0)
        after = heres[-1]

    def hist_add(p, level):
        nonlocal after
        blocks = heres[p].shape[0] // 2
        shape = (blocks,) + heres[p].shape[1:]
        heres[p], sent = ordered(
            halving_kernel,
            [jax.ShapeDtypeStruct(shape, f32), jax.ShapeDtypeStruct(shape, bf16)],
            [heres[p], backs[p]], after, "hist_add")
        after = heres[p]
        backs[p] = swap(sent, "rows", n, 2 << level)

    core_add(0)
    leaf_pack()
    core_add(1)
    leaf_step()
    feat_add(0)
    hist_send(0)
    leaf_step()
    feat_add(1)
    hist_send(1)
    hist_keep()
    leaf_step()
    hist_add(0, 0)
    hist_add(1, 0)
    for level in range(1, levels):
        hist_add(0, level)
        if level == levels - 1:
            update()
        hist_add(1, level)
    update()
    histograms = ordered(
        last_kernel, jax.ShapeDtypeStruct((per * feats, width * parts), f32),
        [a for p in range(parts) for a in (heres[p], backs[p])], after, "last_add")
    return histograms.reshape(per, feats, -1), leaf_values, updated


def solution(mesh):
    n, nf = mesh.shape["rows"], mesh.shape["feat"]
    return jax.shard_map(
        functools.partial(local, n, nf),
        mesh=mesh,
        in_specs=(
            P("rows", "feat"),
            P("rows", "feat"),
            P("feat", "rows"),
            P("rows"),
            P("feat", None),
        ),
        out_specs=(P("rows", "feat", None), P(None, "feat"), P("rows", "feat")),
        check_vma=False,
    )
```

```python
import functools

import jax
import jax.numpy as jnp
from jax import lax
from jax.experimental import pallas as pl
from jax.experimental.pallas import tpu as pltpu
from jax.sharding import PartitionSpec as P

BINS = 256
LEAVES = 64


shrinkage = 0.5
ridge_term = 1.0

f32 = jnp.float32
bf16 = jnp.bfloat16
VMEM_LIMIT = 16 * 1024 * 1024


def block_rows(rows):
    for size in (256, 128, 64, 32, 16):
        if rows % size == 0:
            return size
    return rows


def cost(gflop):
    return pl.CostEstimate(flops=int(gflop * 1e9), transcendentals=0, bytes_accessed=0)


PARAMS = pltpu.CompilerParams(vmem_limit_bytes=VMEM_LIMIT)


def swap(x, axis, size, by):
    return lax.ppermute(x, axis, [(i, i ^ by) for i in range(size)])


def ordered(kernel, out_shape, args, after, name, gflop=0):
    def body(*refs):
        kernel(*refs[:len(args)], *refs[len(args) + 1:])

    many = isinstance(out_shape, (list, tuple))
    return pl.pallas_call(
        body,
        in_specs=[pl.BlockSpec(memory_space=pltpu.VMEM)] * len(args) + [pl.BlockSpec(memory_space=pl.ANY)],
        out_specs=[pl.BlockSpec(memory_space=pltpu.VMEM)] * len(out_shape)
        if many else pl.BlockSpec(memory_space=pltpu.VMEM),
        out_shape=out_shape,
        cost_estimate=cost(gflop),
        compiler_params=PARAMS,
        name=name,
    )(*args, after)


def leaf_hot(leaf_ref, chunk, blk, flip, scale):
    lanes = leaf_ref.shape[1]
    lines = blk // lanes
    leaf = jnp.concatenate([leaf_ref[pl.ds(chunk * lines + j, 1)] for j in range(lines)], axis=1)
    hot = lax.broadcasted_iota(jnp.int32, (LEAVES, blk), 0) == (leaf ^ flip)
    return jnp.where(hot, f32(scale), f32(0)).astype(bf16)


def chunk_place(i, chunks, core):
    per_half = chunks // 2
    half = 1 - core if i < per_half else core
    return half * per_half + i % per_half


def rows_kernel(pos_ref, leaf_hbm, pred_hbm, lab_hbm, w_hbm, send_ref, keep_ref, g_ref, h_ref,
                leaf_buf, pred_buf, lab_buf, w_buf, pred_sem, lab_sem, w_sem, leaf_sem):
    core, side = pos_ref[0], pos_ref[1]
    chunks, blk, _ = pred_buf.shape
    per_half = chunks // 2

    def copies(i):
        at = pl.ds(pl.multiple_of(chunk_place(i, chunks, core) * blk, blk), blk)
        return (pltpu.make_async_copy(pred_hbm.at[at], pred_buf.at[i], pred_sem.at[i]),
                pltpu.make_async_copy(lab_hbm.at[at], lab_buf.at[i], lab_sem.at[i]))

    w_copy = pltpu.make_async_copy(w_hbm, w_buf, w_sem)
    leaf_copy = pltpu.make_async_copy(leaf_hbm, leaf_buf, leaf_sem)
    for i in range(chunks):
        for copy in copies(i):
            copy.start()
        if i == 0:
            w_copy.start()
            leaf_copy.start()
    for i in range(chunks):
        for copy in copies(i):
            copy.wait()
        if i == 0:
            w_copy.wait()
            leaf_copy.wait()
        p = 0.5 * jnp.tanh((pred_buf[i] * 0.5).astype(f32)) + 0.5
        grad = (lab_buf[i].astype(f32) - p).astype(bf16)
        hess = (p - p * p).astype(bf16)
        out = send_ref if i < per_half else keep_ref
        out[pl.ds(i % per_half * blk, blk)] = jnp.dot(grad, w_buf[...], preferred_element_type=f32).astype(bf16)
        hot = leaf_hot(leaf_buf, chunk_place(i, chunks, core), blk, side * (LEAVES // 2), 1.0)
        g = jnp.dot(hot, grad, preferred_element_type=f32)
        h = jnp.dot(hot, hess, preferred_element_type=f32)
        if i == 0:
            g_ref[...] = g
            h_ref[...] = h
        else:
            g_ref[...] += g
            h_ref[...] += h


def rows_pass(pos, leaf, pred, lab, w):
    rows, cols = pred.shape
    blk = block_rows(rows // 2)
    chunks = rows // blk
    vmem = pl.BlockSpec(memory_space=pltpu.VMEM)
    hbm = pl.BlockSpec(memory_space=pl.ANY)
    return pl.pallas_call(
        rows_kernel,
        in_specs=[pl.BlockSpec(memory_space=pltpu.SMEM), hbm, hbm, hbm, hbm],
        out_specs=[vmem] * 4,
        out_shape=[jax.ShapeDtypeStruct((rows // 2, w.shape[1]), bf16)] * 2
        + [jax.ShapeDtypeStruct((LEAVES, cols), f32)] * 2,
        scratch_shapes=[
            pltpu.VMEM(leaf.shape, jnp.int32),
            pltpu.VMEM((chunks, blk, cols), bf16),
            pltpu.VMEM((chunks, blk, cols), bf16),
            pltpu.VMEM(w.shape, bf16),
            pltpu.SemaphoreType.DMA((chunks,)),
            pltpu.SemaphoreType.DMA((chunks,)),
            pltpu.SemaphoreType.DMA,
            pltpu.SemaphoreType.DMA,
        ],
        compiler_params=PARAMS,
        name="rows",
    )(pos, leaf, pred, lab, w)


def part_add(part, parts):
    def kernel(a_ref, b_ref, out_ref):
        width = out_ref.shape[1]
        at = slice(part * width, (part + 1) * width)
        out_ref[...] = (a_ref[:, at].astype(f32) + b_ref[:, at].astype(f32)).astype(bf16)
    return kernel


def add_kernel(a_ref, b_ref, out_ref):
    out_ref[...] = (a_ref[...].astype(f32) + b_ref[...].astype(f32)).astype(out_ref.dtype)


def leaf_pack_kernel(g_ref, h_ref, keep_ref, send_ref):
    half = LEAVES // 2
    keep_ref[:half] = g_ref[:half]
    keep_ref[half:] = h_ref[:half]
    send_ref[:half] = g_ref[half:].astype(bf16)
    send_ref[half:] = h_ref[half:].astype(bf16)


def value_kernel(a_ref, b_ref, out_ref):
    half = LEAVES // 2
    total = a_ref[...].astype(f32) + b_ref[...].astype(f32)
    out_ref[...] = (total[:half] / (total[half:] + ridge_term)).astype(bf16)


def halving_kernel(here_ref, back_ref, keep_ref, send_ref):
    half = keep_ref.shape[0]
    keep_ref[...] = here_ref[:half] + back_ref[:half].astype(f32)
    send_ref[...] = (here_ref[half:] + back_ref[half:].astype(f32)).astype(bf16)


def last_kernel(*refs):
    out_ref = refs[-1]
    width = refs[0].shape[2]
    for p in range(len(refs) // 2):
        out_ref[:, p * width:(p + 1) * width] = refs[2 * p][0] + refs[2 * p + 1][0].astype(f32)


def hist_kernel(codes_ref, after_ref, *refs, per, odd, bits):
    parts = len(refs) // 3
    feats = codes_ref.shape[1]
    half = codes_ref.shape[2]
    codes = codes_ref[...].astype(f32).astype(bf16)
    step = pl.program_id(0)
    place = sum(((step >> b) & 1) << (bits - 1 - b) for b in range(bits))
    base = (2 * place + odd) * per
    levels = (lax.broadcasted_iota(jnp.int32, (per, 1, 1), 0) + base).astype(f32).astype(bf16)
    one = jnp.ones((), bf16)
    zero = jnp.zeros((), bf16)
    total = None
    for h in range(2):
        hot = jnp.where(codes[h][None] == levels, one, zero).reshape(per * feats, half)
        rows = refs[h * parts:(h + 1) * parts]
        sketch = jnp.concatenate([r[...] for r in rows], axis=1) if parts > 1 else rows[0][...]
        term = jnp.dot(hot, sketch, preferred_element_type=f32)
        total = term if total is None else total + term
    width = refs[-1].shape[2]
    for p in range(parts):
        out = refs[2 * parts + p]
        out[0] = total[:, p * width:(p + 1) * width].astype(out.dtype)


def hist_pass(codes, owns, others, per, blocks, odd, dtype, after, gflop):
    feats = codes.shape[1]
    width = owns[0].shape[1]
    parts = len(owns)
    whole = lambda a: pl.BlockSpec(a.shape, lambda i: (0,) * a.ndim)
    return pl.pallas_call(
        functools.partial(hist_kernel, per=per, odd=odd, bits=blocks.bit_length() - 1),
        grid=(blocks,),
        in_specs=[whole(codes), pl.BlockSpec(memory_space=pl.ANY)] + [whole(a) for a in owns + others],
        out_specs=[pl.BlockSpec((1, per * feats, width), lambda i: (i, 0, 0))] * parts,
        out_shape=[jax.ShapeDtypeStruct((blocks, per * feats, width), dtype)] * parts,
        cost_estimate=cost(gflop),
        compiler_params=PARAMS,
        name="hist_send" if odd else "hist_keep",
    )(codes, after, *owns, *others)


def update_kernel(pos_ref, leaf_ref, own_ref, other_ref, pred_ref, after_ref, *rest, first):
    if first:
        new_hbm, values_hbm, done_ref, new_buf, new_sem, values_buf, values_sem = rest
    else:
        _, new_hbm, done_ref, new_buf, new_sem = rest
    side = pos_ref[1]
    chunks, blk, _ = new_buf.shape
    start = 0 if first else chunks
    half = LEAVES // 2

    def write(i):
        return pltpu.make_async_copy(new_buf.at[i], new_hbm.at[pl.ds((start + i) * blk, blk)], new_sem.at[i])

    own, other = own_ref[...], other_ref[...]
    if first:
        low = side == 0
        values_buf[:half] = jnp.where(low, own.astype(f32), other.astype(f32))
        values_buf[half:] = jnp.where(low, other.astype(f32), own.astype(f32))
        values_copy = pltpu.make_async_copy(values_buf, values_hbm, values_sem)
        values_copy.start()
    table = jnp.concatenate([own, other], axis=0)
    for i in range(chunks):
        hot = leaf_hot(leaf_ref, start + i, blk, side * half, shrinkage)
        found = lax.dot_general(hot, table, (((0,), (0,)), ((), ())), preferred_element_type=f32)
        pred = pred_ref[pl.ds((start + i) * blk, blk)]
        new_buf[i] = (pred.astype(f32) + found).astype(bf16)
        write(i).start()
    done_ref[...] = jnp.zeros_like(done_ref)
    if first:
        values_copy.wait()
    for i in range(chunks):
        write(i).wait()


def update_pass(pos, leaf, own, other, pred, after, begun):
    rows, cols = pred.shape
    blk = block_rows(rows // 2)
    chunks = rows // blk // 2
    first = begun is None
    vmem = pl.BlockSpec(memory_space=pltpu.VMEM)
    hbm = pl.BlockSpec(memory_space=pl.ANY)
    new = jax.ShapeDtypeStruct((rows, cols), bf16)
    done = jax.ShapeDtypeStruct((8, 128), f32)
    return pl.pallas_call(
        functools.partial(update_kernel, first=first),
        in_specs=[pl.BlockSpec(memory_space=pltpu.SMEM), vmem, vmem, vmem, vmem, hbm] + [hbm] * (not first),
        out_specs=[hbm] * (1 + first) + [vmem],
        out_shape=[new, jax.ShapeDtypeStruct((LEAVES, cols), f32), done] if first else [new, done],
        scratch_shapes=[
            pltpu.VMEM((chunks, blk, cols), bf16),
            pltpu.SemaphoreType.DMA((chunks,)),
        ] + ([pltpu.VMEM((LEAVES, cols), f32), pltpu.SemaphoreType.DMA] if first else []),
        input_output_aliases={} if first else {6: 0},
        cost_estimate=cost(3.0),
        compiler_params=PARAMS,
        name="update_first" if first else "update_second",
    )(pos, leaf, own, other, pred, after, *([] if first else [begun]))


def local(n, nf, predictions, labels, feature_codes, leaf_index, sketch_weight):
    rows, cols = predictions.shape
    feats = feature_codes.shape[0]
    half = rows // 2
    parts = 2
    width = sketch_weight.shape[1] // parts
    me = lax.axis_index("rows")
    core = lax.axis_index("feat") & 1
    pos = jnp.stack([core, me & 1])
    per = BINS // n
    codes = (feature_codes ^ (me * per)).reshape(feats, 2, half)
    codes = jnp.where(core == 0, codes, codes[:, ::-1]).swapaxes(0, 1)
    lanes = min(128, block_rows(half))
    leaf = leaf_index.reshape(rows // lanes, lanes)

    pred = pltpu.with_memory_space_constraint(predictions, pltpu.HBM)
    lab = pltpu.with_memory_space_constraint(labels, pltpu.HBM)
    weight = pltpu.with_memory_space_constraint(sketch_weight, pltpu.HBM)
    sketch16 = jax.ShapeDtypeStruct((half, width), bf16)
    sums16 = jax.ShapeDtypeStruct((LEAVES, cols), bf16)
    sums32 = jax.ShapeDtypeStruct((LEAVES, cols), f32)

    send, keep, grad, hess = rows_pass(pos, pltpu.with_memory_space_constraint(leaf, pltpu.HBM), pred, lab, weight)
    got = swap(send, "feat", nf, 1)
    after = keep
    pair, crossed, owns, others, backs, heres = ([None] * parts for _ in range(6))
    leaf_state = None
    updated = leaf_values = None
    levels = (n // 2).bit_length() - 1

    def core_add(p):
        nonlocal after
        after = pair[p] = ordered(part_add(p, parts), sketch16, [keep, got], after, "core_add")
        crossed[p] = [swap(after, "feat", nf, t) for t in range(2, nf, 2)]

    def feat_add(p):
        nonlocal after
        own = pair[p]
        for recv in crossed[p]:
            after = own = ordered(add_kernel, sketch16, [own, recv], after, "feat_add")
        owns[p] = own
        others[p] = swap(own, "feat", nf, 1)

    def leaf_pack():
        nonlocal after, leaf_state
        after, sent = ordered(leaf_pack_kernel, [sums32, sums16], [grad, hess], after, "leaf_pack")
        leaf_state = (after, swap(sent, "rows", n, 1), 2)

    def leaf_step():
        nonlocal after, leaf_state
        acc, recv, by = leaf_state
        if by < n:
            after = ordered(add_kernel, sums16, [acc, recv], after, "leaf_add", 0 if by == 2 else 3.0)
            leaf_state = (after, swap(after, "rows", n, by), 2 * by)
        elif by == n:
            values16 = jax.ShapeDtypeStruct((LEAVES // 2, cols), bf16)
            after = ordered(value_kernel, values16, [acc, recv], after, "leaf_value")
            leaf_state = (after, swap(after, "rows", n, 1), 2 * by)

    def update():
        nonlocal after, updated, leaf_values
        while leaf_state[2] <= n:
            leaf_step()
        if updated is None:
            updated, leaf_values, after = update_pass(pos, leaf, leaf_state[0], leaf_state[1], predictions, after, None)
        else:
            updated, after = update_pass(pos, leaf, leaf_state[0], leaf_state[1], predictions, after, updated)

    def hist_send(p):
        nonlocal after
        after, = hist_pass(codes, [owns[p]], [others[p]], per, n // 2, 1, bf16, after, (2.0, 3.0)[p])
        backs[p] = swap(after, "rows", n, 1)

    def hist_keep():
        nonlocal after
        heres[:] = hist_pass(codes, owns, others, per, n // 2, 0, f32, after, 3.0)
        after = heres[-1]

    def hist_add(p, level):
        nonlocal after
        blocks = heres[p].shape[0] // 2
        shape = (blocks,) + heres[p].shape[1:]
        heres[p], sent = ordered(
            halving_kernel,
            [jax.ShapeDtypeStruct(shape, f32), jax.ShapeDtypeStruct(shape, bf16)],
            [heres[p], backs[p]], after, "hist_add")
        after = heres[p]
        backs[p] = swap(sent, "rows", n, 2 << level)

    core_add(0)
    leaf_pack()
    core_add(1)
    leaf_step()
    feat_add(0)
    hist_send(0)
    feat_add(1)
    leaf_step()
    hist_send(1)
    hist_keep()
    hist_add(0, 0)
    leaf_step()
    hist_add(1, 0)
    for level in range(1, levels):
        hist_add(0, level)
        if level == levels - 1:
            update()
        hist_add(1, level)
    update()
    histograms = ordered(
        last_kernel, jax.ShapeDtypeStruct((per * feats, width * parts), f32),
        [a for p in range(parts) for a in (heres[p], backs[p])], after, "last_add")
    return histograms.reshape(per, feats, -1), leaf_values, updated


def solution(mesh):
    n, nf = mesh.shape["rows"], mesh.shape["feat"]
    return jax.shard_map(
        functools.partial(local, n, nf),
        mesh=mesh,
        in_specs=(
            P("rows", "feat"),
            P("rows", "feat"),
            P("feat", "rows"),
            P("rows"),
            P("feat", None),
        ),
        out_specs=(P("rows", "feat", None), P(None, "feat"), P("rows", "feat")),
        check_vma=False,
    )
```

```python
import functools

import jax
import jax.numpy as jnp
from jax import lax
from jax.experimental import pallas as pl
from jax.experimental.pallas import tpu as pltpu
from jax.sharding import PartitionSpec as P

BINS = 256
LEAVES = 64


shrinkage = 0.5
ridge_term = 1.0

f32 = jnp.float32
bf16 = jnp.bfloat16
VMEM_LIMIT = 16 * 1024 * 1024


def block_rows(rows):
    for size in (256, 128, 64, 32, 16):
        if rows % size == 0:
            return size
    return rows


def cost(gflop):
    return pl.CostEstimate(flops=int(gflop * 1e9), transcendentals=0, bytes_accessed=0)


PARAMS = pltpu.CompilerParams(vmem_limit_bytes=VMEM_LIMIT)


def swap(x, axis, size, by):
    return lax.ppermute(x, axis, [(i, i ^ by) for i in range(size)])


def ordered(kernel, out_shape, args, after, name, gflop=0):
    def body(*refs):
        kernel(*refs[:len(args)], *refs[len(args) + 1:])

    many = isinstance(out_shape, (list, tuple))
    return pl.pallas_call(
        body,
        in_specs=[pl.BlockSpec(memory_space=pltpu.VMEM)] * len(args) + [pl.BlockSpec(memory_space=pl.ANY)],
        out_specs=[pl.BlockSpec(memory_space=pltpu.VMEM)] * len(out_shape)
        if many else pl.BlockSpec(memory_space=pltpu.VMEM),
        out_shape=out_shape,
        cost_estimate=cost(gflop),
        compiler_params=PARAMS,
        name=name,
    )(*args, after)


def leaf_hot(leaf_ref, chunk, blk, flip, scale):
    lanes = leaf_ref.shape[1]
    lines = blk // lanes
    leaf = jnp.concatenate([leaf_ref[pl.ds(chunk * lines + j, 1)] for j in range(lines)], axis=1)
    hot = lax.broadcasted_iota(jnp.int32, (LEAVES, blk), 0) == (leaf ^ flip)
    return jnp.where(hot, f32(scale), f32(0)).astype(bf16)


def chunk_place(i, chunks, core):
    per_half = chunks // 2
    half = 1 - core if i < per_half else core
    return half * per_half + i % per_half


def rows_kernel(pos_ref, leaf_hbm, pred_hbm, lab_hbm, w_hbm, send_ref, keep_ref, g_ref, h_ref,
                leaf_buf, pred_buf, lab_buf, w_buf, pred_sem, lab_sem, w_sem, leaf_sem):
    core, side = pos_ref[0], pos_ref[1]
    chunks, blk, _ = pred_buf.shape
    per_half = chunks // 2

    def copies(i):
        at = pl.ds(pl.multiple_of(chunk_place(i, chunks, core) * blk, blk), blk)
        return (pltpu.make_async_copy(pred_hbm.at[at], pred_buf.at[i], pred_sem.at[i]),
                pltpu.make_async_copy(lab_hbm.at[at], lab_buf.at[i], lab_sem.at[i]))

    w_copy = pltpu.make_async_copy(w_hbm, w_buf, w_sem)
    leaf_copy = pltpu.make_async_copy(leaf_hbm, leaf_buf, leaf_sem)
    for i in range(chunks):
        for copy in copies(i):
            copy.start()
        if i == 0:
            w_copy.start()
            leaf_copy.start()
    for i in range(chunks):
        for copy in copies(i):
            copy.wait()
        if i == 0:
            w_copy.wait()
            leaf_copy.wait()
        p = 0.5 * jnp.tanh((pred_buf[i] * 0.5).astype(f32)) + 0.5
        grad = (lab_buf[i].astype(f32) - p).astype(bf16)
        hess = (p - p * p).astype(bf16)
        out = send_ref if i < per_half else keep_ref
        out[pl.ds(i % per_half * blk, blk)] = jnp.dot(grad, w_buf[...], preferred_element_type=f32).astype(bf16)
        hot = leaf_hot(leaf_buf, chunk_place(i, chunks, core), blk, side * (LEAVES // 2), 1.0)
        g = jnp.dot(hot, grad, preferred_element_type=f32)
        h = jnp.dot(hot, hess, preferred_element_type=f32)
        if i == 0:
            g_ref[...] = g
            h_ref[...] = h
        else:
            g_ref[...] += g
            h_ref[...] += h


def rows_pass(pos, leaf, pred, lab, w):
    rows, cols = pred.shape
    blk = block_rows(rows // 2)
    chunks = rows // blk
    vmem = pl.BlockSpec(memory_space=pltpu.VMEM)
    hbm = pl.BlockSpec(memory_space=pl.ANY)
    return pl.pallas_call(
        rows_kernel,
        in_specs=[pl.BlockSpec(memory_space=pltpu.SMEM), hbm, hbm, hbm, hbm],
        out_specs=[vmem] * 4,
        out_shape=[jax.ShapeDtypeStruct((rows // 2, w.shape[1]), bf16)] * 2
        + [jax.ShapeDtypeStruct((LEAVES, cols), f32)] * 2,
        scratch_shapes=[
            pltpu.VMEM(leaf.shape, jnp.int32),
            pltpu.VMEM((chunks, blk, cols), bf16),
            pltpu.VMEM((chunks, blk, cols), bf16),
            pltpu.VMEM(w.shape, bf16),
            pltpu.SemaphoreType.DMA((chunks,)),
            pltpu.SemaphoreType.DMA((chunks,)),
            pltpu.SemaphoreType.DMA,
            pltpu.SemaphoreType.DMA,
        ],
        compiler_params=PARAMS,
        name="rows",
    )(pos, leaf, pred, lab, w)


def part_add(part, parts):
    def kernel(a_ref, b_ref, out_ref):
        width = out_ref.shape[1]
        at = slice(part * width, (part + 1) * width)
        out_ref[...] = (a_ref[:, at].astype(f32) + b_ref[:, at].astype(f32)).astype(bf16)
    return kernel


def add_kernel(a_ref, b_ref, out_ref):
    out_ref[...] = (a_ref[...].astype(f32) + b_ref[...].astype(f32)).astype(out_ref.dtype)


def leaf_pack_kernel(g_ref, h_ref, keep_ref, send_ref):
    half = LEAVES // 2
    keep_ref[:half] = g_ref[:half]
    keep_ref[half:] = h_ref[:half]
    send_ref[:half] = g_ref[half:].astype(bf16)
    send_ref[half:] = h_ref[half:].astype(bf16)


def value_kernel(a_ref, b_ref, out_ref):
    half = LEAVES // 2
    total = a_ref[...].astype(f32) + b_ref[...].astype(f32)
    out_ref[...] = (total[:half] / (total[half:] + ridge_term)).astype(bf16)


def halving_kernel(here_ref, back_ref, keep_ref, send_ref):
    half = keep_ref.shape[0]
    keep_ref[...] = here_ref[:half] + back_ref[:half].astype(f32)
    send_ref[...] = (here_ref[half:] + back_ref[half:].astype(f32)).astype(bf16)


def last_kernel(*refs):
    out_ref = refs[-1]
    width = refs[0].shape[2]
    for p in range(len(refs) // 2):
        out_ref[:, p * width:(p + 1) * width] = refs[2 * p][0] + refs[2 * p + 1][0].astype(f32)


def hist_kernel(codes_ref, after_ref, *refs, per, odd, bits):
    parts = len(refs) // 3
    feats = codes_ref.shape[1]
    half = codes_ref.shape[2]
    codes = codes_ref[...].astype(f32).astype(bf16)
    step = pl.program_id(0)
    place = sum(((step >> b) & 1) << (bits - 1 - b) for b in range(bits))
    base = (2 * place + odd) * per
    levels = (lax.broadcasted_iota(jnp.int32, (per, 1, 1), 0) + base).astype(f32).astype(bf16)
    one = jnp.ones((), bf16)
    zero = jnp.zeros((), bf16)
    total = None
    for h in range(2):
        hot = jnp.where(codes[h][None] == levels, one, zero).reshape(per * feats, half)
        rows = refs[h * parts:(h + 1) * parts]
        sketch = jnp.concatenate([r[...] for r in rows], axis=1) if parts > 1 else rows[0][...]
        term = jnp.dot(hot, sketch, preferred_element_type=f32)
        total = term if total is None else total + term
    width = refs[-1].shape[2]
    for p in range(parts):
        out = refs[2 * parts + p]
        out[0] = total[:, p * width:(p + 1) * width].astype(out.dtype)


def hist_pass(codes, owns, others, per, blocks, odd, dtype, after, gflop):
    feats = codes.shape[1]
    width = owns[0].shape[1]
    parts = len(owns)
    whole = lambda a: pl.BlockSpec(a.shape, lambda i: (0,) * a.ndim)
    return pl.pallas_call(
        functools.partial(hist_kernel, per=per, odd=odd, bits=blocks.bit_length() - 1),
        grid=(blocks,),
        in_specs=[whole(codes), pl.BlockSpec(memory_space=pl.ANY)] + [whole(a) for a in owns + others],
        out_specs=[pl.BlockSpec((1, per * feats, width), lambda i: (i, 0, 0))] * parts,
        out_shape=[jax.ShapeDtypeStruct((blocks, per * feats, width), dtype)] * parts,
        cost_estimate=cost(gflop),
        compiler_params=PARAMS,
        name="hist_send" if odd else "hist_keep",
    )(codes, after, *owns, *others)


def update_kernel(pos_ref, leaf_ref, own_ref, other_ref, pred_ref, after_ref, *rest, first):
    if first:
        new_hbm, values_hbm, done_ref, new_buf, new_sem, values_buf, values_sem = rest
    else:
        _, new_hbm, done_ref, new_buf, new_sem = rest
    side = pos_ref[1]
    chunks, blk, _ = new_buf.shape
    start = 0 if first else chunks
    half = LEAVES // 2

    def write(i):
        return pltpu.make_async_copy(new_buf.at[i], new_hbm.at[pl.ds((start + i) * blk, blk)], new_sem.at[i])

    own, other = own_ref[...], other_ref[...]
    if first:
        low = side == 0
        values_buf[:half] = jnp.where(low, own.astype(f32), other.astype(f32))
        values_buf[half:] = jnp.where(low, other.astype(f32), own.astype(f32))
        values_copy = pltpu.make_async_copy(values_buf, values_hbm, values_sem)
        values_copy.start()
    table = jnp.concatenate([own, other], axis=0)
    for i in range(chunks):
        hot = leaf_hot(leaf_ref, start + i, blk, side * half, shrinkage)
        found = lax.dot_general(hot, table, (((0,), (0,)), ((), ())), preferred_element_type=f32)
        pred = pred_ref[pl.ds((start + i) * blk, blk)]
        new_buf[i] = (pred.astype(f32) + found).astype(bf16)
        write(i).start()
    done_ref[...] = jnp.zeros_like(done_ref)
    if first:
        values_copy.wait()
    for i in range(chunks):
        write(i).wait()


def update_pass(pos, leaf, own, other, pred, after, begun):
    rows, cols = pred.shape
    blk = block_rows(rows // 2)
    chunks = rows // blk // 2
    first = begun is None
    vmem = pl.BlockSpec(memory_space=pltpu.VMEM)
    hbm = pl.BlockSpec(memory_space=pl.ANY)
    new = jax.ShapeDtypeStruct((rows, cols), bf16)
    done = jax.ShapeDtypeStruct((8, 128), f32)
    return pl.pallas_call(
        functools.partial(update_kernel, first=first),
        in_specs=[pl.BlockSpec(memory_space=pltpu.SMEM), vmem, vmem, vmem, vmem, hbm] + [hbm] * (not first),
        out_specs=[hbm] * (1 + first) + [vmem],
        out_shape=[new, jax.ShapeDtypeStruct((LEAVES, cols), f32), done] if first else [new, done],
        scratch_shapes=[
            pltpu.VMEM((chunks, blk, cols), bf16),
            pltpu.SemaphoreType.DMA((chunks,)),
        ] + ([pltpu.VMEM((LEAVES, cols), f32), pltpu.SemaphoreType.DMA] if first else []),
        input_output_aliases={} if first else {6: 0},
        cost_estimate=cost(3.0),
        compiler_params=PARAMS,
        name="update_first" if first else "update_second",
    )(pos, leaf, own, other, pred, after, *([] if first else [begun]))


def local(n, nf, predictions, labels, feature_codes, leaf_index, sketch_weight):
    rows, cols = predictions.shape
    feats = feature_codes.shape[0]
    half = rows // 2
    parts = 2
    width = sketch_weight.shape[1] // parts
    me = lax.axis_index("rows")
    core = lax.axis_index("feat") & 1
    pos = jnp.stack([core, me & 1])
    per = BINS // n
    codes = (feature_codes ^ (me * per)).reshape(feats, 2, half)
    codes = jnp.where(core == 0, codes, codes[:, ::-1]).swapaxes(0, 1)
    lanes = min(128, block_rows(half))
    leaf = leaf_index.reshape(rows // lanes, lanes)

    pred = pltpu.with_memory_space_constraint(predictions, pltpu.HBM)
    lab = pltpu.with_memory_space_constraint(labels, pltpu.HBM)
    weight = pltpu.with_memory_space_constraint(sketch_weight, pltpu.HBM)
    sketch16 = jax.ShapeDtypeStruct((half, width), bf16)
    sums16 = jax.ShapeDtypeStruct((LEAVES, cols), bf16)
    sums32 = jax.ShapeDtypeStruct((LEAVES, cols), f32)

    send, keep, grad, hess = rows_pass(pos, pltpu.with_memory_space_constraint(leaf, pltpu.HBM), pred, lab, weight)
    got = swap(send, "feat", nf, 1)
    after = keep
    pair, crossed, owns, others, backs, heres = ([None] * parts for _ in range(6))
    leaf_state = None
    updated = leaf_values = None
    levels = (n // 2).bit_length() - 1

    def core_add(p):
        nonlocal after
        after = pair[p] = ordered(part_add(p, parts), sketch16, [keep, got], after, "core_add")
        crossed[p] = [swap(after, "feat", nf, t) for t in range(2, nf, 2)]

    def feat_add(p):
        nonlocal after
        own = pair[p]
        for recv in crossed[p]:
            after = own = ordered(add_kernel, sketch16, [own, recv], after, "feat_add")
        owns[p] = own
        others[p] = swap(own, "feat", nf, 1)

    def leaf_pack():
        nonlocal after, leaf_state
        after, sent = ordered(leaf_pack_kernel, [sums32, sums16], [grad, hess], after, "leaf_pack")
        leaf_state = (after, swap(sent, "rows", n, 1), 2)

    def leaf_step():
        nonlocal after, leaf_state
        acc, recv, by = leaf_state
        if by < n:
            after = ordered(add_kernel, sums16, [acc, recv], after, "leaf_add", 0 if by == 2 else 3.0)
            leaf_state = (after, swap(after, "rows", n, by), 2 * by)
        elif by == n:
            values16 = jax.ShapeDtypeStruct((LEAVES // 2, cols), bf16)
            after = ordered(value_kernel, values16, [acc, recv], after, "leaf_value")
            leaf_state = (after, swap(after, "rows", n, 1), 2 * by)

    def update():
        nonlocal after, updated, leaf_values
        while leaf_state[2] <= n:
            leaf_step()
        if updated is None:
            updated, leaf_values, after = update_pass(pos, leaf, leaf_state[0], leaf_state[1], predictions, after, None)
        else:
            updated, after = update_pass(pos, leaf, leaf_state[0], leaf_state[1], predictions, after, updated)

    def hist_send(p):
        nonlocal after
        after, = hist_pass(codes, [owns[p]], [others[p]], per, n // 2, 1, bf16, after, (2.0, 0.0)[p])
        backs[p] = swap(after, "rows", n, 1)

    def hist_keep():
        nonlocal after
        heres[:] = hist_pass(codes, owns, others, per, n // 2, 0, f32, after, 0.0)
        after = heres[-1]

    def hist_add(p, level):
        nonlocal after
        blocks = heres[p].shape[0] // 2
        shape = (blocks,) + heres[p].shape[1:]
        heres[p], sent = ordered(
            halving_kernel,
            [jax.ShapeDtypeStruct(shape, f32), jax.ShapeDtypeStruct(shape, bf16)],
            [heres[p], backs[p]], after, "hist_add")
        after = heres[p]
        backs[p] = swap(sent, "rows", n, 2 << level)

    core_add(0)
    leaf_pack()
    core_add(1)
    feat_add(0)
    leaf_step()
    hist_send(0)
    feat_add(1)
    leaf_step()
    hist_send(1)
    hist_keep()
    for level in range(levels):
        hist_add(0, level)
        hist_add(1, level)
        if level == 0:
            leaf_step()
    update()
    update()
    histograms = ordered(
        last_kernel, jax.ShapeDtypeStruct((per * feats, width * parts), f32),
        [a for p in range(parts) for a in (heres[p], backs[p])], after, "last_add")
    return histograms.reshape(per, feats, -1), leaf_values, updated


def solution(mesh):
    n, nf = mesh.shape["rows"], mesh.shape["feat"]
    return jax.shard_map(
        functools.partial(local, n, nf),
        mesh=mesh,
        in_specs=(
            P("rows", "feat"),
            P("rows", "feat"),
            P("feat", "rows"),
            P("rows"),
            P("feat", None),
        ),
        out_specs=(P("rows", "feat", None), P(None, "feat"), P("rows", "feat")),
        check_vma=False,
    )
```

```python
import functools

import jax
import jax.numpy as jnp
from jax import lax
from jax.experimental import pallas as pl
from jax.experimental.pallas import tpu as pltpu
from jax.sharding import PartitionSpec as P

BINS = 256
LEAVES = 64


shrinkage = 0.5
ridge_term = 1.0

f32 = jnp.float32
bf16 = jnp.bfloat16
VMEM_LIMIT = 16 * 1024 * 1024


def block_rows(rows):
    for size in (256, 128, 64, 32, 16):
        if rows % size == 0:
            return size
    return rows


def cost(gflop):
    return pl.CostEstimate(flops=int(gflop * 1e9), transcendentals=0, bytes_accessed=0)


PARAMS = pltpu.CompilerParams(vmem_limit_bytes=VMEM_LIMIT)


def swap(x, axis, size, by):
    return lax.ppermute(x, axis, [(i, i ^ by) for i in range(size)])


def ordered(kernel, out_shape, args, after, name, gflop=0):
    def body(*refs):
        kernel(*refs[:len(args)], *refs[len(args) + 1:])

    many = isinstance(out_shape, (list, tuple))
    return pl.pallas_call(
        body,
        in_specs=[pl.BlockSpec(memory_space=pltpu.VMEM)] * len(args) + [pl.BlockSpec(memory_space=pl.ANY)],
        out_specs=[pl.BlockSpec(memory_space=pltpu.VMEM)] * len(out_shape)
        if many else pl.BlockSpec(memory_space=pltpu.VMEM),
        out_shape=out_shape,
        cost_estimate=cost(gflop),
        compiler_params=PARAMS,
        name=name,
    )(*args, after)


def leaf_hot(leaf_ref, chunk, blk, flip, scale):
    lanes = leaf_ref.shape[1]
    lines = blk // lanes
    leaf = jnp.concatenate([leaf_ref[pl.ds(chunk * lines + j, 1)] for j in range(lines)], axis=1)
    hot = lax.broadcasted_iota(jnp.int32, (LEAVES, blk), 0) == (leaf ^ flip)
    return jnp.where(hot, f32(scale), f32(0)).astype(bf16)


def chunk_place(i, chunks, core):
    per_half = chunks // 2
    half = 1 - core if i < per_half else core
    return half * per_half + i % per_half


def rows_kernel(pos_ref, leaf_hbm, pred_hbm, lab_hbm, w_hbm, send_ref, keep_ref, g_ref, h_ref,
                leaf_buf, pred_buf, lab_buf, w_buf, pred_sem, lab_sem, w_sem, leaf_sem):
    core, side = pos_ref[0], pos_ref[1]
    chunks, blk, _ = pred_buf.shape
    per_half = chunks // 2

    def copies(i):
        at = pl.ds(pl.multiple_of(chunk_place(i, chunks, core) * blk, blk), blk)
        return (pltpu.make_async_copy(pred_hbm.at[at], pred_buf.at[i], pred_sem.at[i]),
                pltpu.make_async_copy(lab_hbm.at[at], lab_buf.at[i], lab_sem.at[i]))

    w_copy = pltpu.make_async_copy(w_hbm, w_buf, w_sem)
    leaf_copy = pltpu.make_async_copy(leaf_hbm, leaf_buf, leaf_sem)
    for i in range(chunks):
        for copy in copies(i):
            copy.start()
        if i == 0:
            w_copy.start()
            leaf_copy.start()
    for i in range(chunks):
        for copy in copies(i):
            copy.wait()
        if i == 0:
            w_copy.wait()
            leaf_copy.wait()
        p = 0.5 * jnp.tanh((pred_buf[i] * 0.5).astype(f32)) + 0.5
        grad = (lab_buf[i].astype(f32) - p).astype(bf16)
        hess = (p - p * p).astype(bf16)
        out = send_ref if i < per_half else keep_ref
        out[pl.ds(i % per_half * blk, blk)] = jnp.dot(grad, w_buf[...], preferred_element_type=f32).astype(bf16)
        hot = leaf_hot(leaf_buf, chunk_place(i, chunks, core), blk, side * (LEAVES // 2), 1.0)
        g = jnp.dot(hot, grad, preferred_element_type=f32)
        h = jnp.dot(hot, hess, preferred_element_type=f32)
        if i == 0:
            g_ref[...] = g
            h_ref[...] = h
        else:
            g_ref[...] += g
            h_ref[...] += h


def rows_pass(pos, leaf, pred, lab, w):
    rows, cols = pred.shape
    blk = block_rows(rows // 2)
    chunks = rows // blk
    vmem = pl.BlockSpec(memory_space=pltpu.VMEM)
    hbm = pl.BlockSpec(memory_space=pl.ANY)
    return pl.pallas_call(
        rows_kernel,
        in_specs=[pl.BlockSpec(memory_space=pltpu.SMEM), hbm, hbm, hbm, hbm],
        out_specs=[vmem] * 4,
        out_shape=[jax.ShapeDtypeStruct((rows // 2, w.shape[1]), bf16)] * 2
        + [jax.ShapeDtypeStruct((LEAVES, cols), f32)] * 2,
        scratch_shapes=[
            pltpu.VMEM(leaf.shape, jnp.int32),
            pltpu.VMEM((chunks, blk, cols), bf16),
            pltpu.VMEM((chunks, blk, cols), bf16),
            pltpu.VMEM(w.shape, bf16),
            pltpu.SemaphoreType.DMA((chunks,)),
            pltpu.SemaphoreType.DMA((chunks,)),
            pltpu.SemaphoreType.DMA,
            pltpu.SemaphoreType.DMA,
        ],
        compiler_params=PARAMS,
        name="rows",
    )(pos, leaf, pred, lab, w)


def part_add(part, parts):
    def kernel(a_ref, b_ref, out_ref):
        width = out_ref.shape[1]
        at = slice(part * width, (part + 1) * width)
        out_ref[...] = (a_ref[:, at].astype(f32) + b_ref[:, at].astype(f32)).astype(bf16)
    return kernel


def add_kernel(a_ref, b_ref, out_ref):
    out_ref[...] = (a_ref[...].astype(f32) + b_ref[...].astype(f32)).astype(out_ref.dtype)


def leaf_pack_kernel(g_ref, h_ref, keep_ref, send_ref):
    half = LEAVES // 2
    keep_ref[:half] = g_ref[:half]
    keep_ref[half:] = h_ref[:half]
    send_ref[:half] = g_ref[half:].astype(bf16)
    send_ref[half:] = h_ref[half:].astype(bf16)


def value_kernel(a_ref, b_ref, out_ref):
    half = LEAVES // 2
    total = a_ref[...].astype(f32) + b_ref[...].astype(f32)
    out_ref[...] = (total[:half] / (total[half:] + ridge_term)).astype(bf16)


def halving_kernel(here_ref, back_ref, keep_ref, send_ref):
    half = keep_ref.shape[0]
    keep_ref[...] = here_ref[:half] + back_ref[:half].astype(f32)
    send_ref[...] = (here_ref[half:] + back_ref[half:].astype(f32)).astype(bf16)


def last_kernel(*refs):
    out_ref = refs[-1]
    width = refs[0].shape[2]
    for p in range(len(refs) // 2):
        out_ref[:, p * width:(p + 1) * width] = refs[2 * p][0] + refs[2 * p + 1][0].astype(f32)


def hist_kernel(codes_ref, after_ref, *refs, per, odd, bits):
    parts = len(refs) // 3
    feats = codes_ref.shape[1]
    half = codes_ref.shape[2]
    codes = codes_ref[...].astype(f32).astype(bf16)
    step = pl.program_id(0)
    place = sum(((step >> b) & 1) << (bits - 1 - b) for b in range(bits))
    base = (2 * place + odd) * per
    levels = (lax.broadcasted_iota(jnp.int32, (per, 1, 1), 0) + base).astype(f32).astype(bf16)
    one = jnp.ones((), bf16)
    zero = jnp.zeros((), bf16)
    total = None
    for h in range(2):
        hot = jnp.where(codes[h][None] == levels, one, zero).reshape(per * feats, half)
        rows = refs[h * parts:(h + 1) * parts]
        sketch = jnp.concatenate([r[...] for r in rows], axis=1) if parts > 1 else rows[0][...]
        term = jnp.dot(hot, sketch, preferred_element_type=f32)
        total = term if total is None else total + term
    width = refs[-1].shape[2]
    for p in range(parts):
        out = refs[2 * parts + p]
        out[0] = total[:, p * width:(p + 1) * width].astype(out.dtype)


def hist_pass(codes, owns, others, per, blocks, odd, dtype, after, gflop):
    feats = codes.shape[1]
    width = owns[0].shape[1]
    parts = len(owns)
    whole = lambda a: pl.BlockSpec(a.shape, lambda i: (0,) * a.ndim)
    return pl.pallas_call(
        functools.partial(hist_kernel, per=per, odd=odd, bits=blocks.bit_length() - 1),
        grid=(blocks,),
        in_specs=[whole(codes), pl.BlockSpec(memory_space=pl.ANY)] + [whole(a) for a in owns + others],
        out_specs=[pl.BlockSpec((1, per * feats, width), lambda i: (i, 0, 0))] * parts,
        out_shape=[jax.ShapeDtypeStruct((blocks, per * feats, width), dtype)] * parts,
        cost_estimate=cost(gflop),
        compiler_params=PARAMS,
        name="hist_send" if odd else "hist_keep",
    )(codes, after, *owns, *others)


def update_kernel(pos_ref, leaf_ref, own_ref, other_ref, pred_ref, after_ref, *rest, first):
    if first:
        new_hbm, values_hbm, done_ref, new_buf, new_sem, values_buf, values_sem = rest
    else:
        _, new_hbm, done_ref, new_buf, new_sem = rest
    side = pos_ref[1]
    chunks, blk, _ = new_buf.shape
    start = 0 if first else chunks
    half = LEAVES // 2

    def write(i):
        return pltpu.make_async_copy(new_buf.at[i], new_hbm.at[pl.ds((start + i) * blk, blk)], new_sem.at[i])

    own, other = own_ref[...], other_ref[...]
    if first:
        low = side == 0
        values_buf[:half] = jnp.where(low, own.astype(f32), other.astype(f32))
        values_buf[half:] = jnp.where(low, other.astype(f32), own.astype(f32))
        values_copy = pltpu.make_async_copy(values_buf, values_hbm, values_sem)
        values_copy.start()
    table = jnp.concatenate([own, other], axis=0)
    for i in range(chunks):
        hot = leaf_hot(leaf_ref, start + i, blk, side * half, shrinkage)
        found = lax.dot_general(hot, table, (((0,), (0,)), ((), ())), preferred_element_type=f32)
        pred = pred_ref[pl.ds((start + i) * blk, blk)]
        new_buf[i] = (pred.astype(f32) + found).astype(bf16)
        write(i).start()
    done_ref[...] = jnp.zeros_like(done_ref)
    if first:
        values_copy.wait()
    for i in range(chunks):
        write(i).wait()


def update_pass(pos, leaf, own, other, pred, after, begun):
    rows, cols = pred.shape
    blk = block_rows(rows // 2)
    chunks = rows // blk // 2
    first = begun is None
    vmem = pl.BlockSpec(memory_space=pltpu.VMEM)
    hbm = pl.BlockSpec(memory_space=pl.ANY)
    new = jax.ShapeDtypeStruct((rows, cols), bf16)
    done = jax.ShapeDtypeStruct((8, 128), f32)
    return pl.pallas_call(
        functools.partial(update_kernel, first=first),
        in_specs=[pl.BlockSpec(memory_space=pltpu.SMEM), vmem, vmem, vmem, vmem, hbm] + [hbm] * (not first),
        out_specs=[hbm] * (1 + first) + [vmem],
        out_shape=[new, jax.ShapeDtypeStruct((LEAVES, cols), f32), done] if first else [new, done],
        scratch_shapes=[
            pltpu.VMEM((chunks, blk, cols), bf16),
            pltpu.SemaphoreType.DMA((chunks,)),
        ] + ([pltpu.VMEM((LEAVES, cols), f32), pltpu.SemaphoreType.DMA] if first else []),
        input_output_aliases={} if first else {6: 0},
        cost_estimate=cost(3.0),
        compiler_params=PARAMS,
        name="update_first" if first else "update_second",
    )(pos, leaf, own, other, pred, after, *([] if first else [begun]))


def local(n, nf, predictions, labels, feature_codes, leaf_index, sketch_weight):
    rows, cols = predictions.shape
    feats = feature_codes.shape[0]
    half = rows // 2
    parts = 2
    width = sketch_weight.shape[1] // parts
    me = lax.axis_index("rows")
    core = lax.axis_index("feat") & 1
    pos = jnp.stack([core, me & 1])
    per = BINS // n
    codes = (feature_codes ^ (me * per)).reshape(feats, 2, half)
    codes = jnp.where(core == 0, codes, codes[:, ::-1]).swapaxes(0, 1)
    lanes = min(128, block_rows(half))
    leaf = leaf_index.reshape(rows // lanes, lanes)

    pred = pltpu.with_memory_space_constraint(predictions, pltpu.HBM)
    lab = pltpu.with_memory_space_constraint(labels, pltpu.HBM)
    weight = pltpu.with_memory_space_constraint(sketch_weight, pltpu.HBM)
    sketch16 = jax.ShapeDtypeStruct((half, width), bf16)
    sums16 = jax.ShapeDtypeStruct((LEAVES, cols), bf16)
    sums32 = jax.ShapeDtypeStruct((LEAVES, cols), f32)

    send, keep, grad, hess = rows_pass(pos, pltpu.with_memory_space_constraint(leaf, pltpu.HBM), pred, lab, weight)
    got = swap(send, "feat", nf, 1)
    after = keep
    pair, crossed, owns, others, backs, heres = ([None] * parts for _ in range(6))
    leaf_state = None
    updated = leaf_values = None
    levels = (n // 2).bit_length() - 1

    def core_add(p):
        nonlocal after
        after = pair[p] = ordered(part_add(p, parts), sketch16, [keep, got], after, "core_add", 1.0)
        crossed[p] = [swap(after, "feat", nf, t) for t in range(2, nf, 2)]

    def feat_add(p):
        nonlocal after
        own = pair[p]
        for recv in crossed[p]:
            after = own = ordered(add_kernel, sketch16, [own, recv], after, "feat_add")
        owns[p] = own
        others[p] = swap(own, "feat", nf, 1)

    def leaf_pack():
        nonlocal after, leaf_state
        after, sent = ordered(leaf_pack_kernel, [sums32, sums16], [grad, hess], after, "leaf_pack")
        leaf_state = (after, swap(sent, "rows", n, 1), 2)

    def leaf_step():
        nonlocal after, leaf_state
        acc, recv, by = leaf_state
        if by < n:
            after = ordered(add_kernel, sums16, [acc, recv], after, "leaf_add", 1.0 if by == 2 else 3.0)
            leaf_state = (after, swap(after, "rows", n, by), 2 * by)
        elif by == n:
            values16 = jax.ShapeDtypeStruct((LEAVES // 2, cols), bf16)
            after = ordered(value_kernel, values16, [acc, recv], after, "leaf_value")
            leaf_state = (after, swap(after, "rows", n, 1), 2 * by)

    def update():
        nonlocal after, updated, leaf_values
        while leaf_state[2] <= n:
            leaf_step()
        if updated is None:
            updated, leaf_values, after = update_pass(pos, leaf, leaf_state[0], leaf_state[1], predictions, after, None)
        else:
            updated, after = update_pass(pos, leaf, leaf_state[0], leaf_state[1], predictions, after, updated)

    def hist_send(p):
        nonlocal after
        after, = hist_pass(codes, [owns[p]], [others[p]], per, n // 2, 1, bf16, after, (1.0, 3.0)[p])
        backs[p] = swap(after, "rows", n, 1)

    def hist_keep():
        nonlocal after
        heres[:] = hist_pass(codes, owns, others, per, n // 2, 0, f32, after, 3.0)
        after = heres[-1]

    def hist_add(p, level):
        nonlocal after
        blocks = heres[p].shape[0] // 2
        shape = (blocks,) + heres[p].shape[1:]
        heres[p], sent = ordered(
            halving_kernel,
            [jax.ShapeDtypeStruct(shape, f32), jax.ShapeDtypeStruct(shape, bf16)],
            [heres[p], backs[p]], after, "hist_add")
        after = heres[p]
        backs[p] = swap(sent, "rows", n, 2 << level)

    leaf_pack()
    core_add(0)
    core_add(1)
    leaf_step()
    feat_add(0)
    hist_send(0)
    feat_add(1)
    leaf_step()
    hist_send(1)
    hist_keep()
    hist_add(0, 0)
    leaf_step()
    hist_add(1, 0)
    for level in range(1, levels):
        hist_add(0, level)
        if level == levels - 1:
            update()
        hist_add(1, level)
    update()
    histograms = ordered(
        last_kernel, jax.ShapeDtypeStruct((per * feats, width * parts), f32),
        [a for p in range(parts) for a in (heres[p], backs[p])], after, "last_add")
    return histograms.reshape(per, feats, -1), leaf_values, updated


def solution(mesh):
    n, nf = mesh.shape["rows"], mesh.shape["feat"]
    return jax.shard_map(
        functools.partial(local, n, nf),
        mesh=mesh,
        in_specs=(
            P("rows", "feat"),
            P("rows", "feat"),
            P("feat", "rows"),
            P("rows"),
            P("feat", None),
        ),
        out_specs=(P("rows", "feat", None), P(None, "feat"), P("rows", "feat")),
        check_vma=False,
    )
```

```python
import functools

import jax
import jax.numpy as jnp
from jax import lax
from jax.experimental import pallas as pl
from jax.experimental.pallas import tpu as pltpu
from jax.sharding import PartitionSpec as P

BINS = 256
LEAVES = 64


shrinkage = 0.5
ridge_term = 1.0

f32 = jnp.float32
bf16 = jnp.bfloat16
VMEM_LIMIT = 16 * 1024 * 1024


def block_rows(rows):
    for size in (256, 128, 64, 32, 16):
        if rows % size == 0:
            return size
    return rows


def cost(gflop):
    return pl.CostEstimate(flops=int(gflop * 1e9), transcendentals=0, bytes_accessed=0)


PARAMS = pltpu.CompilerParams(vmem_limit_bytes=VMEM_LIMIT)


def swap(x, axis, size, by):
    return lax.ppermute(x, axis, [(i, i ^ by) for i in range(size)])


def ordered(kernel, out_shape, args, after, name, gflop=0):
    def body(*refs):
        kernel(*refs[:len(args)], *refs[len(args) + 1:])

    many = isinstance(out_shape, (list, tuple))
    return pl.pallas_call(
        body,
        in_specs=[pl.BlockSpec(memory_space=pltpu.VMEM)] * len(args) + [pl.BlockSpec(memory_space=pl.ANY)],
        out_specs=[pl.BlockSpec(memory_space=pltpu.VMEM)] * len(out_shape)
        if many else pl.BlockSpec(memory_space=pltpu.VMEM),
        out_shape=out_shape,
        cost_estimate=cost(gflop),
        compiler_params=PARAMS,
        name=name,
    )(*args, after)


def leaf_hot(leaf_ref, chunk, blk, flip, scale):
    lanes = leaf_ref.shape[1]
    lines = blk // lanes
    leaf = jnp.concatenate([leaf_ref[pl.ds(chunk * lines + j, 1)] for j in range(lines)], axis=1)
    hot = lax.broadcasted_iota(jnp.int32, (LEAVES, blk), 0) == (leaf ^ flip)
    return jnp.where(hot, f32(scale), f32(0)).astype(bf16)


def chunk_place(i, chunks, core):
    per_half = chunks // 2
    half = 1 - core if i < per_half else core
    return half * per_half + i % per_half


def rows_kernel(pos_ref, leaf_hbm, pred_hbm, lab_hbm, w_hbm, send_ref, keep_ref, g_ref, h_ref,
                leaf_buf, pred_buf, lab_buf, w_buf, pred_sem, lab_sem, w_sem, leaf_sem):
    core, side = pos_ref[0], pos_ref[1]
    chunks, blk, _ = pred_buf.shape
    per_half = chunks // 2

    def copies(i):
        at = pl.ds(pl.multiple_of(chunk_place(i, chunks, core) * blk, blk), blk)
        return (pltpu.make_async_copy(pred_hbm.at[at], pred_buf.at[i], pred_sem.at[i]),
                pltpu.make_async_copy(lab_hbm.at[at], lab_buf.at[i], lab_sem.at[i]))

    w_copy = pltpu.make_async_copy(w_hbm, w_buf, w_sem)
    leaf_copy = pltpu.make_async_copy(leaf_hbm, leaf_buf, leaf_sem)
    for i in range(chunks):
        for copy in copies(i):
            copy.start()
        if i == 0:
            w_copy.start()
            leaf_copy.start()
    for i in range(chunks):
        for copy in copies(i):
            copy.wait()
        if i == 0:
            w_copy.wait()
            leaf_copy.wait()
        p = 0.5 * jnp.tanh((pred_buf[i] * 0.5).astype(f32)) + 0.5
        grad = (lab_buf[i].astype(f32) - p).astype(bf16)
        hess = (p - p * p).astype(bf16)
        out = send_ref if i < per_half else keep_ref
        out[pl.ds(i % per_half * blk, blk)] = jnp.dot(grad, w_buf[...], preferred_element_type=f32).astype(bf16)
        hot = leaf_hot(leaf_buf, chunk_place(i, chunks, core), blk, side * (LEAVES // 2), 1.0)
        g = jnp.dot(hot, grad, preferred_element_type=f32)
        h = jnp.dot(hot, hess, preferred_element_type=f32)
        if i == 0:
            g_ref[...] = g
            h_ref[...] = h
        else:
            g_ref[...] += g
            h_ref[...] += h


def rows_pass(pos, leaf, pred, lab, w):
    rows, cols = pred.shape
    blk = block_rows(rows // 2)
    chunks = rows // blk
    vmem = pl.BlockSpec(memory_space=pltpu.VMEM)
    hbm = pl.BlockSpec(memory_space=pl.ANY)
    return pl.pallas_call(
        rows_kernel,
        in_specs=[pl.BlockSpec(memory_space=pltpu.SMEM), hbm, hbm, hbm, hbm],
        out_specs=[vmem] * 4,
        out_shape=[jax.ShapeDtypeStruct((rows // 2, w.shape[1]), bf16)] * 2
        + [jax.ShapeDtypeStruct((LEAVES, cols), f32)] * 2,
        scratch_shapes=[
            pltpu.VMEM(leaf.shape, jnp.int32),
            pltpu.VMEM((chunks, blk, cols), bf16),
            pltpu.VMEM((chunks, blk, cols), bf16),
            pltpu.VMEM(w.shape, bf16),
            pltpu.SemaphoreType.DMA((chunks,)),
            pltpu.SemaphoreType.DMA((chunks,)),
            pltpu.SemaphoreType.DMA,
            pltpu.SemaphoreType.DMA,
        ],
        compiler_params=PARAMS,
        name="rows",
    )(pos, leaf, pred, lab, w)


def part_add(part, parts):
    def kernel(a_ref, b_ref, out_ref):
        width = out_ref.shape[1]
        at = slice(part * width, (part + 1) * width)
        out_ref[...] = (a_ref[:, at].astype(f32) + b_ref[:, at].astype(f32)).astype(bf16)
    return kernel


def add_kernel(a_ref, b_ref, out_ref):
    out_ref[...] = (a_ref[...].astype(f32) + b_ref[...].astype(f32)).astype(out_ref.dtype)


def leaf_pack_kernel(g_ref, h_ref, keep_ref, send_ref):
    half = LEAVES // 2
    keep_ref[:half] = g_ref[:half]
    keep_ref[half:] = h_ref[:half]
    send_ref[:half] = g_ref[half:].astype(bf16)
    send_ref[half:] = h_ref[half:].astype(bf16)


def value_kernel(a_ref, b_ref, out_ref):
    half = LEAVES // 2
    total = a_ref[...].astype(f32) + b_ref[...].astype(f32)
    out_ref[...] = (total[:half] / (total[half:] + ridge_term)).astype(bf16)


def halving_kernel(here_ref, back_ref, keep_ref, send_ref):
    half = keep_ref.shape[0]
    keep_ref[...] = here_ref[:half] + back_ref[:half].astype(f32)
    send_ref[...] = (here_ref[half:] + back_ref[half:].astype(f32)).astype(bf16)


def last_kernel(*refs):
    out_ref = refs[-1]
    width = refs[0].shape[2]
    for p in range(len(refs) // 2):
        out_ref[:, p * width:(p + 1) * width] = refs[2 * p][0] + refs[2 * p + 1][0].astype(f32)


def hist_kernel(codes_ref, after_ref, *refs, per, odd, bits):
    parts = len(refs) // 3
    feats = codes_ref.shape[1]
    half = codes_ref.shape[2]
    codes = codes_ref[...].astype(f32).astype(bf16)
    step = pl.program_id(0)
    place = sum(((step >> b) & 1) << (bits - 1 - b) for b in range(bits))
    base = (2 * place + odd) * per
    levels = (lax.broadcasted_iota(jnp.int32, (per, 1, 1), 0) + base).astype(f32).astype(bf16)
    one = jnp.ones((), bf16)
    zero = jnp.zeros((), bf16)
    total = None
    for h in range(2):
        hot = jnp.where(codes[h][None] == levels, one, zero).reshape(per * feats, half)
        rows = refs[h * parts:(h + 1) * parts]
        sketch = jnp.concatenate([r[...] for r in rows], axis=1) if parts > 1 else rows[0][...]
        term = jnp.dot(hot, sketch, preferred_element_type=f32)
        total = term if total is None else total + term
    width = refs[-1].shape[2]
    for p in range(parts):
        out = refs[2 * parts + p]
        out[0] = total[:, p * width:(p + 1) * width].astype(out.dtype)


def hist_pass(codes, owns, others, per, blocks, odd, dtype, after, gflop):
    feats = codes.shape[1]
    width = owns[0].shape[1]
    parts = len(owns)
    whole = lambda a: pl.BlockSpec(a.shape, lambda i: (0,) * a.ndim)
    return pl.pallas_call(
        functools.partial(hist_kernel, per=per, odd=odd, bits=blocks.bit_length() - 1),
        grid=(blocks,),
        in_specs=[whole(codes), pl.BlockSpec(memory_space=pl.ANY)] + [whole(a) for a in owns + others],
        out_specs=[pl.BlockSpec((1, per * feats, width), lambda i: (i, 0, 0))] * parts,
        out_shape=[jax.ShapeDtypeStruct((blocks, per * feats, width), dtype)] * parts,
        cost_estimate=cost(gflop),
        compiler_params=PARAMS,
        name="hist_send" if odd else "hist_keep",
    )(codes, after, *owns, *others)


def update_kernel(pos_ref, leaf_ref, own_ref, other_ref, pred_ref, after_ref, *rest, first):
    if first:
        new_hbm, values_hbm, done_ref, new_buf, new_sem, values_buf, values_sem = rest
    else:
        _, new_hbm, done_ref, new_buf, new_sem = rest
    side = pos_ref[1]
    chunks, blk, _ = new_buf.shape
    start = 0 if first else chunks
    half = LEAVES // 2

    def write(i):
        return pltpu.make_async_copy(new_buf.at[i], new_hbm.at[pl.ds((start + i) * blk, blk)], new_sem.at[i])

    own, other = own_ref[...], other_ref[...]
    if first:
        low = side == 0
        values_buf[:half] = jnp.where(low, own.astype(f32), other.astype(f32))
        values_buf[half:] = jnp.where(low, other.astype(f32), own.astype(f32))
        values_copy = pltpu.make_async_copy(values_buf, values_hbm, values_sem)
        values_copy.start()
    table = jnp.concatenate([own, other], axis=0)
    for i in range(chunks):
        hot = leaf_hot(leaf_ref, start + i, blk, side * half, shrinkage)
        found = lax.dot_general(hot, table, (((0,), (0,)), ((), ())), preferred_element_type=f32)
        pred = pred_ref[pl.ds((start + i) * blk, blk)]
        new_buf[i] = (pred.astype(f32) + found).astype(bf16)
        write(i).start()
    done_ref[...] = jnp.zeros_like(done_ref)
    if first:
        values_copy.wait()
    for i in range(chunks):
        write(i).wait()


def update_pass(pos, leaf, own, other, pred, after, begun):
    rows, cols = pred.shape
    blk = block_rows(rows // 2)
    chunks = rows // blk // 2
    first = begun is None
    vmem = pl.BlockSpec(memory_space=pltpu.VMEM)
    hbm = pl.BlockSpec(memory_space=pl.ANY)
    new = jax.ShapeDtypeStruct((rows, cols), bf16)
    done = jax.ShapeDtypeStruct((8, 128), f32)
    return pl.pallas_call(
        functools.partial(update_kernel, first=first),
        in_specs=[pl.BlockSpec(memory_space=pltpu.SMEM), vmem, vmem, vmem, vmem, hbm] + [hbm] * (not first),
        out_specs=[hbm] * (1 + first) + [vmem],
        out_shape=[new, jax.ShapeDtypeStruct((LEAVES, cols), f32), done] if first else [new, done],
        scratch_shapes=[
            pltpu.VMEM((chunks, blk, cols), bf16),
            pltpu.SemaphoreType.DMA((chunks,)),
        ] + ([pltpu.VMEM((LEAVES, cols), f32), pltpu.SemaphoreType.DMA] if first else []),
        input_output_aliases={} if first else {6: 0},
        cost_estimate=cost(3.0),
        compiler_params=PARAMS,
        name="update_first" if first else "update_second",
    )(pos, leaf, own, other, pred, after, *([] if first else [begun]))


def local(n, nf, predictions, labels, feature_codes, leaf_index, sketch_weight):
    rows, cols = predictions.shape
    feats = feature_codes.shape[0]
    half = rows // 2
    parts = 2
    width = sketch_weight.shape[1] // parts
    me = lax.axis_index("rows")
    core = lax.axis_index("feat") & 1
    pos = jnp.stack([core, me & 1])
    per = BINS // n
    codes = (feature_codes ^ (me * per)).reshape(feats, 2, half)
    codes = jnp.where(core == 0, codes, codes[:, ::-1]).swapaxes(0, 1)
    lanes = min(128, block_rows(half))
    leaf = leaf_index.reshape(rows // lanes, lanes)

    pred = pltpu.with_memory_space_constraint(predictions, pltpu.HBM)
    lab = pltpu.with_memory_space_constraint(labels, pltpu.HBM)
    weight = pltpu.with_memory_space_constraint(sketch_weight, pltpu.HBM)
    sketch16 = jax.ShapeDtypeStruct((half, width), bf16)
    sums16 = jax.ShapeDtypeStruct((LEAVES, cols), bf16)
    sums32 = jax.ShapeDtypeStruct((LEAVES, cols), f32)

    send, keep, grad, hess = rows_pass(pos, pltpu.with_memory_space_constraint(leaf, pltpu.HBM), pred, lab, weight)
    got = swap(send, "feat", nf, 1)
    after = keep
    pair, crossed, owns, others, backs, heres = ([None] * parts for _ in range(6))
    leaf_state = None
    updated = leaf_values = None
    levels = (n // 2).bit_length() - 1

    def core_add(p):
        nonlocal after
        after = pair[p] = ordered(part_add(p, parts), sketch16, [keep, got], after, "core_add", 1.0)
        crossed[p] = [swap(after, "feat", nf, t) for t in range(2, nf, 2)]

    def feat_add(p):
        nonlocal after
        own = pair[p]
        for recv in crossed[p]:
            after = own = ordered(add_kernel, sketch16, [own, recv], after, "feat_add")
        owns[p] = own
        others[p] = swap(own, "feat", nf, 1)

    def leaf_pack():
        nonlocal after, leaf_state
        after, sent = ordered(leaf_pack_kernel, [sums32, sums16], [grad, hess], after, "leaf_pack")
        leaf_state = (after, swap(sent, "rows", n, 1), 2)

    def leaf_step():
        nonlocal after, leaf_state
        acc, recv, by = leaf_state
        if by < n:
            after = ordered(add_kernel, sums16, [acc, recv], after, "leaf_add", 1.0 if by == 2 else 3.0)
            leaf_state = (after, swap(after, "rows", n, by), 2 * by)
        elif by == n:
            values16 = jax.ShapeDtypeStruct((LEAVES // 2, cols), bf16)
            after = ordered(value_kernel, values16, [acc, recv], after, "leaf_value")
            leaf_state = (after, swap(after, "rows", n, 1), 2 * by)

    def update():
        nonlocal after, updated, leaf_values
        while leaf_state[2] <= n:
            leaf_step()
        if updated is None:
            updated, leaf_values, after = update_pass(pos, leaf, leaf_state[0], leaf_state[1], predictions, after, None)
        else:
            updated, after = update_pass(pos, leaf, leaf_state[0], leaf_state[1], predictions, after, updated)

    def hist_send(p):
        nonlocal after
        after, = hist_pass(codes, [owns[p]], [others[p]], per, n // 2, 1, bf16, after, (1.0, 3.0)[p])
        backs[p] = swap(after, "rows", n, 1)

    def hist_keep():
        nonlocal after
        heres[:] = hist_pass(codes, owns, others, per, n // 2, 0, f32, after, 3.0)
        after = heres[-1]

    def hist_add(p, level):
        nonlocal after
        blocks = heres[p].shape[0] // 2
        shape = (blocks,) + heres[p].shape[1:]
        heres[p], sent = ordered(
            halving_kernel,
            [jax.ShapeDtypeStruct(shape, f32), jax.ShapeDtypeStruct(shape, bf16)],
            [heres[p], backs[p]], after, "hist_add")
        after = heres[p]
        backs[p] = swap(sent, "rows", n, 2 << level)

    leaf_pack()
    core_add(0)
    core_add(1)
    leaf_step()
    feat_add(0)
    hist_send(0)
    feat_add(1)
    leaf_step()
    hist_send(1)
    hist_keep()
    for level in range(levels):
        hist_add(0, level)
        if level == levels - 1:
            update()
        hist_add(1, level)
        if level == 0:
            leaf_step()
    update()
    histograms = ordered(
        last_kernel, jax.ShapeDtypeStruct((per * feats, width * parts), f32),
        [a for p in range(parts) for a in (heres[p], backs[p])], after, "last_add")
    return histograms.reshape(per, feats, -1), leaf_values, updated


def solution(mesh):
    n, nf = mesh.shape["rows"], mesh.shape["feat"]
    return jax.shard_map(
        functools.partial(local, n, nf),
        mesh=mesh,
        in_specs=(
            P("rows", "feat"),
            P("rows", "feat"),
            P("feat", "rows"),
            P("rows"),
            P("feat", None),
        ),
        out_specs=(P("rows", "feat", None), P(None, "feat"), P("rows", "feat")),
        check_vma=False,
    )
```

```python
import functools

import jax
import jax.numpy as jnp
from jax import lax
from jax.experimental import pallas as pl
from jax.experimental.pallas import tpu as pltpu
from jax.sharding import PartitionSpec as P

BINS = 256
LEAVES = 64


shrinkage = 0.5
ridge_term = 1.0

f32 = jnp.float32
bf16 = jnp.bfloat16
VMEM_LIMIT = 16 * 1024 * 1024


def block_rows(rows):
    for size in (256, 128, 64, 32, 16):
        if rows % size == 0:
            return size
    return rows


def cost(gflop):
    return pl.CostEstimate(flops=int(gflop * 1e9), transcendentals=0, bytes_accessed=0)


PARAMS = pltpu.CompilerParams(vmem_limit_bytes=VMEM_LIMIT)


def swap(x, axis, size, by):
    return lax.ppermute(x, axis, [(i, i ^ by) for i in range(size)])


def ordered(kernel, out_shape, args, after, name, gflop=0):
    def body(*refs):
        kernel(*refs[:len(args)], *refs[len(args) + 1:])

    many = isinstance(out_shape, (list, tuple))
    return pl.pallas_call(
        body,
        in_specs=[pl.BlockSpec(memory_space=pltpu.VMEM)] * len(args) + [pl.BlockSpec(memory_space=pl.ANY)],
        out_specs=[pl.BlockSpec(memory_space=pltpu.VMEM)] * len(out_shape)
        if many else pl.BlockSpec(memory_space=pltpu.VMEM),
        out_shape=out_shape,
        cost_estimate=cost(gflop),
        compiler_params=PARAMS,
        name=name,
    )(*args, after)


def leaf_hot(leaf_ref, chunk, blk, flip, scale):
    lanes = leaf_ref.shape[1]
    lines = blk // lanes
    leaf = jnp.concatenate([leaf_ref[pl.ds(chunk * lines + j, 1)] for j in range(lines)], axis=1)
    hot = lax.broadcasted_iota(jnp.int32, (LEAVES, blk), 0) == (leaf ^ flip)
    return jnp.where(hot, f32(scale), f32(0)).astype(bf16)


def chunk_place(i, chunks, core):
    per_half = chunks // 2
    half = 1 - core if i < per_half else core
    return half * per_half + i % per_half


def rows_kernel(pos_ref, leaf_hbm, pred_hbm, lab_hbm, w_hbm, send_ref, keep_ref, g_ref, h_ref,
                leaf_buf, pred_buf, lab_buf, w_buf, pred_sem, lab_sem, w_sem, leaf_sem):
    core, side = pos_ref[0], pos_ref[1]
    chunks, blk, _ = pred_buf.shape
    per_half = chunks // 2

    def copies(i):
        at = pl.ds(pl.multiple_of(chunk_place(i, chunks, core) * blk, blk), blk)
        return (pltpu.make_async_copy(pred_hbm.at[at], pred_buf.at[i], pred_sem.at[i]),
                pltpu.make_async_copy(lab_hbm.at[at], lab_buf.at[i], lab_sem.at[i]))

    w_copy = pltpu.make_async_copy(w_hbm, w_buf, w_sem)
    leaf_copy = pltpu.make_async_copy(leaf_hbm, leaf_buf, leaf_sem)
    for i in range(chunks):
        for copy in copies(i):
            copy.start()
        if i == 0:
            w_copy.start()
            leaf_copy.start()
    for i in range(chunks):
        for copy in copies(i):
            copy.wait()
        if i == 0:
            w_copy.wait()
            leaf_copy.wait()
        p = 0.5 * jnp.tanh((pred_buf[i] * 0.5).astype(f32)) + 0.5
        grad = (lab_buf[i].astype(f32) - p).astype(bf16)
        hess = (p - p * p).astype(bf16)
        out = send_ref if i < per_half else keep_ref
        out[pl.ds(i % per_half * blk, blk)] = jnp.dot(grad, w_buf[...], preferred_element_type=f32).astype(bf16)
        hot = leaf_hot(leaf_buf, chunk_place(i, chunks, core), blk, side * (LEAVES // 2), 1.0)
        g = jnp.dot(hot, grad, preferred_element_type=f32)
        h = jnp.dot(hot, hess, preferred_element_type=f32)
        if i == 0:
            g_ref[...] = g
            h_ref[...] = h
        else:
            g_ref[...] += g
            h_ref[...] += h


def rows_pass(pos, leaf, pred, lab, w):
    rows, cols = pred.shape
    blk = block_rows(rows // 2)
    chunks = rows // blk
    vmem = pl.BlockSpec(memory_space=pltpu.VMEM)
    hbm = pl.BlockSpec(memory_space=pl.ANY)
    return pl.pallas_call(
        rows_kernel,
        in_specs=[pl.BlockSpec(memory_space=pltpu.SMEM), hbm, hbm, hbm, hbm],
        out_specs=[vmem] * 4,
        out_shape=[jax.ShapeDtypeStruct((rows // 2, w.shape[1]), bf16)] * 2
        + [jax.ShapeDtypeStruct((LEAVES, cols), f32)] * 2,
        scratch_shapes=[
            pltpu.VMEM(leaf.shape, jnp.int32),
            pltpu.VMEM((chunks, blk, cols), bf16),
            pltpu.VMEM((chunks, blk, cols), bf16),
            pltpu.VMEM(w.shape, bf16),
            pltpu.SemaphoreType.DMA((chunks,)),
            pltpu.SemaphoreType.DMA((chunks,)),
            pltpu.SemaphoreType.DMA,
            pltpu.SemaphoreType.DMA,
        ],
        compiler_params=PARAMS,
        name="rows",
    )(pos, leaf, pred, lab, w)


def part_add(part, parts):
    def kernel(a_ref, b_ref, out_ref):
        width = out_ref.shape[1]
        at = slice(part * width, (part + 1) * width)
        out_ref[...] = (a_ref[:, at].astype(f32) + b_ref[:, at].astype(f32)).astype(bf16)
    return kernel


def add_kernel(a_ref, b_ref, out_ref):
    out_ref[...] = (a_ref[...].astype(f32) + b_ref[...].astype(f32)).astype(out_ref.dtype)


def leaf_pack_kernel(g_ref, h_ref, keep_ref, send_ref):
    half = LEAVES // 2
    keep_ref[:half] = g_ref[:half]
    keep_ref[half:] = h_ref[:half]
    send_ref[:half] = g_ref[half:].astype(bf16)
    send_ref[half:] = h_ref[half:].astype(bf16)


def value_kernel(a_ref, b_ref, out_ref):
    half = LEAVES // 2
    total = a_ref[...].astype(f32) + b_ref[...].astype(f32)
    out_ref[...] = (total[:half] / (total[half:] + ridge_term)).astype(bf16)


def halving_kernel(here_ref, back_ref, keep_ref, send_ref):
    half = keep_ref.shape[0]
    keep_ref[...] = here_ref[:half] + back_ref[:half].astype(f32)
    send_ref[...] = (here_ref[half:] + back_ref[half:].astype(f32)).astype(bf16)


def last_kernel(*refs):
    out_ref = refs[-1]
    width = refs[0].shape[2]
    for p in range(len(refs) // 2):
        out_ref[:, p * width:(p + 1) * width] = refs[2 * p][0] + refs[2 * p + 1][0].astype(f32)


def hist_kernel(codes_ref, after_ref, *refs, per, odd, bits):
    parts = len(refs) // 3
    feats = codes_ref.shape[1]
    half = codes_ref.shape[2]
    codes = codes_ref[...].astype(f32).astype(bf16)
    step = pl.program_id(0)
    place = sum(((step >> b) & 1) << (bits - 1 - b) for b in range(bits))
    base = (2 * place + odd) * per
    levels = (lax.broadcasted_iota(jnp.int32, (per, 1, 1), 0) + base).astype(f32).astype(bf16)
    one = jnp.ones((), bf16)
    zero = jnp.zeros((), bf16)
    total = None
    for h in range(2):
        hot = jnp.where(codes[h][None] == levels, one, zero).reshape(per * feats, half)
        rows = refs[h * parts:(h + 1) * parts]
        sketch = jnp.concatenate([r[...] for r in rows], axis=1) if parts > 1 else rows[0][...]
        term = jnp.dot(hot, sketch, preferred_element_type=f32)
        total = term if total is None else total + term
    width = refs[-1].shape[2]
    for p in range(parts):
        out = refs[2 * parts + p]
        out[0] = total[:, p * width:(p + 1) * width].astype(out.dtype)


def hist_pass(codes, owns, others, per, blocks, odd, dtype, after, gflop):
    feats = codes.shape[1]
    width = owns[0].shape[1]
    parts = len(owns)
    whole = lambda a: pl.BlockSpec(a.shape, lambda i: (0,) * a.ndim)
    return pl.pallas_call(
        functools.partial(hist_kernel, per=per, odd=odd, bits=blocks.bit_length() - 1),
        grid=(blocks,),
        in_specs=[whole(codes), pl.BlockSpec(memory_space=pl.ANY)] + [whole(a) for a in owns + others],
        out_specs=[pl.BlockSpec((1, per * feats, width), lambda i: (i, 0, 0))] * parts,
        out_shape=[jax.ShapeDtypeStruct((blocks, per * feats, width), dtype)] * parts,
        cost_estimate=cost(gflop),
        compiler_params=PARAMS,
        name="hist_send" if odd else "hist_keep",
    )(codes, after, *owns, *others)


def update_kernel(pos_ref, leaf_ref, own_ref, other_ref, pred_ref, after_ref, *rest, first):
    if first:
        new_hbm, values_hbm, done_ref, new_buf, new_sem, values_buf, values_sem = rest
    else:
        _, new_hbm, done_ref, new_buf, new_sem = rest
    side = pos_ref[1]
    chunks, blk, _ = new_buf.shape
    start = 0 if first else chunks
    half = LEAVES // 2

    def write(i):
        return pltpu.make_async_copy(new_buf.at[i], new_hbm.at[pl.ds((start + i) * blk, blk)], new_sem.at[i])

    own, other = own_ref[...], other_ref[...]
    if first:
        low = side == 0
        values_buf[:half] = jnp.where(low, own.astype(f32), other.astype(f32))
        values_buf[half:] = jnp.where(low, other.astype(f32), own.astype(f32))
        values_copy = pltpu.make_async_copy(values_buf, values_hbm, values_sem)
        values_copy.start()
    table = jnp.concatenate([own, other], axis=0)
    for i in range(chunks):
        hot = leaf_hot(leaf_ref, start + i, blk, side * half, shrinkage)
        found = lax.dot_general(hot, table, (((0,), (0,)), ((), ())), preferred_element_type=f32)
        pred = pred_ref[pl.ds((start + i) * blk, blk)]
        new_buf[i] = (pred.astype(f32) + found).astype(bf16)
        write(i).start()
    done_ref[...] = jnp.zeros_like(done_ref)
    if first:
        values_copy.wait()
    for i in range(chunks):
        write(i).wait()


def update_pass(pos, leaf, own, other, pred, after, begun):
    rows, cols = pred.shape
    blk = block_rows(rows // 2)
    chunks = rows // blk // 2
    first = begun is None
    vmem = pl.BlockSpec(memory_space=pltpu.VMEM)
    hbm = pl.BlockSpec(memory_space=pl.ANY)
    new = jax.ShapeDtypeStruct((rows, cols), bf16)
    done = jax.ShapeDtypeStruct((8, 128), f32)
    return pl.pallas_call(
        functools.partial(update_kernel, first=first),
        in_specs=[pl.BlockSpec(memory_space=pltpu.SMEM), vmem, vmem, vmem, vmem, hbm] + [hbm] * (not first),
        out_specs=[hbm] * (1 + first) + [vmem],
        out_shape=[new, jax.ShapeDtypeStruct((LEAVES, cols), f32), done] if first else [new, done],
        scratch_shapes=[
            pltpu.VMEM((chunks, blk, cols), bf16),
            pltpu.SemaphoreType.DMA((chunks,)),
        ] + ([pltpu.VMEM((LEAVES, cols), f32), pltpu.SemaphoreType.DMA] if first else []),
        input_output_aliases={} if first else {6: 0},
        cost_estimate=cost(3.0),
        compiler_params=PARAMS,
        name="update_first" if first else "update_second",
    )(pos, leaf, own, other, pred, after, *([] if first else [begun]))


def local(n, nf, predictions, labels, feature_codes, leaf_index, sketch_weight):
    rows, cols = predictions.shape
    feats = feature_codes.shape[0]
    half = rows // 2
    parts = 2
    width = sketch_weight.shape[1] // parts
    me = lax.axis_index("rows")
    core = lax.axis_index("feat") & 1
    pos = jnp.stack([core, me & 1])
    per = BINS // n
    codes = (feature_codes ^ (me * per)).reshape(feats, 2, half)
    codes = jnp.where(core == 0, codes, codes[:, ::-1]).swapaxes(0, 1)
    lanes = min(128, block_rows(half))
    leaf = leaf_index.reshape(rows // lanes, lanes)

    pred = pltpu.with_memory_space_constraint(predictions, pltpu.HBM)
    lab = pltpu.with_memory_space_constraint(labels, pltpu.HBM)
    weight = pltpu.with_memory_space_constraint(sketch_weight, pltpu.HBM)
    sketch16 = jax.ShapeDtypeStruct((half, width), bf16)
    sums16 = jax.ShapeDtypeStruct((LEAVES, cols), bf16)
    sums32 = jax.ShapeDtypeStruct((LEAVES, cols), f32)

    send, keep, grad, hess = rows_pass(pos, pltpu.with_memory_space_constraint(leaf, pltpu.HBM), pred, lab, weight)
    got = swap(send, "feat", nf, 1)
    after = keep
    pair, crossed, owns, others, backs, heres = ([None] * parts for _ in range(6))
    leaf_state = None
    updated = leaf_values = None
    levels = (n // 2).bit_length() - 1

    def core_add(p):
        nonlocal after
        after = pair[p] = ordered(part_add(p, parts), sketch16, [keep, got], after, "core_add", 1.0)
        crossed[p] = [swap(after, "feat", nf, t) for t in range(2, nf, 2)]

    def feat_add(p):
        nonlocal after
        own = pair[p]
        for recv in crossed[p]:
            after = own = ordered(add_kernel, sketch16, [own, recv], after, "feat_add")
        owns[p] = own
        others[p] = swap(own, "feat", nf, 1)

    def leaf_pack():
        nonlocal after, leaf_state
        after, sent = ordered(leaf_pack_kernel, [sums32, sums16], [grad, hess], after, "leaf_pack")
        leaf_state = (after, swap(sent, "rows", n, 1), 2)

    def leaf_step():
        nonlocal after, leaf_state
        acc, recv, by = leaf_state
        if by < n:
            after = ordered(add_kernel, sums16, [acc, recv], after, "leaf_add", 1.0 if by == 2 else 3.0)
            leaf_state = (after, swap(after, "rows", n, by), 2 * by)
        elif by == n:
            values16 = jax.ShapeDtypeStruct((LEAVES // 2, cols), bf16)
            after = ordered(value_kernel, values16, [acc, recv], after, "leaf_value")
            leaf_state = (after, swap(after, "rows", n, 1), 2 * by)

    def update():
        nonlocal after, updated, leaf_values
        while leaf_state[2] <= n:
            leaf_step()
        if updated is None:
            updated, leaf_values, after = update_pass(pos, leaf, leaf_state[0], leaf_state[1], predictions, after, None)
        else:
            updated, after = update_pass(pos, leaf, leaf_state[0], leaf_state[1], predictions, after, updated)

    def hist_send(p):
        nonlocal after
        after, = hist_pass(codes, [owns[p]], [others[p]], per, n // 2, 1, bf16, after, (3.0, 3.0)[p])
        backs[p] = swap(after, "rows", n, 1)

    def hist_keep():
        nonlocal after
        heres[:] = hist_pass(codes, owns, others, per, n // 2, 0, f32, after, 3.0)
        after = heres[-1]

    def hist_add(p, level):
        nonlocal after
        blocks = heres[p].shape[0] // 2
        shape = (blocks,) + heres[p].shape[1:]
        heres[p], sent = ordered(
            halving_kernel,
            [jax.ShapeDtypeStruct(shape, f32), jax.ShapeDtypeStruct(shape, bf16)],
            [heres[p], backs[p]], after, "hist_add")
        after = heres[p]
        backs[p] = swap(sent, "rows", n, 2 << level)

    leaf_pack()
    core_add(0)
    core_add(1)
    leaf_step()
    feat_add(0)
    hist_send(0)
    feat_add(1)
    leaf_step()
    hist_send(1)
    hist_keep()
    hist_add(0, 0)
    leaf_step()
    hist_add(1, 0)
    for level in range(1, levels):
        hist_add(0, level)
        if level == levels - 1:
            update()
        hist_add(1, level)
    update()
    histograms = ordered(
        last_kernel, jax.ShapeDtypeStruct((per * feats, width * parts), f32),
        [a for p in range(parts) for a in (heres[p], backs[p])], after, "last_add")
    return histograms.reshape(per, feats, -1), leaf_values, updated


def solution(mesh):
    n, nf = mesh.shape["rows"], mesh.shape["feat"]
    return jax.shard_map(
        functools.partial(local, n, nf),
        mesh=mesh,
        in_specs=(
            P("rows", "feat"),
            P("rows", "feat"),
            P("feat", "rows"),
            P("rows"),
            P("feat", None),
        ),
        out_specs=(P("rows", "feat", None), P(None, "feat"), P("rows", "feat")),
        check_vma=False,
    )
```

```python
import functools

import jax
import jax.numpy as jnp
from jax import lax
from jax.experimental import pallas as pl
from jax.experimental.pallas import tpu as pltpu
from jax.sharding import PartitionSpec as P

BINS = 256
LEAVES = 64


shrinkage = 0.5
ridge_term = 1.0

f32 = jnp.float32
bf16 = jnp.bfloat16
VMEM_LIMIT = 16 * 1024 * 1024


def block_rows(rows):
    for size in (256, 128, 64, 32, 16):
        if rows % size == 0:
            return size
    return rows


def cost(gflop):
    return pl.CostEstimate(flops=int(gflop * 1e9), transcendentals=0, bytes_accessed=0)


PARAMS = pltpu.CompilerParams(vmem_limit_bytes=VMEM_LIMIT)


def swap(x, axis, size, by):
    return lax.ppermute(x, axis, [(i, i ^ by) for i in range(size)])


def ordered(kernel, out_shape, args, after, name, gflop=0):
    def body(*refs):
        kernel(*refs[:len(args)], *refs[len(args) + 1:])

    many = isinstance(out_shape, (list, tuple))
    return pl.pallas_call(
        body,
        in_specs=[pl.BlockSpec(memory_space=pltpu.VMEM)] * len(args) + [pl.BlockSpec(memory_space=pl.ANY)],
        out_specs=[pl.BlockSpec(memory_space=pltpu.VMEM)] * len(out_shape)
        if many else pl.BlockSpec(memory_space=pltpu.VMEM),
        out_shape=out_shape,
        cost_estimate=cost(gflop),
        compiler_params=PARAMS,
        name=name,
    )(*args, after)


def leaf_hot(leaf_ref, chunk, blk, flip, scale):
    lanes = leaf_ref.shape[1]
    lines = blk // lanes
    leaf = jnp.concatenate([leaf_ref[pl.ds(chunk * lines + j, 1)] for j in range(lines)], axis=1)
    hot = lax.broadcasted_iota(jnp.int32, (LEAVES, blk), 0) == (leaf ^ flip)
    return jnp.where(hot, f32(scale), f32(0)).astype(bf16)


def chunk_place(i, chunks, core):
    per_half = chunks // 2
    half = 1 - core if i < per_half else core
    return half * per_half + i % per_half


def rows_kernel(pos_ref, leaf_hbm, pred_hbm, lab_hbm, w_hbm, send_ref, keep_ref, g_ref, h_ref,
                leaf_buf, pred_buf, lab_buf, w_buf, pred_sem, lab_sem, w_sem, leaf_sem):
    core, side = pos_ref[0], pos_ref[1]
    chunks, blk, _ = pred_buf.shape
    per_half = chunks // 2

    def copies(i):
        at = pl.ds(pl.multiple_of(chunk_place(i, chunks, core) * blk, blk), blk)
        return (pltpu.make_async_copy(pred_hbm.at[at], pred_buf.at[i], pred_sem.at[i]),
                pltpu.make_async_copy(lab_hbm.at[at], lab_buf.at[i], lab_sem.at[i]))

    w_copy = pltpu.make_async_copy(w_hbm, w_buf, w_sem)
    leaf_copy = pltpu.make_async_copy(leaf_hbm, leaf_buf, leaf_sem)
    for i in range(chunks):
        for copy in copies(i):
            copy.start()
        if i == 0:
            w_copy.start()
            leaf_copy.start()
    for i in range(chunks):
        for copy in copies(i):
            copy.wait()
        if i == 0:
            w_copy.wait()
            leaf_copy.wait()
        p = 0.5 * jnp.tanh((pred_buf[i] * 0.5).astype(f32)) + 0.5
        grad = (lab_buf[i].astype(f32) - p).astype(bf16)
        hess = (p - p * p).astype(bf16)
        out = send_ref if i < per_half else keep_ref
        out[pl.ds(i % per_half * blk, blk)] = jnp.dot(grad, w_buf[...], preferred_element_type=f32).astype(bf16)
        hot = leaf_hot(leaf_buf, chunk_place(i, chunks, core), blk, side * (LEAVES // 2), 1.0)
        g = jnp.dot(hot, grad, preferred_element_type=f32)
        h = jnp.dot(hot, hess, preferred_element_type=f32)
        if i == 0:
            g_ref[...] = g
            h_ref[...] = h
        else:
            g_ref[...] += g
            h_ref[...] += h


def rows_pass(pos, leaf, pred, lab, w):
    rows, cols = pred.shape
    blk = min(128, block_rows(rows // 2))
    chunks = rows // blk
    vmem = pl.BlockSpec(memory_space=pltpu.VMEM)
    hbm = pl.BlockSpec(memory_space=pl.ANY)
    return pl.pallas_call(
        rows_kernel,
        in_specs=[pl.BlockSpec(memory_space=pltpu.SMEM), hbm, hbm, hbm, hbm],
        out_specs=[vmem] * 4,
        out_shape=[jax.ShapeDtypeStruct((rows // 2, w.shape[1]), bf16)] * 2
        + [jax.ShapeDtypeStruct((LEAVES, cols), f32)] * 2,
        scratch_shapes=[
            pltpu.VMEM(leaf.shape, jnp.int32),
            pltpu.VMEM((chunks, blk, cols), bf16),
            pltpu.VMEM((chunks, blk, cols), bf16),
            pltpu.VMEM(w.shape, bf16),
            pltpu.SemaphoreType.DMA((chunks,)),
            pltpu.SemaphoreType.DMA((chunks,)),
            pltpu.SemaphoreType.DMA,
            pltpu.SemaphoreType.DMA,
        ],
        compiler_params=PARAMS,
        name="rows",
    )(pos, leaf, pred, lab, w)


def part_add(part, parts):
    def kernel(a_ref, b_ref, out_ref):
        width = out_ref.shape[1]
        at = slice(part * width, (part + 1) * width)
        out_ref[...] = (a_ref[:, at].astype(f32) + b_ref[:, at].astype(f32)).astype(bf16)
    return kernel


def add_kernel(a_ref, b_ref, out_ref):
    out_ref[...] = (a_ref[...].astype(f32) + b_ref[...].astype(f32)).astype(out_ref.dtype)


def leaf_pack_kernel(g_ref, h_ref, keep_ref, send_ref):
    half = LEAVES // 2
    keep_ref[:half] = g_ref[:half]
    keep_ref[half:] = h_ref[:half]
    send_ref[:half] = g_ref[half:].astype(bf16)
    send_ref[half:] = h_ref[half:].astype(bf16)


def value_kernel(a_ref, b_ref, out_ref):
    half = LEAVES // 2
    total = a_ref[...].astype(f32) + b_ref[...].astype(f32)
    out_ref[...] = (total[:half] / (total[half:] + ridge_term)).astype(bf16)


def halving_kernel(here_ref, back_ref, keep_ref, send_ref):
    half = keep_ref.shape[0]
    keep_ref[...] = here_ref[:half] + back_ref[:half].astype(f32)
    send_ref[...] = (here_ref[half:] + back_ref[half:].astype(f32)).astype(bf16)


def last_kernel(*refs):
    out_ref = refs[-1]
    width = refs[0].shape[2]
    for p in range(len(refs) // 2):
        out_ref[:, p * width:(p + 1) * width] = refs[2 * p][0] + refs[2 * p + 1][0].astype(f32)


def hist_kernel(codes_ref, after_ref, *refs, per, odd, bits):
    parts = len(refs) // 3
    feats = codes_ref.shape[1]
    half = codes_ref.shape[2]
    codes = codes_ref[...].astype(f32).astype(bf16)
    step = pl.program_id(0)
    place = sum(((step >> b) & 1) << (bits - 1 - b) for b in range(bits))
    base = (2 * place + odd) * per
    levels = (lax.broadcasted_iota(jnp.int32, (per, 1, 1), 0) + base).astype(f32).astype(bf16)
    one = jnp.ones((), bf16)
    zero = jnp.zeros((), bf16)
    total = None
    for h in range(2):
        hot = jnp.where(codes[h][None] == levels, one, zero).reshape(per * feats, half)
        rows = refs[h * parts:(h + 1) * parts]
        sketch = jnp.concatenate([r[...] for r in rows], axis=1) if parts > 1 else rows[0][...]
        term = jnp.dot(hot, sketch, preferred_element_type=f32)
        total = term if total is None else total + term
    width = refs[-1].shape[2]
    for p in range(parts):
        out = refs[2 * parts + p]
        out[0] = total[:, p * width:(p + 1) * width].astype(out.dtype)


def hist_pass(codes, owns, others, per, blocks, odd, dtype, after, gflop):
    feats = codes.shape[1]
    width = owns[0].shape[1]
    parts = len(owns)
    whole = lambda a: pl.BlockSpec(a.shape, lambda i: (0,) * a.ndim)
    return pl.pallas_call(
        functools.partial(hist_kernel, per=per, odd=odd, bits=blocks.bit_length() - 1),
        grid=(blocks,),
        in_specs=[whole(codes), pl.BlockSpec(memory_space=pl.ANY)] + [whole(a) for a in owns + others],
        out_specs=[pl.BlockSpec((1, per * feats, width), lambda i: (i, 0, 0))] * parts,
        out_shape=[jax.ShapeDtypeStruct((blocks, per * feats, width), dtype)] * parts,
        cost_estimate=cost(gflop),
        compiler_params=PARAMS,
        name="hist_send" if odd else "hist_keep",
    )(codes, after, *owns, *others)


def update_kernel(pos_ref, leaf_ref, own_ref, other_ref, pred_ref, after_ref, *rest, first):
    if first:
        new_hbm, values_hbm, done_ref, new_buf, new_sem, values_buf, values_sem = rest
    else:
        _, new_hbm, done_ref, new_buf, new_sem = rest
    side = pos_ref[1]
    chunks, blk, _ = new_buf.shape
    start = 0 if first else chunks
    half = LEAVES // 2

    def write(i):
        return pltpu.make_async_copy(new_buf.at[i], new_hbm.at[pl.ds((start + i) * blk, blk)], new_sem.at[i])

    own, other = own_ref[...], other_ref[...]
    if first:
        low = side == 0
        values_buf[:half] = jnp.where(low, own.astype(f32), other.astype(f32))
        values_buf[half:] = jnp.where(low, other.astype(f32), own.astype(f32))
        values_copy = pltpu.make_async_copy(values_buf, values_hbm, values_sem)
        values_copy.start()
    table = jnp.concatenate([own, other], axis=0)
    for i in range(chunks):
        hot = leaf_hot(leaf_ref, start + i, blk, side * half, shrinkage)
        found = lax.dot_general(hot, table, (((0,), (0,)), ((), ())), preferred_element_type=f32)
        pred = pred_ref[pl.ds((start + i) * blk, blk)]
        new_buf[i] = (pred.astype(f32) + found).astype(bf16)
        write(i).start()
    done_ref[...] = jnp.zeros_like(done_ref)
    if first:
        values_copy.wait()
    for i in range(chunks):
        write(i).wait()


def update_pass(pos, leaf, own, other, pred, after, begun):
    rows, cols = pred.shape
    blk = block_rows(rows // 2)
    chunks = rows // blk // 2
    first = begun is None
    vmem = pl.BlockSpec(memory_space=pltpu.VMEM)
    hbm = pl.BlockSpec(memory_space=pl.ANY)
    new = jax.ShapeDtypeStruct((rows, cols), bf16)
    done = jax.ShapeDtypeStruct((8, 128), f32)
    return pl.pallas_call(
        functools.partial(update_kernel, first=first),
        in_specs=[pl.BlockSpec(memory_space=pltpu.SMEM), vmem, vmem, vmem, vmem, hbm] + [hbm] * (not first),
        out_specs=[hbm] * (1 + first) + [vmem],
        out_shape=[new, jax.ShapeDtypeStruct((LEAVES, cols), f32), done] if first else [new, done],
        scratch_shapes=[
            pltpu.VMEM((chunks, blk, cols), bf16),
            pltpu.SemaphoreType.DMA((chunks,)),
        ] + ([pltpu.VMEM((LEAVES, cols), f32), pltpu.SemaphoreType.DMA] if first else []),
        input_output_aliases={} if first else {6: 0},
        cost_estimate=cost(3.0),
        compiler_params=PARAMS,
        name="update_first" if first else "update_second",
    )(pos, leaf, own, other, pred, after, *([] if first else [begun]))


def local(n, nf, predictions, labels, feature_codes, leaf_index, sketch_weight):
    rows, cols = predictions.shape
    feats = feature_codes.shape[0]
    half = rows // 2
    parts = 2
    width = sketch_weight.shape[1] // parts
    me = lax.axis_index("rows")
    core = lax.axis_index("feat") & 1
    pos = jnp.stack([core, me & 1])
    per = BINS // n
    codes = (feature_codes ^ (me * per)).reshape(feats, 2, half)
    codes = jnp.where(core == 0, codes, codes[:, ::-1]).swapaxes(0, 1)
    lanes = min(128, block_rows(half))
    leaf = leaf_index.reshape(rows // lanes, lanes)

    pred = pltpu.with_memory_space_constraint(predictions, pltpu.HBM)
    lab = pltpu.with_memory_space_constraint(labels, pltpu.HBM)
    weight = pltpu.with_memory_space_constraint(sketch_weight, pltpu.HBM)
    sketch16 = jax.ShapeDtypeStruct((half, width), bf16)
    sums16 = jax.ShapeDtypeStruct((LEAVES, cols), bf16)
    sums32 = jax.ShapeDtypeStruct((LEAVES, cols), f32)

    send, keep, grad, hess = rows_pass(pos, pltpu.with_memory_space_constraint(leaf, pltpu.HBM), pred, lab, weight)
    got = swap(send, "feat", nf, 1)
    after = keep
    pair, crossed, owns, others, backs, heres = ([None] * parts for _ in range(6))
    leaf_state = None
    updated = leaf_values = None
    levels = (n // 2).bit_length() - 1

    def core_add(p):
        nonlocal after
        after = pair[p] = ordered(part_add(p, parts), sketch16, [keep, got], after, "core_add", 1.0)
        crossed[p] = [swap(after, "feat", nf, t) for t in range(2, nf, 2)]

    def feat_add(p):
        nonlocal after
        own = pair[p]
        for recv in crossed[p]:
            after = own = ordered(add_kernel, sketch16, [own, recv], after, "feat_add")
        owns[p] = own
        others[p] = swap(own, "feat", nf, 1)

    def leaf_pack():
        nonlocal after, leaf_state
        after, sent = ordered(leaf_pack_kernel, [sums32, sums16], [grad, hess], after, "leaf_pack")
        leaf_state = (after, swap(sent, "rows", n, 1), 2)

    def leaf_step():
        nonlocal after, leaf_state
        acc, recv, by = leaf_state
        if by < n:
            after = ordered(add_kernel, sums16, [acc, recv], after, "leaf_add", 1.0 if by == 2 else 3.0)
            leaf_state = (after, swap(after, "rows", n, by), 2 * by)
        elif by == n:
            values16 = jax.ShapeDtypeStruct((LEAVES // 2, cols), bf16)
            after = ordered(value_kernel, values16, [acc, recv], after, "leaf_value")
            leaf_state = (after, swap(after, "rows", n, 1), 2 * by)

    def update():
        nonlocal after, updated, leaf_values
        while leaf_state[2] <= n:
            leaf_step()
        if updated is None:
            updated, leaf_values, after = update_pass(pos, leaf, leaf_state[0], leaf_state[1], predictions, after, None)
        else:
            updated, after = update_pass(pos, leaf, leaf_state[0], leaf_state[1], predictions, after, updated)

    def hist_send(p):
        nonlocal after
        after, = hist_pass(codes, [owns[p]], [others[p]], per, n // 2, 1, bf16, after, (1.0, 3.0)[p])
        backs[p] = swap(after, "rows", n, 1)

    def hist_keep():
        nonlocal after
        heres[:] = hist_pass(codes, owns, others, per, n // 2, 0, f32, after, 3.0)
        after = heres[-1]

    def hist_add(p, level):
        nonlocal after
        blocks = heres[p].shape[0] // 2
        shape = (blocks,) + heres[p].shape[1:]
        heres[p], sent = ordered(
            halving_kernel,
            [jax.ShapeDtypeStruct(shape, f32), jax.ShapeDtypeStruct(shape, bf16)],
            [heres[p], backs[p]], after, "hist_add")
        after = heres[p]
        backs[p] = swap(sent, "rows", n, 2 << level)

    leaf_pack()
    core_add(0)
    core_add(1)
    leaf_step()
    feat_add(0)
    hist_send(0)
    feat_add(1)
    leaf_step()
    hist_send(1)
    hist_keep()
    hist_add(0, 0)
    leaf_step()
    hist_add(1, 0)
    for level in range(1, levels):
        hist_add(0, level)
        if level == levels - 1:
            update()
        hist_add(1, level)
    update()
    histograms = ordered(
        last_kernel, jax.ShapeDtypeStruct((per * feats, width * parts), f32),
        [a for p in range(parts) for a in (heres[p], backs[p])], after, "last_add")
    return histograms.reshape(per, feats, -1), leaf_values, updated


def solution(mesh):
    n, nf = mesh.shape["rows"], mesh.shape["feat"]
    return jax.shard_map(
        functools.partial(local, n, nf),
        mesh=mesh,
        in_specs=(
            P("rows", "feat"),
            P("rows", "feat"),
            P("feat", "rows"),
            P("rows"),
            P("feat", None),
        ),
        out_specs=(P("rows", "feat", None), P(None, "feat"), P("rows", "feat")),
        check_vma=False,
    )
```

```python
import functools

import jax
import jax.numpy as jnp
from jax import lax
from jax.experimental import pallas as pl
from jax.experimental.pallas import tpu as pltpu
from jax.sharding import PartitionSpec as P

BINS = 256
LEAVES = 64


shrinkage = 0.5
ridge_term = 1.0

f32 = jnp.float32
bf16 = jnp.bfloat16
VMEM_LIMIT = 16 * 1024 * 1024


def block_rows(rows):
    for size in (256, 128, 64, 32, 16):
        if rows % size == 0:
            return size
    return rows


def cost(gflop):
    return pl.CostEstimate(flops=int(gflop * 1e9), transcendentals=0, bytes_accessed=0)


PARAMS = pltpu.CompilerParams(vmem_limit_bytes=VMEM_LIMIT)


def swap(x, axis, size, by):
    return lax.ppermute(x, axis, [(i, i ^ by) for i in range(size)])


def ordered(kernel, out_shape, args, after, name, gflop=0):
    def body(*refs):
        kernel(*refs[:len(args)], *refs[len(args) + 1:])

    many = isinstance(out_shape, (list, tuple))
    return pl.pallas_call(
        body,
        in_specs=[pl.BlockSpec(memory_space=pltpu.VMEM)] * len(args) + [pl.BlockSpec(memory_space=pl.ANY)],
        out_specs=[pl.BlockSpec(memory_space=pltpu.VMEM)] * len(out_shape)
        if many else pl.BlockSpec(memory_space=pltpu.VMEM),
        out_shape=out_shape,
        cost_estimate=cost(gflop),
        compiler_params=PARAMS,
        name=name,
    )(*args, after)


def leaf_hot(leaf_ref, chunk, blk, flip, scale):
    lanes = leaf_ref.shape[1]
    lines = blk // lanes
    leaf = jnp.concatenate([leaf_ref[pl.ds(chunk * lines + j, 1)] for j in range(lines)], axis=1)
    hot = lax.broadcasted_iota(jnp.int32, (LEAVES, blk), 0) == (leaf ^ flip)
    return jnp.where(hot, f32(scale), f32(0)).astype(bf16)


def chunk_place(i, chunks, core):
    per_half = chunks // 2
    half = 1 - core if i < per_half else core
    return half * per_half + i % per_half


def rows_kernel(pos_ref, leaf_hbm, pred_hbm, lab_hbm, w_hbm, send_ref, keep_ref, g_ref, h_ref,
                leaf_buf, pred_buf, lab_buf, w_buf, pred_sem, lab_sem, w_sem, leaf_sem):
    core, side = pos_ref[0], pos_ref[1]
    chunks, blk, _ = pred_buf.shape
    per_half = chunks // 2

    def copies(i):
        at = pl.ds(pl.multiple_of(chunk_place(i, chunks, core) * blk, blk), blk)
        return (pltpu.make_async_copy(pred_hbm.at[at], pred_buf.at[i], pred_sem.at[i]),
                pltpu.make_async_copy(lab_hbm.at[at], lab_buf.at[i], lab_sem.at[i]))

    w_copy = pltpu.make_async_copy(w_hbm, w_buf, w_sem)
    leaf_copy = pltpu.make_async_copy(leaf_hbm, leaf_buf, leaf_sem)
    for i in range(chunks):
        for copy in copies(i):
            copy.start()
        if i == 0:
            w_copy.start()
            leaf_copy.start()
    for i in range(chunks):
        for copy in copies(i):
            copy.wait()
        if i == 0:
            w_copy.wait()
            leaf_copy.wait()
        p = 0.5 * jnp.tanh((pred_buf[i] * 0.5).astype(f32)) + 0.5
        grad = (lab_buf[i].astype(f32) - p).astype(bf16)
        hess = (p - p * p).astype(bf16)
        out = send_ref if i < per_half else keep_ref
        out[pl.ds(i % per_half * blk, blk)] = jnp.dot(grad, w_buf[...], preferred_element_type=f32).astype(bf16)
        hot = leaf_hot(leaf_buf, chunk_place(i, chunks, core), blk, side * (LEAVES // 2), 1.0)
        g = jnp.dot(hot, grad, preferred_element_type=f32)
        h = jnp.dot(hot, hess, preferred_element_type=f32)
        if i == 0:
            g_ref[...] = g
            h_ref[...] = h
        else:
            g_ref[...] += g
            h_ref[...] += h


def rows_pass(pos, leaf, pred, lab, w):
    rows, cols = pred.shape
    blk = block_rows(rows // 2)
    chunks = rows // blk
    vmem = pl.BlockSpec(memory_space=pltpu.VMEM)
    hbm = pl.BlockSpec(memory_space=pl.ANY)
    return pl.pallas_call(
        rows_kernel,
        in_specs=[pl.BlockSpec(memory_space=pltpu.SMEM), hbm, hbm, hbm, hbm],
        out_specs=[vmem] * 4,
        out_shape=[jax.ShapeDtypeStruct((rows // 2, w.shape[1]), bf16)] * 2
        + [jax.ShapeDtypeStruct((LEAVES, cols), f32)] * 2,
        scratch_shapes=[
            pltpu.VMEM(leaf.shape, jnp.int32),
            pltpu.VMEM((chunks, blk, cols), bf16),
            pltpu.VMEM((chunks, blk, cols), bf16),
            pltpu.VMEM(w.shape, bf16),
            pltpu.SemaphoreType.DMA((chunks,)),
            pltpu.SemaphoreType.DMA((chunks,)),
            pltpu.SemaphoreType.DMA,
            pltpu.SemaphoreType.DMA,
        ],
        compiler_params=PARAMS,
        name="rows",
    )(pos, leaf, pred, lab, w)


def part_add(part, parts):
    def kernel(a_ref, b_ref, out_ref):
        width = out_ref.shape[1]
        at = slice(part * width, (part + 1) * width)
        out_ref[...] = (a_ref[:, at].astype(f32) + b_ref[:, at].astype(f32)).astype(bf16)
    return kernel


def add_kernel(a_ref, b_ref, out_ref):
    out_ref[...] = (a_ref[...].astype(f32) + b_ref[...].astype(f32)).astype(out_ref.dtype)


def leaf_pack_kernel(g_ref, h_ref, keep_ref, send_ref):
    half = LEAVES // 2
    keep_ref[:half] = g_ref[:half]
    keep_ref[half:] = h_ref[:half]
    send_ref[:half] = g_ref[half:].astype(bf16)
    send_ref[half:] = h_ref[half:].astype(bf16)


def value_kernel(a_ref, b_ref, out_ref):
    half = LEAVES // 2
    total = a_ref[...].astype(f32) + b_ref[...].astype(f32)
    out_ref[...] = (total[:half] / (total[half:] + ridge_term)).astype(bf16)


def halving_kernel(here_ref, back_ref, keep_ref, send_ref):
    half = keep_ref.shape[0]
    keep_ref[...] = here_ref[:half] + back_ref[:half].astype(f32)
    send_ref[...] = (here_ref[half:] + back_ref[half:].astype(f32)).astype(bf16)


def last_kernel(*refs):
    out_ref = refs[-1]
    width = refs[0].shape[2]
    for p in range(len(refs) // 2):
        out_ref[:, p * width:(p + 1) * width] = refs[2 * p][0] + refs[2 * p + 1][0].astype(f32)


def hist_kernel(codes_ref, after_ref, *refs, per, odd, bits):
    parts = len(refs) // 3
    feats = codes_ref.shape[1]
    half = codes_ref.shape[2]
    codes = codes_ref[...].astype(f32).astype(bf16)
    step = pl.program_id(0)
    place = sum(((step >> b) & 1) << (bits - 1 - b) for b in range(bits))
    base = (2 * place + odd) * per
    levels = (lax.broadcasted_iota(jnp.int32, (per, 1, 1), 0) + base).astype(f32).astype(bf16)
    one = jnp.ones((), bf16)
    zero = jnp.zeros((), bf16)
    total = None
    for h in range(2):
        hot = jnp.where(codes[h][None] == levels, one, zero).reshape(per * feats, half)
        rows = refs[h * parts:(h + 1) * parts]
        sketch = jnp.concatenate([r[...] for r in rows], axis=1) if parts > 1 else rows[0][...]
        term = jnp.dot(hot, sketch, preferred_element_type=f32)
        total = term if total is None else total + term
    width = refs[-1].shape[2]
    for p in range(parts):
        out = refs[2 * parts + p]
        out[0] = total[:, p * width:(p + 1) * width].astype(out.dtype)


def hist_pass(codes, owns, others, per, blocks, odd, dtype, after, gflop):
    feats = codes.shape[1]
    width = owns[0].shape[1]
    parts = len(owns)
    whole = lambda a: pl.BlockSpec(a.shape, lambda i: (0,) * a.ndim)
    return pl.pallas_call(
        functools.partial(hist_kernel, per=per, odd=odd, bits=blocks.bit_length() - 1),
        grid=(blocks,),
        in_specs=[whole(codes), pl.BlockSpec(memory_space=pl.ANY)] + [whole(a) for a in owns + others],
        out_specs=[pl.BlockSpec((1, per * feats, width), lambda i: (i, 0, 0))] * parts,
        out_shape=[jax.ShapeDtypeStruct((blocks, per * feats, width), dtype)] * parts,
        cost_estimate=cost(gflop),
        compiler_params=PARAMS,
        name="hist_send" if odd else "hist_keep",
    )(codes, after, *owns, *others)


def update_kernel(pos_ref, leaf_ref, own_ref, other_ref, pred_ref, after_ref, *rest, first):
    if first:
        new_hbm, values_hbm, done_ref, new_buf, new_sem, values_buf, values_sem = rest
    else:
        _, new_hbm, done_ref, new_buf, new_sem = rest
    side = pos_ref[1]
    chunks, blk, _ = new_buf.shape
    start = 0 if first else chunks
    half = LEAVES // 2

    def write(i):
        return pltpu.make_async_copy(new_buf.at[i], new_hbm.at[pl.ds((start + i) * blk, blk)], new_sem.at[i])

    own, other = own_ref[...], other_ref[...]
    if first:
        low = side == 0
        values_buf[:half] = jnp.where(low, own.astype(f32), other.astype(f32))
        values_buf[half:] = jnp.where(low, other.astype(f32), own.astype(f32))
        values_copy = pltpu.make_async_copy(values_buf, values_hbm, values_sem)
        values_copy.start()
    table = jnp.concatenate([own, other], axis=0)
    for i in range(chunks):
        hot = leaf_hot(leaf_ref, start + i, blk, side * half, shrinkage)
        found = lax.dot_general(hot, table, (((0,), (0,)), ((), ())), preferred_element_type=f32)
        pred = pred_ref[pl.ds((start + i) * blk, blk)]
        new_buf[i] = (pred.astype(f32) + found).astype(bf16)
        write(i).start()
    done_ref[...] = jnp.zeros_like(done_ref)
    if first:
        values_copy.wait()
    for i in range(chunks):
        write(i).wait()


def update_pass(pos, leaf, own, other, pred, after, begun):
    rows, cols = pred.shape
    blk = block_rows(rows // 2)
    chunks = rows // blk // 2
    first = begun is None
    vmem = pl.BlockSpec(memory_space=pltpu.VMEM)
    hbm = pl.BlockSpec(memory_space=pl.ANY)
    new = jax.ShapeDtypeStruct((rows, cols), bf16)
    done = jax.ShapeDtypeStruct((8, 128), f32)
    return pl.pallas_call(
        functools.partial(update_kernel, first=first),
        in_specs=[pl.BlockSpec(memory_space=pltpu.SMEM), vmem, vmem, vmem, vmem, hbm] + [hbm] * (not first),
        out_specs=[hbm] * (1 + first) + [vmem],
        out_shape=[new, jax.ShapeDtypeStruct((LEAVES, cols), f32), done] if first else [new, done],
        scratch_shapes=[
            pltpu.VMEM((chunks, blk, cols), bf16),
            pltpu.SemaphoreType.DMA((chunks,)),
        ] + ([pltpu.VMEM((LEAVES, cols), f32), pltpu.SemaphoreType.DMA] if first else []),
        input_output_aliases={} if first else {6: 0},
        cost_estimate=cost(3.0),
        compiler_params=PARAMS,
        name="update_first" if first else "update_second",
    )(pos, leaf, own, other, pred, after, *([] if first else [begun]))


def local(n, nf, predictions, labels, feature_codes, leaf_index, sketch_weight):
    rows, cols = predictions.shape
    feats = feature_codes.shape[0]
    half = rows // 2
    parts = 2
    width = sketch_weight.shape[1] // parts
    me = lax.axis_index("rows")
    core = lax.axis_index("feat") & 1
    pos = jnp.stack([core, me & 1])
    per = BINS // n
    codes = (feature_codes ^ (me * per)).reshape(feats, 2, half)
    codes = jnp.where(core == 0, codes, codes[:, ::-1]).swapaxes(0, 1)
    lanes = min(128, block_rows(half))
    leaf = leaf_index.reshape(rows // lanes, lanes)

    pred = pltpu.with_memory_space_constraint(predictions, pltpu.HBM)
    lab = pltpu.with_memory_space_constraint(labels, pltpu.HBM)
    weight = pltpu.with_memory_space_constraint(sketch_weight, pltpu.HBM)
    sketch16 = jax.ShapeDtypeStruct((half, width), bf16)
    sums16 = jax.ShapeDtypeStruct((LEAVES, cols), bf16)
    sums32 = jax.ShapeDtypeStruct((LEAVES, cols), f32)

    send, keep, grad, hess = rows_pass(pos, pltpu.with_memory_space_constraint(leaf, pltpu.HBM), pred, lab, weight)
    got = swap(send, "feat", nf, 1)
    after = keep
    pair, crossed, owns, others, backs, heres = ([None] * parts for _ in range(6))
    leaf_state = None
    updated = leaf_values = None
    levels = (n // 2).bit_length() - 1

    def core_add(p):
        nonlocal after
        after = pair[p] = ordered(part_add(p, parts), sketch16, [keep, got], after, "core_add", 1.0)
        crossed[p] = [swap(after, "feat", nf, t) for t in range(2, nf, 2)]

    def feat_add(p):
        nonlocal after
        own = pair[p]
        for recv in crossed[p]:
            after = own = ordered(add_kernel, sketch16, [own, recv], after, "feat_add")
        owns[p] = own
        others[p] = swap(own, "feat", nf, 1)

    def leaf_pack():
        nonlocal after, leaf_state
        after, sent = ordered(leaf_pack_kernel, [sums32, sums16], [grad, hess], after, "leaf_pack")
        leaf_state = (after, swap(sent, "rows", n, 1), 2)

    def leaf_step():
        nonlocal after, leaf_state
        acc, recv, by = leaf_state
        if by < n:
            after = ordered(add_kernel, sums16, [acc, recv], after, "leaf_add", 1.0 if by == 2 else 3.0)
            leaf_state = (after, swap(after, "rows", n, by), 2 * by)
        elif by == n:
            values16 = jax.ShapeDtypeStruct((LEAVES // 2, cols), bf16)
            after = ordered(value_kernel, values16, [acc, recv], after, "leaf_value")
            leaf_state = (after, swap(after, "rows", n, 1), 2 * by)

    def update():
        nonlocal after, updated, leaf_values
        while leaf_state[2] <= n:
            leaf_step()
        if updated is None:
            updated, leaf_values, after = update_pass(pos, leaf, leaf_state[0], leaf_state[1], predictions, after, None)
        else:
            updated, after = update_pass(pos, leaf, leaf_state[0], leaf_state[1], predictions, after, updated)

    def hist_send(p):
        nonlocal after
        after, = hist_pass(codes, [owns[p]], [others[p]], per, n // 2, 1, bf16, after, (1.0, 3.0)[p])
        backs[p] = swap(after, "rows", n, 1)

    def hist_keep():
        nonlocal after
        heres[:] = hist_pass(codes, owns, others, per, n // 2, 0, f32, after, 3.0)
        after = heres[-1]

    def hist_add(p, level):
        nonlocal after
        blocks = heres[p].shape[0] // 2
        shape = (blocks,) + heres[p].shape[1:]
        heres[p], sent = ordered(
            halving_kernel,
            [jax.ShapeDtypeStruct(shape, f32), jax.ShapeDtypeStruct(shape, bf16)],
            [heres[p], backs[p]], after, "hist_add")
        after = heres[p]
        backs[p] = swap(sent, "rows", n, 2 << level)

    leaf_pack()
    core_add(0)
    core_add(1)
    leaf_step()
    feat_add(0)
    hist_send(0)
    feat_add(1)
    leaf_step()
    hist_send(1)
    hist_keep()
    hist_add(0, 0)
    leaf_step()
    hist_add(1, 0)
    for level in range(1, levels):
        if level == levels - 1:
            update()
        hist_add(0, level)
        hist_add(1, level)
    update()
    histograms = ordered(
        last_kernel, jax.ShapeDtypeStruct((per * feats, width * parts), f32),
        [a for p in range(parts) for a in (heres[p], backs[p])], after, "last_add")
    return histograms.reshape(per, feats, -1), leaf_values, updated


def solution(mesh):
    n, nf = mesh.shape["rows"], mesh.shape["feat"]
    return jax.shard_map(
        functools.partial(local, n, nf),
        mesh=mesh,
        in_specs=(
            P("rows", "feat"),
            P("rows", "feat"),
            P("feat", "rows"),
            P("rows"),
            P("feat", None),
        ),
        out_specs=(P("rows", "feat", None), P(None, "feat"), P("rows", "feat")),
        check_vma=False,
    )
```
